32 devices in a mesh: seq: 16 (over z, y, x), mp: 2 (over core).
Axes of the slice: x: 2, y: 2, z: 4, core: 2. Of those that a mesh axis runs over, the one named last changes fastest.
Arguments:
- tokens: bfloat16 [4, 4096, 512], P(None, 'seq'), may hold values from -6 to 6
- first_gain: float32 [512], replicated, may hold values from 0.5 to 1.5
- first_bias: float32 [512], replicated, may hold values from -3 to 3
- query_weight: bfloat16 [512, 512], P(None, 'mp'), may hold values from -0.25 to 0.25
- query_bias: float32 [512], P('mp'), may hold values from -3 to 3
- key_weight: bfloat16 [512, 512], P(None, 'mp'), may hold values from -0.25 to 0.25
- key_bias: float32 [512], P('mp'), may hold values from -3 to 3
- value_weight: bfloat16 [512, 512], P(None, 'mp'), may hold values from -0.25 to 0.25
- value_bias: float32 [512], P('mp'), may hold values from -3 to 3
- output_weight: bfloat16 [512, 512], P('mp'), may hold values from -1.5 to 1.5
- output_bias: float32 [512], replicated, may hold values from -3 to 3
- second_gain: float32 [512], replicated, may hold values from 0.5 to 1.5
- second_bias: float32 [512], replicated, may hold values from -3 to 3
- up_weight: bfloat16 [512, 2048], P(None, 'mp'), may hold values from -0.25 to 0.25
- up_bias: float32 [2048], P('mp'), may hold values from -3 to 3
- down_weight: bfloat16 [2048, 512], P('mp'), may hold values from -0.125 to 0.125
- down_bias: float32 [512], replicated, may hold values from -3 to 3
- cotangent: bfloat16 [4, 4096, 512], P(None, 'seq'), may hold values from -6 to 6
- doc_starts: int32 [4, 4096], P(None, 'seq'), may hold values from 0 to 1, as said below
- valid_mask: int32 [4, 4096], P(None, 'seq'), may hold values 0 or 1
Outputs:
- layer_out: bfloat16 [4, 4096, 512], P(None, 'seq')
- grad_tokens: float32 [4, 4096, 512], P(None, 'seq')
- lowest_norm: float32 [], replicated
- grad_first_gain: float32 [512], replicated
- grad_first_bias: float32 [512], replicated
- grad_query_weight: float32 [512, 512], P(None, 'mp')
- grad_query_bias: float32 [512], P('mp')
- grad_key_weight: float32 [512, 512], P(None, 'mp')
- grad_key_bias: float32 [512], P('mp')
- grad_value_weight: float32 [512, 512], P(None, 'mp')
- grad_value_bias: float32 [512], P('mp')
- grad_output_weight: float32 [512, 512], P('mp')
- grad_output_bias: float32 [512], replicated
- grad_second_gain: float32 [512], replicated
- grad_second_bias: float32 [512], replicated
- grad_up_weight: float32 [512, 2048], P(None, 'mp')
- grad_up_bias: float32 [2048], P('mp')
- grad_down_weight: float32 [2048, 512], P('mp')
- grad_down_bias: float32 [512], replicated
The draws below stay inside these ranges and needn't reach their ends.
Inputs may be any that keep to these rules, and one draw needn't show every extreme that they name: `doc_starts`: the first entry of every row is 1; in one row, drawn from the seed, no other entry is 1.
All inputs are finite; a program needn't handle non-finite values. No bound on the sum of `valid_mask` on one device may be relied on, other than what follows from the above.
Results may differ from the reference program's by a relative error of at most 0.035.
The reference program's roundings to bfloat16 on the way count: a program that leaves them out, or rounds other values in their place, can miss the bound.
Values may be sent and summed in bfloat16 or wider, within the bound.
No kernel may reach another device: no remote copies, remote signals or barrier semaphores. Data moves between devices by JAX's collectives and lax.ppermute only.
A program may use at most 256 MiB of HBM per device.

```python
import jax
import jax.numpy as jnp
from jax import lax

D = 512
HEADS = 8
HEAD_DIM = 64
FF = 2048
ROWS = 4
BLOCK = 256
DOC_MEAN = 512
ROW_LEN = 4096
N_SEQ = 16


def draw_doc_starts(key, part):
    key = jax.random.fold_in(key, 11)
    key_rows, key_pick = jax.random.split(key)
    markers = jax.random.randint(key_rows, (ROWS, ROW_LEN), 0, DOC_MEAN)
    starts = (markers == 0).astype(jnp.int32)
    column = lax.broadcasted_iota(jnp.int32, (ROWS, ROW_LEN), 1)
    row_ids = lax.broadcasted_iota(jnp.int32, (ROWS, ROW_LEN), 0)
    chosen = jax.random.randint(key_pick, (), 0, ROWS)
    starts = jnp.where(row_ids == chosen, 0, starts)
    return jnp.where(column == 0, 1, starts).astype(jnp.int32)


def with_ends(values, rng, smallest, high):
    place = [jax.random.randint(jax.random.fold_in(rng, axis), (), 0, length) for axis, length in enumerate(values.shape)]
    longest = values.shape.index(max(values.shape))
    beside = place[:longest] + [(place[longest] + 1) % values.shape[longest]] + place[longest + 1:]
    return values.at[tuple(place)].set(smallest).at[tuple(beside)].set(high)


def shard_levels(key, dims, cuts, smallest, high):
    def one(dim, shards_of):
        steps = jax.random.uniform(jax.random.fold_in(jax.random.fold_in(key, 6), dim), (shards_of,), jnp.float32, smallest / len(cuts), high / len(cuts))
        return jnp.repeat(jnp.exp(steps), dims[dim] // shards_of).reshape((-1,) + (1,) * (len(dims) - dim - 1))

    loudness = one(*cuts[0])
    for cut in cuts[1:]:
        loudness = loudness * one(*cut)
    return loudness


def normal_values(own_key, shape, scale, limit, shards=(), held_as=jnp.bfloat16):
    level = shard_levels(own_key, shape, shards, -0.22, 0.18) if shards else 1.0
    drawn = jax.random.normal(own_key, shape, jnp.float32) * scale * level
    return jnp.minimum(jnp.maximum(drawn, -limit), limit).astype(held_as)


def setup_inputs(seed: int = 0) -> dict:
    key_of = jax.random.split(jax.random.key(seed), 21)
    tokens = normal_values(key_of[0], (ROWS, ROW_LEN, D), 1.0, 6.0, ((1, 16),))
    first_gain = jnp.clip(1.0 + 0.1 * jax.random.normal(key_of[1], (D,), jnp.float32), 0.5, 1.5)
    first_bias = normal_values(key_of[2], (D,), 0.5, 3.0, (), jnp.float32)
    query_weight = normal_values(key_of[3], (D, HEADS * HEAD_DIM), D ** -0.5, 0.25, ((1, 2),))
    query_bias = normal_values(key_of[4], (HEADS * HEAD_DIM,), 0.5, 3.0, ((0, 2),), jnp.float32)
    key_weight = normal_values(key_of[5], (D, HEADS * HEAD_DIM), D ** -0.5, 0.25, ((1, 2),))
    key_bias = normal_values(key_of[6], (HEADS * HEAD_DIM,), 0.5, 3.0, ((0, 2),), jnp.float32)
    value_weight = normal_values(key_of[7], (D, HEADS * HEAD_DIM), D ** -0.5, 0.25, ((1, 2),))
    value_bias = normal_values(key_of[8], (HEADS * HEAD_DIM,), 0.5, 3.0, ((0, 2),), jnp.float32)
    output_weight = normal_values(key_of[9], (HEADS * HEAD_DIM, D), (D // 32) ** -0.5, 1.5, ((0, 2),))
    output_bias = normal_values(key_of[10], (D,), 0.5, 3.0, (), jnp.float32)
    second_gain = jnp.clip(1.0 + 0.1 * jax.random.normal(key_of[11], (D,), jnp.float32), 0.5, 1.5)
    second_bias = normal_values(key_of[12], (D,), 0.5, 3.0, (), jnp.float32)
    up_weight = normal_values(key_of[13], (D, FF), D ** -0.5, 0.25, ((1, 2),))
    up_bias = normal_values(key_of[14], (FF,), 0.5, 3.0, ((0, 2),), jnp.float32)
    down_weight = normal_values(key_of[15], (FF, D), FF ** -0.5, 0.125, ((0, 2),))
    down_bias = normal_values(key_of[16], (D,), 0.5, 3.0, (), jnp.float32)
    cotangent = normal_values(key_of[17], (ROWS, ROW_LEN, D), 1.0, 6.0, ((1, 16),))
    doc_starts = draw_doc_starts(jax.random.fold_in(key_of[20], 71), 0)
    valid_mask = with_ends((jax.random.randint(key_of[19], (ROWS, ROW_LEN), 0, 8) < 7).astype(jnp.int32), jax.random.fold_in(key_of[19], 1), 0, 1)
    return dict(tokens=tokens, first_gain=first_gain, first_bias=first_bias, query_weight=query_weight, query_bias=query_bias, key_weight=key_weight, key_bias=key_bias, value_weight=value_weight, value_bias=value_bias, output_weight=output_weight, output_bias=output_bias, second_gain=second_gain, second_bias=second_bias, up_weight=up_weight, up_bias=up_bias, down_weight=down_weight, down_bias=down_bias, cotangent=cotangent, doc_starts=doc_starts, valid_mask=valid_mask)


EPSILON = 1e-05
LARGE_VALUE = 1e+30

@jax.custom_vjp
def low(v):
    return lax.optimization_barrier(v.astype(jnp.bfloat16)).astype(jnp.float32)

@jax.custom_vjp
def low_back(v):
    return v

def low_keep(v):
    return (low(v), None)

def low_pass(kept, grad):
    return (grad,)

def back_keep(v):
    return (v, None)

def back_low(kept, grad):
    return (low(grad),)
low.defvjp(low_keep, low_pass)
low_back.defvjp(back_keep, back_low)

def feature(values):
    return jax.nn.softplus(values)

def layer_norm(values, gain_row, offset):
    average = lax.optimization_barrier(jnp.mean(values, axis=-1, keepdims=True))
    centred = values - average
    spread = lax.optimization_barrier(jnp.mean(centred * centred, axis=-1, keepdims=True))
    return centred * lax.rsqrt(spread + EPSILON) * gain_row + offset

def matmul(left_side, right_side):
    return jnp.dot(left_side, right_side, precision=lax.Precision.HIGHEST, preferred_element_type=jnp.float32)

def split_heads(values):
    return values.reshape(ROWS, ROW_LEN, HEADS, HEAD_DIM)

def block_step(carry_in, inputs):
    state_in, key_total = carry_in
    query_blk, key_blk, value_blk, starts_blk, valid_blk = inputs
    highest = lax.Precision.HIGHEST
    segment = jnp.cumsum(starts_blk, axis=1)
    length = segment.shape[1]
    position = lax.broadcasted_iota(jnp.int32, (length, length), 0)
    earlier = lax.broadcasted_iota(jnp.int32, (length, length), 1)
    key_mask = ((segment[:, :, None] == segment[:, None, :]) & (position >= earlier)[None] & (valid_blk[:, None, :] > 0)).astype(jnp.float32)
    carried = (segment == 0).astype(jnp.float32)
    last_seg = ((segment == segment[:, -1:]) & (valid_blk > 0)).astype(jnp.float32)
    restart = (segment[:, -1] > 0).astype(jnp.float32)
    raw_scores = jnp.einsum('rthe,rshe->rhts', query_blk, key_blk, precision=highest) * key_mask[:, None]
    scores = low_back(raw_scores)
    weights = low(scores)
    within = low_back(jnp.einsum('rhts,rshe->rthe', weights, value_blk, precision=highest))
    across = jnp.einsum('rthe,rhef->rthf', query_blk, state_in, precision=highest) * carried[:, :, None, None]
    normaliser = jnp.transpose(lax.optimization_barrier(jnp.sum(scores, axis=-1)), (0, 2, 1)) + jnp.einsum('rthe,rhe->rth', query_blk, key_total, precision=highest) * carried[:, :, None]
    result = (within + across) / jnp.maximum(normaliser, 1.0)[..., None]
    key_last = key_blk * last_seg[:, :, None, None]
    kept_share = 1.0 - restart
    new_state = state_in * kept_share[:, None, None, None] + jnp.einsum('rshe,rshf->rhef', key_last, value_blk, precision=highest)
    new_total = key_total * kept_share[:, None, None] + lax.optimization_barrier(jnp.sum(key_last, axis=1))
    return ((new_state, new_total), (result, normaliser))

def attention(query_feat, key_feat, value_all, doc_starts, valid_mask):

    def to_blocks(values):
        return jnp.moveaxis(values.reshape((ROWS, N_SEQ, BLOCK) + values.shape[2:]), 1, 0)
    start_state = (jnp.zeros((ROWS, HEADS, HEAD_DIM, HEAD_DIM), jnp.float32), jnp.zeros((ROWS, HEADS, HEAD_DIM), jnp.float32))
    unused, (result, normaliser) = lax.scan(jax.checkpoint(block_step), start_state, (to_blocks(query_feat), to_blocks(key_feat), to_blocks(value_all), to_blocks(doc_starts), to_blocks(valid_mask)))
    result = jnp.moveaxis(result, 0, 1).reshape(ROWS, ROW_LEN, HEADS * HEAD_DIM)
    normaliser = jnp.moveaxis(normaliser, 0, 1).reshape(ROWS, ROW_LEN, HEADS)
    return (result, normaliser)

def reference(tokens, first_gain, first_bias, query_weight, query_bias, key_weight, key_bias, value_weight, value_bias, output_weight, output_bias, second_gain, second_bias, up_weight, up_bias, down_weight, down_bias, cotangent, doc_starts, valid_mask):

    def forward(params):
        inputs, gain_one, bias_one, weight_query, bias_query, weight_key, bias_key, weight_value, bias_value, weight_output, bias_output, gain_two, bias_two, weight_up, bias_up, weight_down, bias_down = params
        first_normed = low(layer_norm(inputs, gain_one, bias_one))
        query_feat = low(feature(low_back(split_heads(matmul(first_normed, weight_query) + bias_query))))
        key_feat = low(feature(low_back(split_heads(matmul(first_normed, weight_key) + bias_key))))
        value_all = low_back(low(split_heads(matmul(first_normed, weight_value) + bias_value)))
        attended, normaliser = attention(query_feat, key_feat, value_all, doc_starts, valid_mask)
        branch = low_back(matmul(low(attended), weight_output) + bias_output)
        middle = inputs + branch
        second_normed = low(layer_norm(middle, gain_two, bias_two))
        up_pre = low_back(matmul(second_normed, weight_up) + bias_up)
        active = low(jax.nn.gelu(up_pre, approximate=False))
        ffn_out = low_back(matmul(active, weight_down) + bias_down)
        return (middle + ffn_out, normaliser)
    floats = tuple((member.astype(jnp.float32) for member in (tokens, first_gain, first_bias, query_weight, query_bias, key_weight, key_bias, value_weight, value_bias, output_weight, output_bias, second_gain, second_bias, up_weight, up_bias, down_weight, down_bias)))
    layer_result, pullback, normaliser = jax.vjp(forward, floats, has_aux=True)
    gradients, = pullback(cotangent.astype(jnp.float32))
    lowest = jnp.min(jnp.where(valid_mask[:, :, None] > 0, normaliser, LARGE_VALUE))
    return (layer_result.astype(jnp.bfloat16), gradients[0], lowest, gradients[1], gradients[2], gradients[3], gradients[4], gradients[5], gradients[6], gradients[7], gradients[8], gradients[9], gradients[10], gradients[11], gradients[12], gradients[13], gradients[14], gradients[15], gradients[16])
```

```python
import jax
import jax.numpy as jnp
from jax import lax
from jax.sharding import PartitionSpec as P

HEAD_DIM = 64
LANES = 128
VECTOR_ROWS = 128


EPSILON = 1e-05
LARGE_VALUE = 1e30


def swap(value):
    return lax.ppermute(value, "mp", [(0, 1), (1, 0)])


def scan_blocks(state, total, restart, extra, backward):
    count = lax.axis_size("seq")
    rows, heads = state.shape[:2]
    flat = state.reshape(rows * heads * HEAD_DIM * HEAD_DIM // LANES, LANES)
    piece = flat.shape[0] // count
    per_row = count // rows
    totals = total.reshape(rows, 1, heads * HEAD_DIM // LANES, LANES)
    totals = jnp.broadcast_to(totals, (rows, per_row) + totals.shape[2:])
    tall = totals.shape[2]
    height = -(-(piece + tall + 2) // 8) * 8
    totals = totals.reshape(count, tall, LANES)
    flags = jnp.broadcast_to(jnp.repeat(restart, per_row)[:, None, None], (count, 1, LANES))
    extras = jnp.broadcast_to(extra[None, None, None], (count, 1, LANES))
    fill = jnp.zeros((count, height - piece - tall - 2, LANES), jnp.float32)
    packed = jnp.concatenate(
        [flat.reshape(count, piece, LANES), totals, flags, extras, fill], axis=1
    )
    held = lax.all_to_all(packed, "seq", 0, 0)
    flag = held[:, piece + tall : piece + tall + 1]
    seen = held[:, piece + tall + 1, 0]
    order = range(count - 1, 0, -1) if backward else range(count - 1)
    running = jnp.zeros_like(held[0])
    entries = {(count - 1 if backward else 0): running}
    for block in order:
        running = held[block] + (1.0 - flag[block]) * running
        entries[block - 1 if backward else block + 1] = running
    scanned = jnp.stack([entries[block] for block in range(count)])
    mine = lax.all_to_all(scanned, "seq", 0, 0)
    state_in = mine[:, :piece].reshape(state.shape)
    total_in = mine.reshape(rows, per_row, height, LANES)[:, 0, piece : piece + tall]
    return state_in, total_in.reshape(total.shape), seen


def sum_over_seq(values):
    count = lax.axis_size("seq")
    outer = 2 ** ((count.bit_length() - 1) // 2)
    inner = count // outer
    near = [[o * inner + i for i in range(inner)] for o in range(outer)]
    far = [[o * inner + i for o in range(outer)] for i in range(inner)]
    rows, columns = values.shape

    def exchange(parts, groups):
        return lax.all_to_all(parts, "seq", 0, 0, axis_index_groups=groups)

    def reduce(value, size, groups):
        parts = exchange(value.reshape(size, value.shape[0] // size, columns), groups)
        return jnp.sum(parts.astype(jnp.float32), axis=0).astype(jnp.bfloat16)

    def gather(value, size, groups):
        parts = jnp.broadcast_to(value[None], (size,) + value.shape)
        return exchange(parts, groups).reshape(size * value.shape[0], columns)

    part = reduce(reduce(values, inner, near), outer, far)
    return gather(gather(part, outer, far), inner, near)


def normalize(values):
    average = jnp.mean(values, axis=-1, keepdims=True)
    centred = values - average
    spread = jnp.mean(centred * centred, axis=-1, keepdims=True)
    inverse = lax.rsqrt(spread + EPSILON)
    return (centred * inverse, inverse)


def norm_backward(grad_out, normed, inverse, gain_row):
    grad_normed = grad_out * gain_row
    first_term = jnp.mean(grad_normed, axis=-1, keepdims=True)
    second_term = jnp.mean(grad_normed * normed, axis=-1, keepdims=True)
    return inverse * (grad_normed - first_term - normed * second_term)


def feature(values):
    return jax.nn.softplus(values)


def feature_slope(values):
    return jax.nn.sigmoid(values)


def gelu_slope(values):
    cumulative = 0.5 * (1.0 + lax.erf(values * 0.7071067811865476))
    density = 0.3989422804014327 * jnp.exp(-0.5 * values * values)
    return cumulative + values * density


def matmul(left_side, right_side):
    return jnp.dot(left_side, right_side, preferred_element_type=jnp.float32)


def contract_rows(left_side, right_side):
    return jnp.einsum("ta,tb->ab", left_side, right_side, preferred_element_type=jnp.float32)


def contract_cols(left_side, right_side):
    return jnp.einsum("ta,ba->tb", left_side, right_side, preferred_element_type=jnp.float32)


def run_layer(
    tokens,
    first_gain,
    first_bias,
    query_weight,
    query_bias,
    key_weight,
    key_bias,
    value_weight,
    value_bias,
    output_weight,
    output_bias,
    second_gain,
    second_bias,
    up_weight,
    up_bias,
    down_weight,
    down_bias,
    cotangent,
    doc_starts,
    valid_mask,
):
    row_count, block_len, model_width = tokens.shape
    local_width = query_weight.shape[1]
    local_heads = local_width // HEAD_DIM
    tok_count = row_count * block_len
    highest = lax.Precision.HIGHEST
    head_shape = (row_count, block_len, local_heads, HEAD_DIM)
    inputs = tokens.reshape(tok_count, model_width).astype(jnp.float32)
    normed_one, inverse_one = normalize(inputs)
    first_low = (normed_one * first_gain + first_bias).astype(jnp.bfloat16)
    query_pre = (matmul(first_low, query_weight) + query_bias).reshape(head_shape)
    key_pre = (matmul(first_low, key_weight) + key_bias).reshape(head_shape)
    value_low = (
        (matmul(first_low, value_weight) + value_bias).astype(jnp.bfloat16).reshape(head_shape)
    )
    query_feat = feature(query_pre).astype(jnp.bfloat16)
    key_feat = feature(key_pre).astype(jnp.bfloat16)
    segment = jnp.cumsum(doc_starts, axis=1)
    position = lax.broadcasted_iota(jnp.int32, (block_len, block_len), 0)
    earlier_pos = lax.broadcasted_iota(jnp.int32, (block_len, block_len), 1)
    valid_keys = valid_mask > 0
    key_mask = (
        (segment[:, :, None] == segment[:, None, :])
        & (position >= earlier_pos)[None]
        & valid_keys[:, None, :]
    ).astype(jnp.float32)[:, None]
    carried = (segment == 0).astype(jnp.float32)
    last_seg = ((segment == segment[:, -1:]) & valid_keys).astype(jnp.float32)
    restart = (segment[:, -1] > 0).astype(jnp.float32)
    raw_scores = (
        jnp.einsum("rthe,rshe->rhts", query_feat, key_feat, preferred_element_type=jnp.float32)
        * key_mask
    )
    weights_low = raw_scores.astype(jnp.bfloat16)
    within = jnp.einsum(
        "rhts,rshe->rthe", weights_low, value_low, preferred_element_type=jnp.float32
    )
    key_last = key_feat * last_seg[:, :, None, None].astype(jnp.bfloat16)
    state_local = jnp.einsum(
        "rshe,rshf->rhef", key_last, value_low, preferred_element_type=jnp.float32
    )
    total_local = jnp.sum(key_last.astype(jnp.float32), axis=1)
    state_in, total_in, unused_seen = scan_blocks(
        state_local, total_local, restart, jnp.zeros((), jnp.float32), False
    )
    query_wide = query_feat.astype(jnp.float32)
    across = (
        jnp.einsum("rthe,rhef->rthf", query_wide, state_in, precision=highest)
        * carried[:, :, None, None]
    )
    normaliser = (
        jnp.transpose(jnp.sum(raw_scores, axis=-1), (0, 2, 1))
        + jnp.einsum("rthe,rhe->rth", query_wide, total_in, precision=highest) * carried[:, :, None]
    )
    divisor = jnp.maximum(normaliser, 1.0)
    attended = (within + across) / divisor[..., None]
    attended_low = attended.reshape(tok_count, local_width).astype(jnp.bfloat16)
    local_min = jnp.min(jnp.where(valid_keys[:, :, None], normaliser, LARGE_VALUE))
    branch = matmul(attended_low, output_weight)
    middle = inputs + branch + output_bias
    normed_two, inverse_two = normalize(middle)
    second_low = (normed_two * second_gain + second_bias).astype(jnp.bfloat16)
    up_pre = matmul(second_low, up_weight) + up_bias
    active_low = jax.nn.gelu(up_pre, approximate=False).astype(jnp.bfloat16)
    ffn_out = matmul(active_low, down_weight)
    layer_out = (
        (middle + ffn_out + down_bias)
        .astype(jnp.bfloat16)
        .reshape(row_count, block_len, model_width)
    )
    grad_low = cotangent.reshape(tok_count, model_width)
    grad_out = grad_low.astype(jnp.float32)
    grad_down = contract_rows(active_low, grad_low)
    grad_down_bias = jnp.sum(grad_out, axis=0)
    grad_up_low = (contract_cols(grad_low, down_weight) * gelu_slope(up_pre)).astype(jnp.bfloat16)
    grad_up = contract_rows(second_low, grad_up_low)
    grad_up_bias = jnp.sum(grad_up_low.astype(jnp.float32), axis=0)
    grad_second = contract_cols(grad_up_low, up_weight)
    grad_second_gain = jnp.sum(grad_second * normed_two, axis=0)
    grad_second_bias = jnp.sum(grad_second, axis=0)
    grad_middle = grad_out + norm_backward(grad_second, normed_two, inverse_two, second_gain)
    grad_branch = grad_middle.astype(jnp.bfloat16)
    grad_output = contract_rows(attended_low, grad_branch)
    grad_output_bias = jnp.sum(grad_branch.astype(jnp.float32), axis=0)
    grad_attended = contract_cols(grad_branch, output_weight).reshape(head_shape)
    grad_num = grad_attended / divisor[..., None]
    grad_norm = jnp.where(
        normaliser > 1.0, -jnp.sum(grad_attended * attended, axis=-1) / divisor, 0.0
    )
    grad_within_low = grad_num.astype(jnp.bfloat16)
    grad_weights = jnp.einsum(
        "rthe,rshe->rhts", grad_within_low, value_low, preferred_element_type=jnp.float32
    )
    grad_values = jnp.einsum(
        "rhts,rthe->rshe", weights_low, grad_within_low, preferred_element_type=jnp.float32
    )
    grad_scores = (
        (grad_weights + jnp.transpose(grad_norm, (0, 2, 1))[..., None]) * key_mask
    ).astype(jnp.bfloat16)
    grad_query = jnp.einsum(
        "rhts,rshe->rthe", grad_scores, key_feat, preferred_element_type=jnp.float32
    )
    grad_key = jnp.einsum(
        "rhts,rthe->rshe", grad_scores, query_feat, preferred_element_type=jnp.float32
    )
    grad_across = grad_num * carried[:, :, None, None]
    grad_norm_carried = grad_norm * carried[:, :, None]
    grad_query = (
        grad_query
        + jnp.einsum("rthf,rhef->rthe", grad_across, state_in, precision=highest)
        + grad_norm_carried[..., None] * total_in[:, None]
    )
    grad_state_in = jnp.einsum("rthe,rthf->rhef", query_wide, grad_across, precision=highest)
    grad_total_in = jnp.einsum("rthe,rth->rhe", query_wide, grad_norm_carried, precision=highest)
    grad_state_loc, grad_total_loc, seen = scan_blocks(
        grad_state_in, grad_total_in, restart, local_min, True
    )
    lowest_norm = jnp.min(seen)
    lowest_norm = jnp.minimum(lowest_norm, swap(lowest_norm[None])[0])
    last_wide = last_seg[:, :, None, None]
    grad_key = grad_key + last_wide * (
        jnp.einsum(
            "rshf,rhef->rshe", value_low.astype(jnp.float32), grad_state_loc, precision=highest
        )
        + grad_total_loc[:, None]
    )
    grad_values = grad_values + last_wide * jnp.einsum(
        "rshe,rhef->rshf", key_feat.astype(jnp.float32), grad_state_loc, precision=highest
    )
    grad_query_low = (
        (grad_query * feature_slope(query_pre)).astype(jnp.bfloat16).reshape(tok_count, local_width)
    )
    grad_key_low = (
        (grad_key * feature_slope(key_pre)).astype(jnp.bfloat16).reshape(tok_count, local_width)
    )
    grad_value_low = grad_values.astype(jnp.bfloat16).reshape(tok_count, local_width)
    grad_first = (
        contract_cols(grad_query_low, query_weight)
        + contract_cols(grad_key_low, key_weight)
        + contract_cols(grad_value_low, value_weight)
    )
    grad_first_gain = jnp.sum(grad_first * normed_one, axis=0)
    grad_first_bias = jnp.sum(grad_first, axis=0)
    grad_tokens = (
        grad_middle + norm_backward(grad_first, normed_one, inverse_one, first_gain)
    ).reshape(row_count, block_len, model_width)
    grad_query_w = contract_rows(first_low, grad_query_low)
    grad_query_b = jnp.sum(grad_query_low.astype(jnp.float32), axis=0)
    grad_key_w = contract_rows(first_low, grad_key_low)
    grad_key_b = jnp.sum(grad_key_low.astype(jnp.float32), axis=0)
    grad_value_w = contract_rows(first_low, grad_value_low)
    grad_value_b = jnp.sum(grad_value_low.astype(jnp.float32), axis=0)
    weight_grads = (
        grad_first_gain,
        grad_first_bias,
        grad_query_w,
        grad_query_b,
        grad_key_w,
        grad_key_b,
        grad_value_w,
        grad_value_b,
        grad_output,
        grad_output_bias,
        grad_second_gain,
        grad_second_bias,
        grad_up,
        grad_up_bias,
        grad_down,
        grad_down_bias,
    )
    return (layer_out, grad_tokens, lowest_norm, weight_grads)


def per_device(
    tokens,
    first_gain,
    first_bias,
    query_weight,
    query_bias,
    key_weight,
    key_bias,
    value_weight,
    value_bias,
    output_weight,
    output_bias,
    second_gain,
    second_bias,
    up_weight,
    up_bias,
    down_weight,
    down_bias,
    cotangent,
    doc_starts,
    valid_mask,
):
    share_count = lax.axis_size("mp")
    share_index = lax.axis_index("mp")
    attn_width = query_weight.shape[1]
    ff_width = up_weight.shape[1]

    def both(own, dim):
        return jnp.concatenate([own, swap(own)], axis=dim)

    biases = swap(jnp.concatenate([query_bias, key_bias, value_bias, up_bias]))
    other_q, other_k, other_v, other_up = jnp.split(
        biases, [attn_width, 2 * attn_width, 3 * attn_width]
    )
    rows_here = tokens.shape[0] // share_count
    row_start = share_index * rows_here

    def own_rows(values):
        return lax.dynamic_slice_in_dim(values, row_start, rows_here, 0)

    layer_part, grad_part, lowest_norm, grads = run_layer(
        own_rows(tokens),
        first_gain,
        first_bias,
        both(query_weight, 1),
        jnp.concatenate([query_bias, other_q]),
        both(key_weight, 1),
        jnp.concatenate([key_bias, other_k]),
        both(value_weight, 1),
        jnp.concatenate([value_bias, other_v]),
        both(output_weight, 0),
        output_bias,
        second_gain,
        second_bias,
        both(up_weight, 1),
        jnp.concatenate([up_bias, other_up]),
        both(down_weight, 0),
        down_bias,
        own_rows(cotangent),
        own_rows(doc_starts),
        own_rows(valid_mask),
    )

    def all_rows(own):
        other = swap(own)
        first = jnp.where(share_index == 0, own, other)
        return jnp.concatenate([first, jnp.where(share_index == 0, other, own)], axis=0)

    layer_out, grad_tokens = (all_rows(layer_part), all_rows(grad_part))

    def shared(whole, dim):
        own, other = jnp.split(whole, 2, axis=dim)
        return (own + swap(other.astype(jnp.bfloat16)).astype(jnp.float32)).astype(jnp.bfloat16)

    grad_up, grad_down = (shared(grads[12], 1), shared(grads[14], 0))
    grad_q, grad_k, grad_v = (shared(grads[2], 1), shared(grads[4], 1), shared(grads[6], 1))
    grad_o = shared(grads[8], 0)
    width = grad_down.shape[1]
    half = grad_up.shape[1] // 2
    ffn = sum_over_seq(
        jnp.concatenate([grad_down, grad_up[:, :half], grad_up[:, half:]], axis=0)
    ).astype(jnp.float32)
    grad_down = ffn[:ff_width]
    grad_up = jnp.concatenate(jnp.split(ffn[ff_width:], 2, axis=0), axis=1)
    own_vectors, other_vectors = ([], [])
    for index in (3, 5, 7, 13):
        own, other = jnp.split(grads[index], 2)
        own_vectors.append(own)
        other_vectors.append(other)
    every = [grads[index] for index in (0, 1, 9, 10, 11, 15)]
    received = swap(jnp.concatenate(other_vectors + every))
    vectors = (jnp.concatenate(own_vectors + every) + received).astype(jnp.bfloat16)
    used = vectors.shape[0] // VECTOR_ROWS
    vectors = jnp.pad(vectors.reshape(VECTOR_ROWS, used), ((0, 0), (0, width - used)))
    v_half = grad_v.shape[0] // 2
    rest = sum_over_seq(
        jnp.concatenate(
            [
                jnp.concatenate([grad_q, grad_k], axis=1),
                jnp.concatenate([grad_v[:v_half], grad_v[v_half:]], axis=1),
                grad_o,
                vectors,
            ],
            axis=0,
        )
    ).astype(jnp.float32)
    top = grad_q.shape[0]
    grad_q, grad_k = (rest[:top, :attn_width], rest[:top, attn_width:])
    grad_v = rest[top : top + v_half]
    grad_v = jnp.concatenate([grad_v[:, :attn_width], grad_v[:, attn_width:]], axis=0)
    grad_o = rest[top + v_half : top + v_half + attn_width]
    vectors = rest[top + v_half + attn_width :, :used].reshape(-1)
    cuts = [attn_width, 2 * attn_width, 3 * attn_width, 3 * attn_width + ff_width]
    cuts += [cuts[-1] + width * step for step in range(1, 6)]
    q_b, k_b, v_b, up_b, gain_1, bias_1, out_b, gain_2, bias_2, down_b = jnp.split(vectors, cuts)
    return (
        layer_out,
        grad_tokens,
        lowest_norm,
        gain_1,
        bias_1,
        grad_q,
        q_b,
        grad_k,
        k_b,
        grad_v,
        v_b,
        grad_o,
        out_b,
        gain_2,
        bias_2,
        grad_up,
        up_b,
        grad_down,
        down_b,
    )


def solution(mesh):
    return jax.shard_map(
        per_device,
        mesh=mesh,
        in_specs=(
            P(None, "seq", None),
            P(),
            P(),
            P(None, "mp"),
            P("mp"),
            P(None, "mp"),
            P("mp"),
            P(None, "mp"),
            P("mp"),
            P("mp", None),
            P(),
            P(),
            P(),
            P(None, "mp"),
            P("mp"),
            P("mp", None),
            P(),
            P(None, "seq", None),
            P(None, "seq"),
            P(None, "seq"),
        ),
        out_specs=(
            P(None, "seq", None),
            P(None, "seq", None),
            P(),
            P(),
            P(),
            P(None, "mp"),
            P("mp"),
            P(None, "mp"),
            P("mp"),
            P(None, "mp"),
            P("mp"),
            P("mp", None),
            P(),
            P(),
            P(),
            P(None, "mp"),
            P("mp"),
            P("mp", None),
            P(),
        ),
        check_vma=False,
    )
```

```python
import functools

import jax
import jax.numpy as jnp
from jax import lax
from jax.experimental import pallas as pl
from jax.experimental.pallas import tpu as pltpu
from jax.sharding import PartitionSpec as P

HEAD_DIM = 64
LANES = 128
EPSILON = 1e-05
LARGE_VALUE = 1e30
MEBI = 1024 * 1024

low = jnp.bfloat16
wide = jnp.float32


def dot(left, right):
    return jnp.dot(left, right, preferred_element_type=wide)


def dot_nt(left, right):
    return lax.dot_general(left, right, (((1,), (1,)), ((), ())), preferred_element_type=wide)


def dot_tn(left, right):
    return lax.dot_general(left, right, (((0,), (0,)), ((), ())), preferred_element_type=wide)


def iota(shape, dim):
    return lax.broadcasted_iota(jnp.int32, shape, dim)


def first_head(shape):
    return iota(shape, 1) < HEAD_DIM


def only_head(pair, head):
    keep = first_head(pair.shape) if head == 0 else jnp.logical_not(first_head(pair.shape))
    return jnp.where(keep, pair, jnp.zeros_like(pair))


def head_sums(pair):
    keep = first_head(pair.shape)
    one = jnp.sum(jnp.where(keep, pair, 0.0), axis=1, keepdims=True)
    two = jnp.sum(jnp.where(keep, 0.0, pair), axis=1, keepdims=True)
    return jnp.where(keep, one, two)


def spread_heads(columns):
    return jnp.where(first_head((columns.shape[0], LANES)), columns[:, 0:1], columns[:, 1:2])


def two_terms(value):
    high = value.astype(low)
    return high, (value - high.astype(wide)).astype(low)


def two_blocks(state):
    return jnp.concatenate([only_head(state, 0), only_head(state, 1)], axis=0)


def compact(product):
    return jnp.where(
        first_head((HEAD_DIM, LANES)), product[:HEAD_DIM], product[HEAD_DIM:]
    )


def normalize(values):
    average = jnp.mean(values, axis=1, keepdims=True)
    centred = values - average
    spread = jnp.mean(centred * centred, axis=1, keepdims=True)
    inverse = lax.rsqrt(spread + EPSILON)
    return (centred * inverse, inverse)


def norm_backward(grad_out, normed, inverse, gain_row):
    grad_normed = grad_out * gain_row
    first_term = jnp.mean(grad_normed, axis=1, keepdims=True)
    second_term = jnp.mean(grad_normed * normed, axis=1, keepdims=True)
    return inverse * (grad_normed - first_term - normed * second_term)


def column_sums(values):
    return jnp.sum(values, axis=0, keepdims=True)


TILE = 32


def tiles(count):
    return [slice(start, start + TILE) for start in range(0, count, TILE)]


def fold_rows(values):
    total = values[0:8]
    for start in range(8, values.shape[0], 8):
        total = total + values[start : start + 8]
    return total


class Sizes:
    def __init__(self, blocks, rows, block, width, attn, hidden):
        self.blocks, self.rows, self.block = blocks, rows, block
        self.width, self.attn, self.hidden = width, attn, hidden
        self.toks = rows * block
        self.pairs = 2 * attn // LANES
        self.group = blocks // (rows * self.pairs)
        self.slice = HEAD_DIM // self.group
        self.height = -(-(self.slice + 3) // 8) * 8

    def at(self, row, tile):
        return slice(row * self.block + tile.start, row * self.block + tile.stop)

    def span(self, row):
        return slice(row * self.block, (row + 1) * self.block)


def lanes_of(pair):
    return slice(pair * LANES, (pair + 1) * LANES)


def write_state(z, sent_ref, held_ref, row, pair, state, total, restart, extra):
    held_ref[...] = state
    for step in range(z.group):
        index = (row * z.pairs + pair) * z.group + step
        sent_ref[index, 0 : z.slice, :] = held_ref[step * z.slice : (step + 1) * z.slice, :]
        sent_ref[index, z.slice : z.slice + 1, :] = total
        sent_ref[index, z.slice + 1 : z.slice + 2, :] = jnp.broadcast_to(restart, (1, LANES))
        sent_ref[index, z.slice + 2 : z.slice + 3, :] = extra
        if z.height > z.slice + 3:
            sent_ref[index, z.slice + 3 : z.height, :] = jnp.zeros(
                (z.height - z.slice - 3, LANES), wide
            )


def read_state(z, got_ref, held_ref, row, pair):
    start = (row * z.pairs + pair) * z.group
    for step in range(z.group):
        held_ref[step * z.slice : (step + 1) * z.slice, :] = got_ref[start + step, 0 : z.slice, :]
    return held_ref[...], got_ref[start, z.slice : z.slice + 1, :]


def mask_of(z, cols_ref, segs_ref, row):
    here = cols_ref[z.span(row), 0:1]
    there = segs_ref[row * 8 : row * 8 + 1, :]
    shape = (z.block, z.block)
    return jnp.logical_and(here == there, iota(shape, 0) >= iota(shape, 1))


def project_kernel(
    z,
    mine_ref,
    tokens_ref,
    starts_ref,
    valid_ref,
    gain_ref,
    bias_ref,
    wk_ref,
    wk2_ref,
    bk_ref,
    wv_ref,
    wv2_ref,
    bv_ref,
    other_bias_ref,
    first_ref,
    kslope_ref,
    kfeat_ref,
    vlow_ref,
    cols_ref,
    segs_ref,
    sent_ref,
    held_ref,
    pre_ref,
):
    mine = mine_ref[0]
    for row in range(z.rows):
        for tile in tiles(z.block):
            x = tokens_ref[row, tile, :].astype(wide)
            normed, _ = normalize(x)
            first_ref[z.at(row, tile), :] = (normed * gain_ref[...] + bias_ref[...]).astype(low)
    a = z.attn
    first = first_ref[...]
    for part, (wk, wv, bk, bv) in enumerate(
        (
            (wk_ref, wv_ref, bk_ref[...], bv_ref[...]),
            (wk2_ref, wv2_ref, other_bias_ref[:, a : 2 * a], other_bias_ref[:, 2 * a : 3 * a]),
        )
    ):
        lanes = slice(part * a, (part + 1) * a)
        pre_ref[part] = dot(first, wk[...])
        vlow_ref[:, lanes] = (dot(first, wv[...]) + bv).astype(low)
        for tile in tiles(z.toks):
            key_pre = pre_ref[part, tile, :] + bk
            kslope_ref[tile, lanes] = jax.nn.sigmoid(key_pre).astype(low)
            kfeat_ref[tile, lanes] = softplus(key_pre).astype(low)
    square = (z.block, z.block)
    upto = iota(square, 0) <= iota(square, 1)
    upper = jnp.where(upto, 1.0, 0.0).astype(low)
    since = jnp.where(iota(square, 0) >= iota(square, 1), 1.0, 0.0).astype(low)
    same = jnp.where(iota(square, 0) == iota(square, 1), 1.0, 0.0).astype(low)
    for row in range(z.rows):
        other = z.rows + row

        def pick(ref):
            value = jnp.where(mine == 0, ref[row : row + 1, :], ref[other : other + 1, :])
            return jnp.broadcast_to(value.astype(wide), (8, z.block)).astype(low)

        starts, valid = pick(starts_ref), pick(valid_ref)
        seg_row = dot(starts, upper)
        seg_col = dot_nt(since, starts)[:, 0:1]
        valid_col = dot_nt(same, valid)[:, 0:1]
        seg_end = seg_row[0:1, z.block - 1 : z.block]
        segs_ref[row * 8 : (row + 1) * 8, :] = jnp.where(valid.astype(wide) > 0.0, seg_row, -1.0)
        carried = jnp.where(seg_col == 0.0, 1.0, 0.0)
        last = jnp.where(jnp.logical_and(seg_col == seg_end, valid_col > 0.0), 1.0, 0.0)
        restart = jnp.where(seg_end > 0.0, 1.0, 0.0)
        lane = iota((z.block, LANES), 1)
        cols = jnp.where(lane == 0, seg_col, 0.0)
        cols = jnp.where(lane == 1, carried, cols)
        cols = jnp.where(lane == 2, last, cols)
        cols = jnp.where(lane == 3, valid_col, cols)
        cols = jnp.where(lane == 4, restart, cols)
        cols_ref[z.span(row), :] = cols
        for pair in range(z.pairs):
            keys = kfeat_ref[z.span(row), lanes_of(pair)].astype(wide) * last
            product = dot_tn(keys.astype(low), vlow_ref[z.span(row), lanes_of(pair)])
            write_state(
                z,
                sent_ref,
                held_ref,
                row,
                pair,
                compact(product),
                column_sums(keys),
                restart,
                jnp.zeros((1, LANES), wide),
            )


def softplus(values):
    return jnp.maximum(values, 0.0) + jnp.log1p(jnp.exp(-jnp.abs(values)))


def scan_kernel(z, backward, held_ref, scanned_ref, lowest_ref):
    flag = z.slice + 1
    running = jnp.zeros((z.height, LANES), wide)
    least = jnp.full((1, LANES), LARGE_VALUE, wide)
    for step in range(z.blocks):
        block = z.blocks - 1 - step if backward else step
        scanned_ref[block] = running
        here = held_ref[block]
        running = here + (1.0 - here[flag : flag + 1, :]) * running
        least = jnp.minimum(least, here[flag + 1 : flag + 2, :])
    lowest_ref[...] = jnp.broadcast_to(least, (8, LANES))


def score_kernel(
    z,
    first_ref,
    wq_ref,
    wq2_ref,
    bq_ref,
    other_bias_ref,
    kfeat_ref,
    vlow_ref,
    cols_ref,
    segs_ref,
    qslope_ref,
    qfeat_ref,
    weights_ref,
    within_ref,
    sums_ref,
    pre_ref,
):
    a = z.attn
    for part, (wq, bq) in enumerate(((wq_ref, bq_ref[...]), (wq2_ref, other_bias_ref[:, 0:a]))):
        lanes = slice(part * a, (part + 1) * a)
        pre_ref[part] = dot(first_ref[...], wq[...])
        for tile in tiles(z.toks):
            query_pre = pre_ref[part, tile, :] + bq
            qslope_ref[tile, lanes] = jax.nn.sigmoid(query_pre).astype(low)
            qfeat_ref[tile, lanes] = softplus(query_pre).astype(low)
    for row in range(z.rows):
        mask = mask_of(z, cols_ref, segs_ref, row)
        table = jnp.zeros((z.block, LANES), wide)
        for pair in range(z.pairs):
            here = (z.span(row), lanes_of(pair))
            queries, keys, values = qfeat_ref[here], kfeat_ref[here], vlow_ref[here]
            within = jnp.zeros((z.block, LANES), wide)
            sums = []
            for head in range(2):
                scores = jnp.where(mask, dot_nt(only_head(queries, head), keys), 0.0)
                weights = scores.astype(low)
                weights_ref[(row * z.pairs + pair) * 2 + head] = weights
                within = within + dot(weights, only_head(values, head))
                sums.append(jnp.sum(scores, axis=1, keepdims=True))
            within_ref[here] = within
            lane = iota((z.block, LANES), 1)
            table = jnp.where(lane == 2 * pair, sums[0], table)
            table = jnp.where(lane == 2 * pair + 1, sums[1], table)
        sums_ref[z.span(row), :] = table


def middle_kernel(
    z,
    mine_ref,
    got_ref,
    qfeat_ref,
    within_ref,
    sums_ref,
    cols_ref,
    tokens_ref,
    cot_ref,
    wo_ref,
    wo2_ref,
    ob_ref,
    gain_ref,
    bias_ref,
    wup_ref,
    wup2_ref,
    bup_ref,
    bup2_ref,
    wd_ref,
    wd2_ref,
    db_ref,
    layer_ref,
    act_ref,
    act2_ref,
    gup_ref,
    gup2_ref,
    second_ref,
    gbr_ref,
    att_ref,
    att2_ref,
    gnum_ref,
    gnorm_ref,
    sent_ref,
    vec_ref,
    s_mid,
    s_n2,
    s_r2,
    s_ffn,
    s_gsec,
    s_att,
    s_norm,
    s_min,
    held_ref,
    s_up,
    s_gact,
):
    step = pl.program_id(0)
    a = z.attn

    @pl.when(step == 0)
    def _():
        least = jnp.full((1, 1), LARGE_VALUE, wide)
        for row in range(z.rows):
            carried = cols_ref[z.span(row), 1:2]
            valid = cols_ref[z.span(row), 3:4]
            for pair in range(z.pairs):
                here = (z.span(row), lanes_of(pair))
                state, total = read_state(z, got_ref, held_ref, row, pair)
                high, rest = two_terms(two_blocks(state))
                queries = qfeat_ref[here]
                across = dot(
                    jnp.concatenate([queries, queries], axis=1),
                    jnp.concatenate([high, rest], axis=0),
                )
                norm = spread_heads(sums_ref[z.span(row), 2 * pair : 2 * pair + 2])
                norm = norm + carried * head_sums(queries.astype(wide) * total)
                s_norm[here] = norm
                seen = jnp.where(valid > 0.0, norm, LARGE_VALUE)
                seen = jnp.min(jnp.min(seen, axis=0, keepdims=True), axis=1, keepdims=True)
                least = jnp.minimum(least, seen)
                attended = (within_ref[here] + across * carried) / jnp.maximum(norm, 1.0)
                s_att[here] = attended
        s_min[...] = jnp.broadcast_to(least, (8, LANES))
        att_ref[...] = s_att[:, 0:a].astype(low)
        att2_ref[...] = s_att[:, a : 2 * a].astype(low)
        s_mid[...] = dot(att_ref[...], wo_ref[...]) + dot(att2_ref[...], wo2_ref[...])
        for row in range(z.rows):
            for tile in tiles(z.block):
                here = z.at(row, tile)
                middle = tokens_ref[row, tile, :].astype(wide) + s_mid[here, :] + ob_ref[...]
                s_mid[here, :] = middle
                normed, inverse = normalize(middle)
                s_n2[here, :] = normed
                s_r2[here, :] = jnp.broadcast_to(inverse, (TILE, LANES))
                second_ref[here, :] = (normed * gain_ref[...] + bias_ref[...]).astype(low)
        s_ffn[...] = jnp.zeros_like(s_ffn)
        s_gsec[...] = jnp.zeros_like(s_gsec)
        vec_ref[...] = jnp.zeros_like(vec_ref)

    for part, (wup, bup, wd, act_out, gup_out) in enumerate(
        (
            (wup_ref, bup_ref, wd_ref, act_ref, gup_ref),
            (wup2_ref, bup2_ref, wd2_ref, act2_ref, gup2_ref),
        )
    ):
        sums = jnp.zeros((8, bup.shape[1]), wide)
        for row in range(z.rows):
            span = z.span(row)
            s_up[row] = dot(second_ref[span, :], wup[...])
            s_gact[row] = dot_nt(cot_ref[row], wd[...])
            for tile in tiles(z.block):
                up = s_up[row, tile, :] + bup[...]
                share = 0.5 * (1.0 + lax.erf(up * 0.7071067811865476))
                density = 0.3989422804014327 * jnp.exp(-0.5 * up * up)
                act_out[z.at(row, tile), :] = (up * share).astype(low)
                gup = (s_gact[row, tile, :] * (share + up * density)).astype(low)
                gup_out[z.at(row, tile), :] = gup
                sums = sums + fold_rows(gup.astype(wide))
            s_ffn[span, :] += dot(act_out[span, :], wd[...])
            s_gsec[span, :] += dot_nt(gup_out[span, :], wup[...])
        vec_ref[pl.ds(4 + part * pl.num_programs(0) + step, 1), :] = column_sums(sums)

    @pl.when(step == pl.num_programs(0) - 1)
    def _():
        sums = [jnp.zeros((8, z.width), wide) for _ in range(4)]
        for row in range(z.rows):
            for tile in tiles(z.block):
                here = z.at(row, tile)
                layer_ref[here, :] = (s_mid[here, :] + s_ffn[here, :] + db_ref[...]).astype(low)
                grad_out = cot_ref[row, tile, :].astype(wide)
                grad_second, normed = s_gsec[here, :], s_n2[here, :]
                inverse = s_r2[here, 0:1]
                grad_middle = grad_out + norm_backward(
                    grad_second, normed, inverse, gain_ref[...]
                )
                grad_branch = grad_middle.astype(low)
                gbr_ref[here, :] = grad_branch
                values = (grad_branch.astype(wide), grad_second * normed, grad_second, grad_out)
                sums = [total + fold_rows(value) for total, value in zip(sums, values)]
        for line, total in enumerate(sums):
            vec_ref[line : line + 1, :] = column_sums(total)
        grad_branch = gbr_ref[...]
        gnum_ref[:, 0:a] = dot_nt(grad_branch, wo_ref[...])
        gnum_ref[:, a : 2 * a] = dot_nt(grad_branch, wo2_ref[...])
        for row in range(z.rows):
            carried = cols_ref[z.span(row), 1:2]
            restart = cols_ref[row * z.block : row * z.block + 1, 4:5]
            table = jnp.zeros((z.block, LANES), wide)
            for pair in range(z.pairs):
                here = (z.span(row), lanes_of(pair))
                grad_att, norm = gnum_ref[here], s_norm[here]
                inverse = 1.0 / jnp.maximum(norm, 1.0)
                grad_num = grad_att * inverse
                gnum_ref[here] = grad_num
                along = head_sums(grad_att * s_att[here])
                grad_norm = jnp.where(norm > 1.0, -along * inverse, 0.0)
                lane = iota((z.block, LANES), 1)
                table = jnp.where(lane == 2 * pair, grad_norm[:, 0:1], table)
                table = jnp.where(
                    lane == 2 * pair + 1, grad_norm[:, HEAD_DIM : HEAD_DIM + 1], table
                )
                queries = qfeat_ref[here]
                high, rest = two_terms(grad_num * carried)
                product = dot_tn(queries, jnp.concatenate([high, rest], axis=1))
                product = product[:, 0:LANES] + product[:, LANES : 2 * LANES]
                total = column_sums(queries.astype(wide) * (grad_norm * carried))
                write_state(
                    z,
                    sent_ref,
                    held_ref,
                    row,
                    pair,
                    compact(product),
                    total,
                    restart,
                    s_min[0:1, :],
                )
            gnorm_ref[z.span(row), :] = table


def local_kernel(
    z,
    got_ref,
    weights_ref,
    qfeat_ref,
    kfeat_ref,
    vlow_ref,
    gnum_ref,
    gnorm_ref,
    qslope_ref,
    cols_ref,
    segs_ref,
    gq_ref,
    gq2_ref,
    gk_ref,
    gv_ref,
    vec_ref,
    held_ref,
):
    a = z.attn
    vec_ref[...] = jnp.zeros_like(vec_ref)
    half = z.pairs // 2
    for row in range(z.rows):
        mask = mask_of(z, cols_ref, segs_ref, row)
        carried = cols_ref[z.span(row), 1:2]
        for pair in range(z.pairs):
            here = (z.span(row), lanes_of(pair))
            queries, keys, values = qfeat_ref[here], kfeat_ref[here], vlow_ref[here]
            state, total = read_state(z, got_ref, held_ref, row, pair)
            high, rest = two_terms(two_blocks(state))
            grad_norm = spread_heads(gnorm_ref[z.span(row), 2 * pair : 2 * pair + 2])
            num_high, num_rest = two_terms(gnum_ref[here])
            grad_q = carried * (
                dot_nt(
                    jnp.concatenate([num_high, num_rest, num_high], axis=1),
                    jnp.concatenate([high, high, rest], axis=1),
                )
                + grad_norm * total
            )
            grad_k = jnp.zeros((z.block, LANES), wide)
            grad_v = jnp.zeros((z.block, LANES), wide)
            for head in range(2):
                grad_low = only_head(num_high, head)
                norm_col = grad_norm[:, head * HEAD_DIM : head * HEAD_DIM + 1]
                grad_scores = jnp.where(mask, dot_nt(grad_low, values) + norm_col, 0.0).astype(low)
                grad_q = grad_q + dot(grad_scores, only_head(keys, head))
                grad_k = grad_k + dot_tn(grad_scores, only_head(queries, head))
                weights = weights_ref[(row * z.pairs + pair) * 2 + head]
                grad_v = grad_v + dot_tn(weights, grad_low)
            gk_ref[here] = grad_k.astype(low)
            gv_ref[here] = grad_v.astype(low)
            grad_low = (grad_q * qslope_ref[here].astype(wide)).astype(low)
            out = gq_ref if pair < half else gq2_ref
            out[z.span(row), lanes_of(pair % half)] = grad_low
            vec_ref[0:1, lanes_of(pair)] += column_sums(grad_low.astype(wide))


def ffn_grad_kernel(
    z,
    mine_ref,
    act_ref,
    act2_ref,
    cot_ref,
    cot2_ref,
    second_ref,
    second2_ref,
    gup_ref,
    gup2_ref,
    down_keep_ref,
    down_give_ref,
    up_keep_ref,
    up_give_ref,
):
    c1 = cot_ref[...].reshape(z.toks, z.width)
    c2 = cot2_ref[...].reshape(z.toks, z.width)
    down = (dot_tn(act_ref[...], c1) + dot_tn(act2_ref[...], c2)).astype(low)
    up = dot_tn(second_ref[...], gup_ref[...]) + dot_tn(second2_ref[...], gup2_ref[...])
    up = up.astype(low)
    rows, fold = down.shape[0], z.width // up.shape[1]
    tall = z.width // fold
    for distance in range(4):
        down_out = down_give_ref if distance % 2 else down_keep_ref
        up_out = up_give_ref if distance // 2 else up_keep_ref

        @pl.when(pl.program_id(0) == distance)
        def _():
            start = (distance // 2) * rows
            down_out[start : start + rows, :] = down
            start = (distance % 2) * tall
            for i in range(fold):
                lanes = slice(i * up.shape[1], (i + 1) * up.shape[1])
                up_out[start : start + tall, lanes] = up[i * tall : (i + 1) * tall]


def added(kept, got):
    return (kept.astype(wide) + got.astype(wide)).astype(low)


def first_pair_kernel(down_ref, down_got, up_ref, up_got, dk_ref, dg_ref, uk_ref, ug_ref):
    half = dk_ref.shape[0]
    for kept, got, keep, give in (
        (down_ref, down_got, dk_ref, dg_ref),
        (up_ref, up_got, uk_ref, ug_ref),
    ):
        keep[...] = added(kept[0:half, :], got[0:half, :])
        give[...] = added(kept[half : 2 * half, :], got[half : 2 * half, :])


def second_pair_kernel(level, mine_ref, down_ref, down_got, up_ref, up_got, *outs):
    rows = outs[0].shape[0] // 2
    for distance, out_ref in enumerate(outs):
        start = jnp.bitwise_xor(mine_ref[1 + level.index], distance) * rows
        span = pl.ds(pl.multiple_of(start, rows), rows)
        out_ref[0:rows, :] = added(down_ref[span, :], down_got[span, :])
        out_ref[rows : 2 * rows, :] = added(up_ref[span, :], up_got[span, :])


def sum_kernel(level, mine_ref, *refs):
    pieces, outs = refs[: level.radix], refs[level.radix :]
    rows = outs[0].shape[0]
    place = mine_ref[1 + level.index + 1] if len(outs) > 1 else None
    for distance, out_ref in enumerate(outs):
        start = 0
        if place is not None:
            start = pl.multiple_of(jnp.bitwise_xor(place, distance) * rows, rows)
        total = pieces[0][pl.ds(start, rows), :].astype(wide)
        for piece in pieces[1:]:
            total = total + piece[pl.ds(start, rows), :].astype(wide)
        out_ref[...] = total.astype(low)


def join_kernel(level, mine_ref, *refs):
    pieces, outs = refs[: level.radix], refs[level.radix :]
    rows = pieces[0].shape[0] // len(outs)
    for distance, piece in enumerate(pieces):
        place = jnp.bitwise_xor(mine_ref[1 + level.index], distance)
        for i, out_ref in enumerate(outs):
            span = pl.ds(pl.multiple_of(place * rows, rows), rows)
            out_ref[span, :] = piece[i * rows : (i + 1) * rows, :]


def unpack_ffn_kernel(z, mine_ref, *refs):
    downs, ups, (down_ref, up_ref) = refs[:4], refs[4:8], refs[8:]
    rows = z.hidden // 4
    fold = z.width // rows
    tall = z.width // fold
    for distance in range(4):
        place = jnp.bitwise_xor(mine_ref[1], distance)
        span = pl.ds(pl.multiple_of(place * rows, rows), rows)
        down_ref[span, :] = downs[distance][...].astype(wide)
        for i in range(fold):
            lanes = slice(i * rows, (i + 1) * rows)
            up_ref[i * tall : (i + 1) * tall, span] = ups[distance][:, lanes].astype(wide)


def final_kernel(
    z,
    mine_ref,
    got_ref,
    kfeat_ref,
    vlow_ref,
    kslope_ref,
    gk_ref,
    gv_ref,
    cols_ref,
    gq_ref,
    gq2_ref,
    wq_ref,
    wq2_ref,
    wk_ref,
    wk2_ref,
    wv_ref,
    wv2_ref,
    tokens_ref,
    gain_ref,
    gbr_ref,
    vec_mid_ref,
    vec_loc_ref,
    gk1_ref,
    gk2_ref,
    gv1_ref,
    gv2_ref,
    gtok_ref,
    keep_ref,
    give_ref,
    held_ref,
    s_first,
):
    a = z.attn
    half = z.pairs // 2
    keep_ref[...] = jnp.zeros_like(keep_ref)
    give_ref[...] = jnp.zeros_like(give_ref)
    for row in range(z.rows):
        last = cols_ref[z.span(row), 2:3]
        for pair in range(z.pairs):
            here = (z.span(row), lanes_of(pair))
            keys, values = kfeat_ref[here], vlow_ref[here]
            state, total = read_state(z, got_ref, held_ref, row, pair)
            high, rest = two_terms(two_blocks(state))
            grad_k = gk_ref[here].astype(wide) + last * (
                dot_nt(
                    jnp.concatenate([values, values], axis=1),
                    jnp.concatenate([high, rest], axis=1),
                )
                + total
            )
            grad_v = gv_ref[here].astype(wide) + last * dot(
                jnp.concatenate([keys, keys], axis=1), jnp.concatenate([high, rest], axis=0)
            )
            grad_k = (grad_k * kslope_ref[here].astype(wide)).astype(low)
            grad_v = grad_v.astype(low)
            out_k, out_v = (gk1_ref, gv1_ref) if pair < half else (gk2_ref, gv2_ref)
            there = (z.span(row), lanes_of(pair % half))
            out_k[there] = grad_k
            out_v[there] = grad_v
    halves = (
        (keep_ref, gq_ref, gk1_ref, gv1_ref, wq_ref, wk_ref, wv_ref, 0),
        (give_ref, gq2_ref, gk2_ref, gv2_ref, wq2_ref, wk2_ref, wv2_ref, 1),
    )
    steps = z.hidden // z.width
    for out, gq, gk, gv, wq, wk, wv, part in halves:
        partial = dot_nt(gq[...], wq[...]) + dot_nt(gk[...], wk[...])
        partial = partial + dot_nt(gv[...], wv[...])
        if part == 0:
            s_first[...] = partial
        else:
            s_first[...] += partial
        out[2:6, :] = vec_mid_ref[0:4, :]
        out[6:7, 0:a] = vec_loc_ref[0:1, part * a : (part + 1) * a]
        out[6:7, a : 2 * a] = column_sums(gk[...].astype(wide))
        out[7:8, 0:a] = column_sums(gv[...].astype(wide))
        out[8 : 8 + steps, :] = vec_mid_ref[4 + part * steps : 4 + (part + 1) * steps, :]
    sums = [jnp.zeros((8, z.width), wide) for _ in range(2)]
    for row in range(z.rows):
        for tile in tiles(z.block):
            here = z.at(row, tile)
            normed, inverse = normalize(tokens_ref[row, tile, :].astype(wide))
            grad_first = s_first[here, :]
            grad_tokens = norm_backward(grad_first, normed, inverse, gain_ref[...])
            gtok_ref[here, :] = (gbr_ref[here, :].astype(wide) + grad_tokens).astype(low)
            values = (grad_first * normed, grad_first)
            sums = [total + fold_rows(value) for total, value in zip(sums, values)]
    for line, total in enumerate(sums):
        for out in (keep_ref, give_ref):
            out[line : line + 1, :] = column_sums(total)


def attn_grad_kernel(
    z,
    radix,
    mine_ref,
    first_ref,
    first2_ref,
    gq_ref,
    gq2_ref,
    gk_ref,
    gk2_ref,
    gv_ref,
    gv2_ref,
    att_ref,
    att2_ref,
    gbr_ref,
    gbr2_ref,
    keep_ref,
    got_ref,
    *outs,
):
    outs, out_ref = outs[:radix], outs[radix]
    a, w = z.attn, z.width
    first, first2 = first_ref[...], first2_ref[...]
    out_ref[0:w, 0:a] = (dot_tn(first, gq_ref[...]) + dot_tn(first2, gq2_ref[...])).astype(low)
    out_ref[0:w, a : 2 * a] = (dot_tn(first, gk_ref[...]) + dot_tn(first2, gk2_ref[...])).astype(
        low
    )
    grad_v = (dot_tn(first, gv_ref[...]) + dot_tn(first2, gv2_ref[...])).astype(low)
    half = w // 2
    out_ref[w : w + half, 0:a] = grad_v[0:half]
    out_ref[w : w + half, a : 2 * a] = grad_v[half:w]
    out_ref[w + half : w + half + a, :] = (
        dot_tn(att_ref[...], gbr_ref[...]) + dot_tn(att2_ref[...], gbr2_ref[...])
    ).astype(low)
    start = w + half + a
    out_ref[start:, :] = jnp.zeros((out_ref.shape[0] - start, w), low)
    out_ref[start : start + 16, :] = (keep_ref[...] + got_ref[...]).astype(low)
    for distance, out in enumerate(outs):
        rows = out.shape[0]
        first_row = jnp.bitwise_xor(mine_ref[1], distance) * rows
        out[...] = out_ref[pl.ds(pl.multiple_of(first_row, rows), rows), :]


def place_kernel(mine_ref, one_ref, one2_ref, two_ref, two2_ref, out_one_ref, out_two_ref):
    step = pl.program_id(0)

    @pl.when(step == 0)
    def _():
        out_one_ref[...] = one_ref[...].reshape(out_one_ref.shape)
        out_two_ref[...] = two_ref[...].reshape(out_two_ref.shape).astype(wide)

    @pl.when(step == 1)
    def _():
        out_one_ref[...] = one2_ref[...].reshape(out_one_ref.shape)
        out_two_ref[...] = two2_ref[...].reshape(out_two_ref.shape).astype(wide)


def unpack_attn_kernel(z, level, mine_ref, *refs):
    pieces, refs = refs[: level.radix], refs[level.radix :]
    lowest_ref, lowest2_ref, q_ref, k_ref, v_ref, o_ref = refs[:6]
    vecs, sums_ref = refs[6:17], refs[17]
    join_kernel(level, mine_ref, *pieces, sums_ref)
    a, w = z.attn, z.width
    half = w // 2
    q_ref[...] = sums_ref[0:w, 0:a].astype(wide)
    k_ref[...] = sums_ref[0:w, a : 2 * a].astype(wide)
    v_ref[0:half, :] = sums_ref[w : w + half, 0:a].astype(wide)
    v_ref[half:w, :] = sums_ref[w : w + half, a : 2 * a].astype(wide)
    o_ref[...] = sums_ref[w + half : w + half + a, :].astype(wide)
    start = w + half + a
    table = sums_ref[start : start + 16, :].astype(wide)
    g1, b1, ob, g2, b2, db, qb, kb, vb, upb, least = vecs
    for row, out in enumerate((g1, b1, ob, g2, b2, db)):
        out[...] = table[row : row + 1, :]
    qb[...] = table[6:7, 0:a]
    kb[...] = table[6:7, a : 2 * a]
    vb[...] = table[7:8, 0:a]
    for part in range(z.hidden // w):
        upb[:, part * w : (part + 1) * w] = table[8 + part : 9 + part, :]
    least[...] = jnp.minimum(lowest_ref[0:1, 0:1], lowest2_ref[0:1, 0:1])


def swap(value):
    return lax.ppermute(value, "mp", [(0, 1), (1, 0)])


def over_blocks(value):
    return lax.all_to_all(value, "seq", 0, 0)


class Level:
    def __init__(self, index, shift, radix):
        self.index, self.shift, self.radix = index, shift, radix

    def exchange(self, value, distance, count):
        other = distance << self.shift
        return lax.ppermute(value, "seq", [(i, i ^ other) for i in range(count)])


def levels_of(count):
    levels, shift = [], 0
    while (1 << shift) < count:
        radix = 4 if (4 << shift) <= count else 2
        levels.append(Level(len(levels), shift, radix))
        shift += 2 if radix == 4 else 1
    return levels


def shape(dims, kind):
    return jax.ShapeDtypeStruct(tuple(dims), kind)


HELD = pl.BlockSpec(memory_space=pltpu.VMEM)


def full(value):
    dims = tuple(value.shape)
    return pl.BlockSpec(dims, lambda *_: (0,) * len(dims))


def call(kernel, ins, outs, flops, mine=None, specs=None, out_specs=None, grid=(1,), scratch=(), limit=58, after=None, held=(), held_out=()):
    specs, out_specs = specs or {}, out_specs or {}
    in_list = [specs.get(i, full(value)) for i, value in enumerate(ins)]
    out_list = [out_specs.get(i, full(value)) for i, value in enumerate(outs)]
    in_list = [HELD if i in held else spec for i, spec in enumerate(in_list)]
    out_list = [HELD if i in held_out else spec for i, spec in enumerate(out_list)]
    moved = sum(v.size * v.dtype.itemsize for v in list(ins) + list(outs))
    head = 0 if mine is None else 1
    ins = list(ins)
    body = kernel
    if after is not None:
        spot = head + len(ins)
        in_list.append(pl.BlockSpec(memory_space=pl.ANY))
        ins.append(after)

        def body(*refs):
            kernel(*refs[:spot], *refs[spot + 1 :])

    return pl.pallas_call(
        body,
        grid_spec=pltpu.PrefetchScalarGridSpec(
            num_scalar_prefetch=head,
            grid=grid,
            in_specs=in_list,
            out_specs=out_list,
            scratch_shapes=list(scratch),
        ),
        out_shape=list(outs),
        compiler_params=pltpu.CompilerParams(vmem_limit_bytes=limit * MEBI),
        cost_estimate=pl.CostEstimate(flops=int(flops), bytes_accessed=int(moved), transcendentals=0),
    )(*(() if mine is None else (mine,)), *ins)


def per_device(
    tokens,
    first_gain,
    first_bias,
    query_weight,
    query_bias,
    key_weight,
    key_bias,
    value_weight,
    value_bias,
    output_weight,
    output_bias,
    second_gain,
    second_bias,
    up_weight,
    up_bias,
    down_weight,
    down_bias,
    cotangent,
    doc_starts,
    valid_mask,
):
    blocks = lax.axis_size("seq")
    shares = lax.axis_size("mp")
    all_rows, block, width = tokens.shape
    a, hidden = query_weight.shape[1], up_weight.shape[1]
    z = Sizes(blocks, all_rows // shares, block, width, a, hidden)
    t = z.toks
    levels = levels_of(blocks)
    me = lax.axis_index("seq")
    places = [(me >> level.shift) & (level.radix - 1) for level in levels]
    mine = jnp.stack([lax.axis_index("mp")] + places).astype(jnp.int32)

    def row(vector):
        return vector.reshape(1, vector.shape[0])

    g1, b1, g2, b2 = row(first_gain), row(first_bias), row(second_gain), row(second_bias)
    ob, db = row(output_bias), row(down_bias)
    wk2, wv2, wq2 = swap(key_weight), swap(value_weight), swap(query_weight)
    other_bias = swap(row(jnp.concatenate([query_bias, key_bias, value_bias, up_bias])))
    wo2, wup2, wd2 = swap(output_weight), swap(up_weight), swap(down_weight)

    def own_block(other=False):
        if other:
            return pl.BlockSpec((z.rows, block, width), lambda i, m: (1 - m[0], 0, 0))
        return pl.BlockSpec((z.rows, block, width), lambda i, m: (m[0], 0, 0))

    part = functools.partial
    sent_shape = shape((blocks, z.height, LANES), wide)
    state_scratch = pltpu.VMEM((HEAD_DIM, LANES), wide)
    thin = shape((t, LANES), wide)
    narrow, broad, half = shape((t, width), low), shape((t, width), wide), shape((t, a), low)

    first, kslope, kfeat, vlow, cols, segs, sent = call(
        part(project_kernel, z),
        (
            tokens,
            doc_starts,
            valid_mask,
            g1,
            b1,
            key_weight,
            wk2,
            row(key_bias),
            value_weight,
            wv2,
            row(value_bias),
            other_bias,
        ),
        (
            narrow,
            narrow,
            narrow,
            narrow,
            thin,
            shape((8 * z.rows, block), wide),
            sent_shape,
        ),
        4e9,
        mine,
        specs={0: own_block()},
        scratch=[state_scratch, pltpu.VMEM((2, t, a), wide)],
    )

    def scan(held, backward, after):
        return call(
            part(scan_kernel, z, backward),
            (held,),
            (sent_shape, shape((8, LANES), wide)),
            1e8,
            limit=8,
            after=after,
            held=(0,),
            held_out=(0, 1),
        )

    arriving = over_blocks(sent)
    qslope, qfeat, weights, within, sums = call(
        part(score_kernel, z),
        (first, query_weight, wq2, row(query_bias), other_bias, kfeat, vlow, cols, segs),
        (narrow, narrow, shape((z.rows * z.pairs * 2, block, block), low), broad, thin),
        4e9,
        scratch=[pltpu.VMEM((2, t, a), wide)],
    )
    entering, _ = scan(arriving, False, qfeat)
    entering = over_blocks(entering)
    steps = hidden // width
    up_block = pl.BlockSpec((width, width), lambda i, m: (0, i))
    down_block = pl.BlockSpec((width, width), lambda i, m: (i, 0))
    tok_block = pl.BlockSpec((t, width), lambda i, m: (0, i))
    bias_block = pl.BlockSpec((1, width), lambda i, m: (0, i))
    other_up = other_bias[:, 3 * a :]
    wider = shape((t, hidden), low)
    (
        layer,
        act,
        act2,
        gup,
        gup2,
        second,
        gbr,
        att,
        att2,
        gnum,
        gnorm,
        sent_back,
        vec_mid,
    ) = call(
        part(middle_kernel, z),
        (
            entering,
            qfeat,
            within,
            sums,
            cols,
            tokens,
            cotangent,
            output_weight,
            wo2,
            ob,
            g2,
            b2,
            up_weight,
            wup2,
            row(up_bias),
            other_up,
            down_weight,
            wd2,
            db,
        ),
        (
            narrow,
            wider,
            wider,
            wider,
            wider,
            narrow,
            narrow,
            half,
            half,
            broad,
            thin,
            sent_shape,
            shape((16, width), wide),
        ),
        12e9,
        mine,
        specs={
            5: own_block(),
            6: own_block(),
            12: up_block,
            13: up_block,
            14: bias_block,
            15: bias_block,
            16: down_block,
            17: down_block,
        },
        out_specs={1: tok_block, 2: tok_block, 3: tok_block, 4: tok_block},
        held=(0,),
        grid=(steps,),
        scratch=[
            pltpu.VMEM((t, width), wide),
            pltpu.VMEM((t, width), wide),
            pltpu.VMEM((t, LANES), wide),
            pltpu.VMEM((t, width), wide),
            pltpu.VMEM((t, width), wide),
            pltpu.VMEM((t, 2 * a), wide),
            pltpu.VMEM((t, 2 * a), wide),
            pltpu.VMEM((8, LANES), wide),
            state_scratch,
            pltpu.VMEM((z.rows, block, width), wide),
            pltpu.VMEM((z.rows, block, width), wide),
        ],
    )
    act_in, gup_in, second_in = swap(act2), swap(gup2), swap(second)
    leaving = over_blocks(sent_back)
    piece = hidden // 4
    act_block = pl.BlockSpec((t, piece), lambda i, m: (0, jnp.bitwise_xor(m[1], i)))
    two = shape((2 * piece, width), low)
    one = shape((piece, width), low)
    down_keep, down_give, up_keep, up_give = call(
        part(ffn_grad_kernel, z),
        (act, act_in, cotangent, cotangent, second, second_in, gup, gup_in),
        (two, two, two, two),
        4e9,
        mine,
        specs={
            0: act_block,
            1: act_block,
            2: own_block(),
            3: own_block(True),
            6: act_block,
            7: act_block,
        },
        grid=(4,),
    )

    def to(value, distance):
        return levels[0].exchange(value, distance, blocks)

    def spread(level, parts):
        return [parts[0]] + [level.exchange(p, d, blocks) for d, p in enumerate(parts) if d]

    def summed(number, parts, after):
        level = levels[number]
        following = levels[number + 1].radix if number + 1 < len(levels) else 1
        rows = parts[0].shape[0] // following
        return call(
            part(sum_kernel, level),
            parts,
            [shape((rows, width), low)] * following,
            1e6,
            mine,
            limit=8,
            after=after,
            held=range(len(parts)),
            held_out=range(following),
        )

    def joined(number, value, count, after):
        level = levels[number]
        rows = level.radix * value.shape[0] // count
        return call(
            part(join_kernel, level),
            spread(level, [value] * level.radix),
            [shape((rows, width), low)] * count,
            1e6,
            mine,
            limit=8,
            after=after,
            held=range(level.radix),
            held_out=range(count),
        )

    leaving, lowest = scan(leaving, True, down_keep)
    scanned = lowest
    leaving = over_blocks(leaving)
    down_got, up_got = to(down_give, 1), to(up_give, 2)
    gq, gq2, gk_local, gv_local, vec_loc = call(
        part(local_kernel, z),
        (entering, weights, qfeat, kfeat, vlow, gnum, gnorm, qslope, cols, segs),
        (half, half, narrow, narrow, shape((8, 2 * a), wide)),
        6e9,
        scratch=[state_scratch],
        after=scanned,
    )
    table = shape((16, width), wide)
    gk, gk2, gv, gv2, gtok, keep, give = call(
        part(final_kernel, z),
        (
            leaving,
            kfeat,
            vlow,
            kslope,
            gk_local,
            gv_local,
            cols,
            gq,
            gq2,
            query_weight,
            wq2,
            key_weight,
            wk2,
            value_weight,
            wv2,
            tokens,
            g1,
            gbr,
            vec_mid,
            vec_loc,
        ),
        (half, half, half, half, narrow, table, table),
        4e9,
        mine,
        specs={15: own_block()},
        scratch=[state_scratch, pltpu.VMEM((t, width), wide)],
        held=(0,),
    )
    down_keep, down_give, up_keep, up_give = call(
        first_pair_kernel,
        (down_keep, down_got, up_keep, up_got),
        (one, one, one, one),
        1e6,
        limit=8,
        after=keep,
        held=range(4),
        held_out=range(4),
    )
    down_got, up_got = to(down_give, 2), to(up_give, 1)
    unit = 16 * blocks
    height = -(-(2 * width + 16) // unit) * unit
    radix = levels[0].radix
    rest = call(
        part(attn_grad_kernel, z, radix),
        (
            first,
            swap(first),
            gq,
            swap(gq2),
            gk,
            swap(gk2),
            gv,
            swap(gv2),
            att,
            swap(att2),
            gbr,
            swap(gbr),
            keep,
            swap(give),
        ),
        [shape((height // radix, width), low)] * radix,
        2e9,
        mine,
        scratch=[pltpu.VMEM((height, width), low)],
        after=down_keep,
    )
    rest_done = rest[0]
    radix = levels[1].radix
    parts = call(
        part(second_pair_kernel, levels[1]),
        (down_keep, down_got, up_keep, up_got),
        [shape((2 * piece // radix, width), low)] * radix,
        1e6,
        mine,
        limit=8,
        after=rest_done,
        held=range(4),
        held_out=range(radix),
    )
    for number in range(1, len(levels)):
        parts = summed(number, spread(levels[number], parts), rest_done)
    (ffn,) = parts
    rest = summed(0, spread(levels[0], rest), ffn)
    for number in range(len(levels) - 1, 1, -1):
        (ffn,) = joined(number, ffn, 1, rest[0])
    down, up = joined(1, ffn, 2, rest[0])
    for number in range(1, len(levels)):
        rest = summed(number, spread(levels[number], rest), down)
    (rest,) = rest
    down_x, down_y, up_x, up_y = to(down, 1), to(down, 2), to(up, 1), to(up, 2)
    ffn_pieces = (down, down_x, down_y, to(down_y, 1), up, up_x, up_y, to(up_x, 2))
    placed = pl.BlockSpec(
        (z.rows, block, width), lambda i, m: (jnp.where(i == 0, m[0], 1 - m[0]), 0, 0)
    )
    layer_out, grad_tokens = call(
        place_kernel,
        (layer, swap(layer), gtok, swap(gtok)),
        (shape(tokens.shape, low), shape(tokens.shape, wide)),
        1e6,
        mine,
        out_specs={0: placed, 1: placed},
        grid=(2,),
        after=rest,
    )
    for number in range(len(levels) - 1, 0, -1):
        (rest,) = joined(number, rest, 1, grad_tokens)
    rest_pieces = spread(levels[0], [rest] * levels[0].radix)
    grad_down, grad_up = call(
        part(unpack_ffn_kernel, z),
        ffn_pieces,
        (shape((hidden, width), wide), shape((width, hidden), wide)),
        1e6,
        mine,
        after=rest,
    )
    (grad_q, grad_k, grad_v, grad_o, g1, b1, ob, g2, b2, db, qb, kb, vb, upb, least) = call(
        part(unpack_attn_kernel, z, levels[0]),
        (*rest_pieces, lowest, swap(lowest)),
        (
            shape((width, a), wide),
            shape((width, a), wide),
            shape((width, a), wide),
            shape((a, width), wide),
        )
        + tuple(shape((1, width), wide) for _ in range(6))
        + tuple(shape((1, a), wide) for _ in range(3))
        + (shape((1, hidden), wide), shape((1, 1), wide)),
        1e6,
        mine,
        scratch=[pltpu.VMEM((height, width), low)],
        after=grad_down,
    )

    def flat(table):
        return table.reshape(table.shape[1])

    return (
        layer_out,
        grad_tokens,
        least.reshape(()),
        flat(g1),
        flat(b1),
        grad_q,
        flat(qb),
        grad_k,
        flat(kb),
        grad_v,
        flat(vb),
        grad_o,
        flat(ob),
        flat(g2),
        flat(b2),
        grad_up,
        flat(upb),
        grad_down,
        flat(db),
    )


def solution(mesh):
    return jax.shard_map(
        per_device,
        mesh=mesh,
        in_specs=(
            P(None, "seq", None),
            P(),
            P(),
            P(None, "mp"),
            P("mp"),
            P(None, "mp"),
            P("mp"),
            P(None, "mp"),
            P("mp"),
            P("mp", None),
            P(),
            P(),
            P(),
            P(None, "mp"),
            P("mp"),
            P("mp", None),
            P(),
            P(None, "seq", None),
            P(None, "seq"),
            P(None, "seq"),
        ),
        out_specs=(
            P(None, "seq", None),
            P(None, "seq", None),
            P(),
            P(),
            P(),
            P(None, "mp"),
            P("mp"),
            P(None, "mp"),
            P("mp"),
            P(None, "mp"),
            P("mp"),
            P("mp", None),
            P(),
            P(),
            P(),
            P(None, "mp"),
            P("mp"),
            P("mp", None),
            P(),
        ),
        check_vma=False,
    )
```

```python
import functools

import jax
import jax.numpy as jnp
from jax import lax
from jax.experimental import pallas as pl
from jax.experimental.pallas import tpu as pltpu
from jax.sharding import PartitionSpec as P

HEAD_DIM = 64
LANES = 128
EPSILON = 1e-05
LARGE_VALUE = 1e30
TINY = 1e-30
ORDER = (
    "KF",
    "S",
    "KD",
    "KE",
    "p1",
    "KG",
    "p2",
    "P",
    "h1",
    "s1",
    "h2",
    "s2",
    "d1",
    "d2",
    "j",
    "c",
    "U3",
    "UB",
    "UA",
)
MEBI = 1024 * 1024

low = jnp.bfloat16
wide = jnp.float32


def dot(left, right):
    return jnp.dot(left, right, preferred_element_type=wide)


def dot_nt(left, right):
    return lax.dot_general(left, right, (((1,), (1,)), ((), ())), preferred_element_type=wide)


def dot_tn(left, right):
    return lax.dot_general(left, right, (((0,), (0,)), ((), ())), preferred_element_type=wide)


def iota(shape, dim):
    return lax.broadcasted_iota(jnp.int32, shape, dim)


def first_head(shape):
    return iota(shape, 1) < HEAD_DIM


def only_head(pair, head):
    keep = first_head(pair.shape) if head == 0 else jnp.logical_not(first_head(pair.shape))
    return jnp.where(keep, pair, jnp.zeros_like(pair))


def head_sums(pair):
    keep = first_head(pair.shape)
    one = jnp.sum(jnp.where(keep, pair, 0.0), axis=1, keepdims=True)
    two = jnp.sum(jnp.where(keep, 0.0, pair), axis=1, keepdims=True)
    return jnp.where(keep, one, two)


def spread_heads(columns):
    return jnp.where(first_head((columns.shape[0], LANES)), columns[:, 0:1], columns[:, 1:2])


def two_terms(value):
    high = value.astype(low)
    return high, (value - high.astype(wide)).astype(low)


def two_blocks(state):
    return jnp.concatenate([only_head(state, 0), only_head(state, 1)], axis=0)


def compact(product):
    return jnp.where(
        first_head((HEAD_DIM, LANES)), product[:HEAD_DIM], product[HEAD_DIM:]
    )


def normalize(values):
    average = jnp.mean(values, axis=1, keepdims=True)
    centred = values - average
    spread = jnp.mean(centred * centred, axis=1, keepdims=True)
    inverse = lax.rsqrt(spread + EPSILON)
    return (centred * inverse, inverse)


def norm_backward(grad_out, normed, inverse, gain_row):
    grad_normed = grad_out * gain_row
    first_term = jnp.mean(grad_normed, axis=1, keepdims=True)
    second_term = jnp.mean(grad_normed * normed, axis=1, keepdims=True)
    return inverse * (grad_normed - first_term - normed * second_term)


def column_sums(values):
    return jnp.sum(values, axis=0, keepdims=True)


TILE = 32


def tiles(count):
    return [slice(start, start + TILE) for start in range(0, count, TILE)]


def fold_rows(values):
    total = values[0:8]
    for start in range(8, values.shape[0], 8):
        total = total + values[start : start + 8]
    return total


class Sizes:
    def __init__(self, blocks, rows, block, width, attn, hidden):
        self.blocks, self.rows, self.block = blocks, rows, block
        self.width, self.attn, self.hidden = width, attn, hidden
        self.toks = rows * block
        self.pairs = 2 * attn // LANES
        self.group = blocks // (rows * self.pairs)
        self.slice = HEAD_DIM // self.group
        self.height = -(-(self.slice + 7) // 16) * 16

    def at(self, row, tile):
        return slice(row * self.block + tile.start, row * self.block + tile.stop)

    def span(self, row):
        return slice(row * self.block, (row + 1) * self.block)


def lanes_of(pair):
    return slice(pair * LANES, (pair + 1) * LANES)


def rows_in_lanes(rows):
    same = jnp.where(iota((LANES, LANES), 0) == iota((LANES, LANES), 1), 1.0, 0.0).astype(low)
    return dot_nt(same, rows)


def write_piece(z, sent_ref, index, stage_ref, body, total, centre, restart, extra):
    k = z.slice
    stage_ref[0:k, :] = body
    line = k
    for value in (total, centre):
        for term in two_terms(value):
            stage_ref[line : line + 1, :] = term.astype(wide)
            line += 1
    stage_ref[line : line + 1, :] = jnp.broadcast_to(restart, (1, LANES))
    for term in two_terms(extra):
        line += 1
        stage_ref[line : line + 1, :] = term.astype(wide)
    if z.height > k + 7:
        stage_ref[k + 7 : z.height, :] = jnp.zeros((z.height - k - 7, LANES), wide)
    sent_ref[index] = stage_ref[...].astype(low)


def pair_sum(piece, line):
    return piece[line : line + 1, :] + piece[line + 1 : line + 2, :]


def centred(state, spread):
    centre = column_sums(state) / jnp.maximum(column_sums(spread), TINY)
    high, rest = two_terms(centre)
    centre = high.astype(wide) + rest.astype(wide)
    return state - spread * centre, centre


def write_state(z, sent_ref, held_ref, stage_ref, row, pair, state, total, centre, restart, extra):
    number = row * z.pairs + pair
    if state is not None:
        held_ref[number] = state
    for step in range(z.group):
        index = number * z.group + step
        body = held_ref[number, step * z.slice : (step + 1) * z.slice, :]
        write_piece(z, sent_ref, index, stage_ref, body, total, centre, restart, extra)


def read_states(z, got_ref, held_ref, backward):
    lane = iota((1, LANES), 1)
    place = jnp.where(lane < HEAD_DIM, lane, lane - HEAD_DIM) // z.slice
    totals, centres = [], []
    for number in range(z.rows * z.pairs):
        total = jnp.zeros((1, LANES), wide)
        centre = jnp.zeros((HEAD_DIM, LANES), wide)
        for step in range(z.group):
            piece = got_ref[number * z.group + step].astype(wide)
            held_ref[number, step * z.slice : (step + 1) * z.slice, :] = piece[0 : z.slice, :]
            total = jnp.where(place == step, pair_sum(piece, z.slice), total)
            if not backward:
                here = iota((HEAD_DIM, LANES), 0) // z.slice == step
                centre = jnp.where(here, pair_sum(piece, z.slice + 2), centre)
        totals.append(total)
        centres.append(centre)
    if not backward:
        high, rest = two_terms(jnp.concatenate(totals, axis=0))
        columns = rows_in_lanes(jnp.concatenate([high, rest], axis=0))
        count = len(totals)
        columns = columns[:, 0:count] + columns[:, count : 2 * count]
        for number, centre in enumerate(centres):
            column = columns[:, number : number + 1]
            spread = jnp.where(
                first_head((HEAD_DIM, LANES)), column[0:HEAD_DIM], column[HEAD_DIM:LANES]
            )
            held_ref[number] = held_ref[number] + spread * centre
    return totals


def mask_of(z, cols_ref, segs_ref, row):
    here = cols_ref[z.span(row), 0:1]
    there = segs_ref[row * 8 : row * 8 + 1, :]
    shape = (z.block, z.block)
    return jnp.logical_and(here == there, iota(shape, 0) >= iota(shape, 1))


def project_kernel(
    z,
    mine_ref,
    tokens_ref,
    starts_ref,
    valid_ref,
    gain_ref,
    bias_ref,
    wk_ref,
    wk2_ref,
    bk_ref,
    wv_ref,
    wv2_ref,
    bv_ref,
    other_bias_ref,
    first_ref,
    kslope_ref,
    kfeat_ref,
    vlow_ref,
    cols_ref,
    segs_ref,
    sent_ref,
    means_ref,
    held_ref,
    stage_ref,
    pre_ref,
):
    mine = mine_ref[0]
    for row in range(z.rows):
        for tile in tiles(z.block):
            x = tokens_ref[row, tile, :].astype(wide)
            normed, _ = normalize(x)
            first_ref[z.at(row, tile), :] = (normed * gain_ref[...] + bias_ref[...]).astype(low)
    a = z.attn
    first = first_ref[...]
    for part, (wk, wv, bk, bv) in enumerate(
        (
            (wk_ref, wv_ref, bk_ref[...], bv_ref[...]),
            (wk2_ref, wv2_ref, other_bias_ref[:, a : 2 * a], other_bias_ref[:, 2 * a : 3 * a]),
        )
    ):
        lanes = slice(part * a, (part + 1) * a)
        pre_ref[part] = dot(first, wk[...])
        vlow_ref[:, lanes] = (dot(first, wv[...]) + bv).astype(low)
        for tile in tiles(z.toks):
            key_pre = pre_ref[part, tile, :] + bk
            kslope_ref[tile, lanes] = jax.nn.sigmoid(key_pre).astype(low)
            kfeat_ref[tile, lanes] = softplus(key_pre).astype(low)
    square = (z.block, z.block)
    upto = iota(square, 0) <= iota(square, 1)
    upper = jnp.where(upto, 1.0, 0.0).astype(low)
    since = jnp.where(iota(square, 0) >= iota(square, 1), 1.0, 0.0).astype(low)
    same = jnp.where(iota(square, 0) == iota(square, 1), 1.0, 0.0).astype(low)
    for row in range(z.rows):
        other = z.rows + row

        def pick(ref):
            value = jnp.where(mine == 0, ref[row : row + 1, :], ref[other : other + 1, :])
            return jnp.broadcast_to(value.astype(wide), (8, z.block)).astype(low)

        starts, valid = pick(starts_ref), pick(valid_ref)
        seg_row = dot(starts, upper)
        seg_col = dot_nt(since, starts)[:, 0:1]
        valid_col = dot_nt(same, valid)[:, 0:1]
        seg_end = seg_row[0:1, z.block - 1 : z.block]
        segs_ref[row * 8 : (row + 1) * 8, :] = jnp.where(valid.astype(wide) > 0.0, seg_row, -1.0)
        carried = jnp.where(seg_col == 0.0, 1.0, 0.0)
        last = jnp.where(jnp.logical_and(seg_col == seg_end, valid_col > 0.0), 1.0, 0.0)
        restart = jnp.where(seg_end > 0.0, 1.0, 0.0)
        lane = iota((z.block, LANES), 1)
        cols = jnp.where(lane == 0, seg_col, 0.0)
        cols = jnp.where(lane == 1, carried, cols)
        cols = jnp.where(lane == 2, last, cols)
        cols = jnp.where(lane == 3, valid_col, cols)
        cols = jnp.where(lane == 4, restart, cols)
        cols_ref[z.span(row), :] = cols
        for pair in range(z.pairs):
            keys = kfeat_ref[z.span(row), lanes_of(pair)].astype(wide) * last
            keys_low, values = keys.astype(low), vlow_ref[z.span(row), lanes_of(pair)]
            ones = jnp.ones((z.block, LANES), low)
            product = dot_tn(keys_low, jnp.concatenate([values, ones], axis=1))
            spread = compact(product[:, LANES : 2 * LANES])
            state, centre = centred(compact(product[:, 0:LANES]), spread)
            line = row * z.pairs + pair
            means_ref[line : line + 1, :] = column_sums(values.astype(wide)) * (1.0 / z.block)
            write_state(
                z,
                sent_ref,
                held_ref,
                stage_ref,
                row,
                pair,
                state,
                column_sums(keys),
                centre,
                restart,
                jnp.zeros((1, LANES), wide),
            )


def softplus(values):
    return jnp.maximum(values, 0.0) + jnp.log1p(jnp.exp(-jnp.abs(values)))


def scan_kernel(z, backward, mine_ref, held_ref, scanned_ref, lowest_ref, stage_ref, rows_ref, runs_ref):
    k = z.slice
    shift = (mine_ref[z.me] & (z.group - 1)) * k
    picks = []
    for head in range(2):
        hit = iota((k, LANES), 1) == iota((k, LANES), 0) + shift + head * HEAD_DIM
        picks.append(jnp.where(hit, 1.0, 0.0).astype(low))
    half = iota((k, LANES), 1) < HEAD_DIM
    lane = iota((k, LANES), 1)
    columns = [jnp.zeros((k, LANES), wide) for _ in range(2)]
    if not backward:
        for block in range(z.blocks):
            rows_ref[0, block : block + 1, :] = held_ref[block, k : k + 16, :].astype(wide)[0:1]
            rows_ref[1, block : block + 1, :] = held_ref[block, k : k + 16, :].astype(wide)[1:2]
        terms = [rows_ref[i].astype(low) for i in range(2)]
        columns = [dot_nt(pick, terms[0]) + dot_nt(pick, terms[1]) for pick in picks]
    run = jnp.zeros((k, LANES), wide)
    run_total = jnp.zeros((1, LANES), wide)
    run_spread = jnp.zeros((k, LANES), wide)
    least = jnp.full((1, LANES), LARGE_VALUE, wide)
    none = jnp.zeros((1, LANES), wide)
    for step in range(z.blocks):
        block = z.blocks - 1 - step if backward else step
        here = held_ref[block].astype(wide)
        state, total, centre = here[0:k], pair_sum(here, k), pair_sum(here, k + 2)
        keep = 1.0 - here[k + 4 : k + 5]
        least = jnp.minimum(least, pair_sum(here, k + 5))
        if backward:
            lost = (run - run.astype(low).astype(wide)) * centre
            for head in range(2):
                sums = jnp.sum(only_head(lost, head), axis=1, keepdims=True)
                columns[head] = jnp.where(lane == block, sums, columns[head])
            runs_ref[block] = run
            rows_ref[0, block : block + 1, :] = run_total
        else:
            body, middle = centred(run, run_spread)
            write_piece(z, scanned_ref, block, stage_ref, body, run_total, middle, none, none)
            spread = jnp.where(
                half, columns[0][:, block : block + 1], columns[1][:, block : block + 1]
            )
            state = state + spread * centre
            run_spread = spread + keep * run_spread
        run = state + keep * run
        run_total = total + keep * run_total
    if backward:
        moved = dot_tn(columns[0].astype(low), picks[0]) + dot_tn(columns[1].astype(low), picks[1])
        for block in range(z.blocks):
            total = rows_ref[0, block : block + 1, :] + moved[block : block + 1, :]
            write_piece(z, scanned_ref, block, stage_ref, runs_ref[block], total, none, none, none)
    lowest_ref[...] = jnp.broadcast_to(least, (8, LANES))


def score_kernel(
    z,
    first_ref,
    wq_ref,
    wq2_ref,
    bq_ref,
    other_bias_ref,
    kfeat_ref,
    vlow_ref,
    cols_ref,
    segs_ref,
    qslope_ref,
    qfeat_ref,
    weights_ref,
    within_ref,
    sums_ref,
    pre_ref,
):
    a = z.attn
    for part, (wq, bq) in enumerate(((wq_ref, bq_ref[...]), (wq2_ref, other_bias_ref[:, 0:a]))):
        lanes = slice(part * a, (part + 1) * a)
        pre_ref[part] = dot(first_ref[...], wq[...])
        for tile in tiles(z.toks):
            query_pre = pre_ref[part, tile, :] + bq
            qslope_ref[tile, lanes] = jax.nn.sigmoid(query_pre).astype(low)
            qfeat_ref[tile, lanes] = softplus(query_pre).astype(low)
    for row in range(z.rows):
        mask = mask_of(z, cols_ref, segs_ref, row)
        table = jnp.zeros((z.block, LANES), wide)
        for pair in range(z.pairs):
            here = (z.span(row), lanes_of(pair))
            queries, keys, values = qfeat_ref[here], kfeat_ref[here], vlow_ref[here]
            within = jnp.zeros((z.block, LANES), wide)
            sums = []
            for head in range(2):
                scores = jnp.where(mask, dot_nt(only_head(queries, head), keys), 0.0)
                weights = scores.astype(low)
                weights_ref[(row * z.pairs + pair) * 2 + head] = weights
                within = within + dot(weights, only_head(values, head))
                sums.append(jnp.sum(scores, axis=1, keepdims=True))
            within_ref[here] = within
            lane = iota((z.block, LANES), 1)
            table = jnp.where(lane == 2 * pair, sums[0], table)
            table = jnp.where(lane == 2 * pair + 1, sums[1], table)
        sums_ref[z.span(row), :] = table


def middle_kernel(
    z,
    mine_ref,
    got_ref,
    qfeat_ref,
    within_ref,
    sums_ref,
    cols_ref,
    tokens_ref,
    cot_ref,
    wo_ref,
    wo2_ref,
    ob_ref,
    gain_ref,
    bias_ref,
    wup_ref,
    wup2_ref,
    bup_ref,
    bup2_ref,
    wd_ref,
    wd2_ref,
    db_ref,
    means_ref,
    layer_ref,
    act_ref,
    act2_ref,
    gup_ref,
    gup2_ref,
    second_ref,
    gbr_ref,
    att_ref,
    att2_ref,
    gnum_ref,
    gnorm_ref,
    sent_ref,
    vec_ref,
    s_mid,
    s_n2,
    s_r2,
    s_ffn,
    s_gsec,
    s_att,
    s_norm,
    s_min,
    held_ref,
    stage_ref,
    s_lost,
    s_up,
    s_gact,
):
    step = pl.program_id(0)
    a = z.attn

    @pl.when(step == 0)
    def _():
        totals = read_states(z, got_ref, held_ref, False)
        least = jnp.full((1, 1), LARGE_VALUE, wide)
        for row in range(z.rows):
            carried = cols_ref[z.span(row), 1:2]
            valid = cols_ref[z.span(row), 3:4]
            for pair in range(z.pairs):
                here = (z.span(row), lanes_of(pair))
                state, total = held_ref[row * z.pairs + pair], totals[row * z.pairs + pair]
                high, rest = two_terms(two_blocks(state))
                queries = qfeat_ref[here]
                across = dot(
                    jnp.concatenate([queries, queries], axis=1),
                    jnp.concatenate([high, rest], axis=0),
                )
                norm = spread_heads(sums_ref[z.span(row), 2 * pair : 2 * pair + 2])
                norm = norm + carried * head_sums(queries.astype(wide) * total)
                s_norm[here] = norm
                seen = jnp.where(valid > 0.0, norm, LARGE_VALUE)
                seen = jnp.min(jnp.min(seen, axis=0, keepdims=True), axis=1, keepdims=True)
                least = jnp.minimum(least, seen)
                attended = (within_ref[here] + across * carried) / jnp.maximum(norm, 1.0)
                s_att[here] = attended
        s_min[...] = jnp.broadcast_to(least, (8, LANES))
        att_ref[...] = s_att[:, 0:a].astype(low)
        att2_ref[...] = s_att[:, a : 2 * a].astype(low)
        s_mid[...] = dot(att_ref[...], wo_ref[...]) + dot(att2_ref[...], wo2_ref[...])
        for row in range(z.rows):
            for tile in tiles(z.block):
                here = z.at(row, tile)
                middle = tokens_ref[row, tile, :].astype(wide) + s_mid[here, :] + ob_ref[...]
                s_mid[here, :] = middle
                normed, inverse = normalize(middle)
                s_n2[here, :] = normed
                s_r2[here, :] = jnp.broadcast_to(inverse, (TILE, LANES))
                second_ref[here, :] = (normed * gain_ref[...] + bias_ref[...]).astype(low)
        s_ffn[...] = jnp.zeros_like(s_ffn)
        s_gsec[...] = jnp.zeros_like(s_gsec)
        vec_ref[...] = jnp.zeros_like(vec_ref)

    for part, (wup, bup, wd, act_out, gup_out) in enumerate(
        (
            (wup_ref, bup_ref, wd_ref, act_ref, gup_ref),
            (wup2_ref, bup2_ref, wd2_ref, act2_ref, gup2_ref),
        )
    ):
        sums = jnp.zeros((8, bup.shape[1]), wide)
        for row in range(z.rows):
            span = z.span(row)
            s_up[row] = dot(second_ref[span, :], wup[...])
            s_gact[row] = dot_nt(cot_ref[row], wd[...])
            for tile in tiles(z.block):
                up = s_up[row, tile, :] + bup[...]
                share = 0.5 * (1.0 + lax.erf(up * 0.7071067811865476))
                density = 0.3989422804014327 * jnp.exp(-0.5 * up * up)
                act_out[z.at(row, tile), :] = (up * share).astype(low)
                gup = (s_gact[row, tile, :] * (share + up * density)).astype(low)
                gup_out[z.at(row, tile), :] = gup
                sums = sums + fold_rows(gup.astype(wide))
            s_ffn[span, :] += dot(act_out[span, :], wd[...])
            s_gsec[span, :] += dot_nt(gup_out[span, :], wup[...])
        vec_ref[pl.ds(4 + part * pl.num_programs(0) + step, 1), :] = column_sums(sums)

    @pl.when(step == pl.num_programs(0) - 1)
    def _():
        sums = [jnp.zeros((8, z.width), wide) for _ in range(4)]
        for row in range(z.rows):
            for tile in tiles(z.block):
                here = z.at(row, tile)
                layer_ref[here, :] = (s_mid[here, :] + s_ffn[here, :] + db_ref[...]).astype(low)
                grad_out = cot_ref[row, tile, :].astype(wide)
                grad_second, normed = s_gsec[here, :], s_n2[here, :]
                inverse = s_r2[here, 0:1]
                grad_middle = grad_out + norm_backward(
                    grad_second, normed, inverse, gain_ref[...]
                )
                grad_branch = grad_middle.astype(low)
                gbr_ref[here, :] = grad_branch
                values = (grad_branch.astype(wide), grad_second * normed, grad_second, grad_out)
                sums = [total + fold_rows(value) for total, value in zip(sums, values)]
        for line, total in enumerate(sums):
            vec_ref[line : line + 1, :] = column_sums(total)
        grad_branch = gbr_ref[...]
        gnum_ref[:, 0:a] = dot_nt(grad_branch, wo_ref[...])
        gnum_ref[:, a : 2 * a] = dot_nt(grad_branch, wo2_ref[...])
        totals, centres = [], []
        for row in range(z.rows):
            carried = cols_ref[z.span(row), 1:2]
            table = jnp.zeros((z.block, LANES), wide)
            for pair in range(z.pairs):
                here = (z.span(row), lanes_of(pair))
                grad_att, norm = gnum_ref[here], s_norm[here]
                inverse = 1.0 / jnp.maximum(norm, 1.0)
                grad_num = grad_att * inverse
                gnum_ref[here] = grad_num
                along = head_sums(grad_att * s_att[here])
                grad_norm = jnp.where(norm > 1.0, -along * inverse, 0.0)
                lane = iota((z.block, LANES), 1)
                table = jnp.where(lane == 2 * pair, grad_norm[:, 0:1], table)
                table = jnp.where(
                    lane == 2 * pair + 1, grad_norm[:, HEAD_DIM : HEAD_DIM + 1], table
                )
                queries = qfeat_ref[here]
                high, rest = two_terms(grad_num * carried)
                product = dot_tn(queries, jnp.concatenate([high, rest], axis=1))
                product = product[:, 0:LANES] + product[:, LANES : 2 * LANES]
                total = column_sums(queries.astype(wide) * (grad_norm * carried))
                state = compact(product)
                number = row * z.pairs + pair
                held_ref[number] = state
                centre = means_ref[number : number + 1, :].astype(low).astype(wide)
                lost = (state - state.astype(low).astype(wide)) * centre
                s_lost[number * LANES : (number + 1) * LANES, :] = two_blocks(lost).astype(low)
                totals.append(total)
                centres.append(centre)
            gnorm_ref[z.span(row), :] = table
        lost = dot_nt(jnp.ones((8, LANES), low), s_lost[...])
        for row in range(z.rows):
            restart = cols_ref[row * z.block : row * z.block + 1, 4:5]
            for pair in range(z.pairs):
                number = row * z.pairs + pair
                total = totals[number] + lost[0:1, lanes_of(number)]
                write_state(
                    z,
                    sent_ref,
                    held_ref,
                    stage_ref,
                    row,
                    pair,
                    None,
                    total,
                    centres[number],
                    restart,
                    s_min[0:1, :],
                )


def local_kernel(
    z,
    got_ref,
    weights_ref,
    qfeat_ref,
    kfeat_ref,
    vlow_ref,
    gnum_ref,
    gnorm_ref,
    qslope_ref,
    cols_ref,
    segs_ref,
    gq_ref,
    gq2_ref,
    gk_ref,
    gv_ref,
    vec_ref,
    held_ref,
):
    a = z.attn
    vec_ref[...] = jnp.zeros_like(vec_ref)
    half = z.pairs // 2
    totals = read_states(z, got_ref, held_ref, False)
    for row in range(z.rows):
        mask = mask_of(z, cols_ref, segs_ref, row)
        carried = cols_ref[z.span(row), 1:2]
        for pair in range(z.pairs):
            here = (z.span(row), lanes_of(pair))
            queries, keys, values = qfeat_ref[here], kfeat_ref[here], vlow_ref[here]
            state, total = held_ref[row * z.pairs + pair], totals[row * z.pairs + pair]
            high, rest = two_terms(two_blocks(state))
            grad_norm = spread_heads(gnorm_ref[z.span(row), 2 * pair : 2 * pair + 2])
            num_high, num_rest = two_terms(gnum_ref[here])
            grad_q = carried * (
                dot_nt(
                    jnp.concatenate([num_high, num_rest, num_high], axis=1),
                    jnp.concatenate([high, high, rest], axis=1),
                )
                + grad_norm * total
            )
            grad_k = jnp.zeros((z.block, LANES), wide)
            grad_v = jnp.zeros((z.block, LANES), wide)
            for head in range(2):
                grad_low = only_head(num_high, head)
                norm_col = grad_norm[:, head * HEAD_DIM : head * HEAD_DIM + 1]
                grad_scores = jnp.where(mask, dot_nt(grad_low, values) + norm_col, 0.0).astype(low)
                grad_q = grad_q + dot(grad_scores, only_head(keys, head))
                grad_k = grad_k + dot_tn(grad_scores, only_head(queries, head))
                weights = weights_ref[(row * z.pairs + pair) * 2 + head]
                grad_v = grad_v + dot_tn(weights, grad_low)
            gk_ref[here] = grad_k.astype(low)
            gv_ref[here] = grad_v.astype(low)
            grad_low = (grad_q * qslope_ref[here].astype(wide)).astype(low)
            out = gq_ref if pair < half else gq2_ref
            out[z.span(row), lanes_of(pair % half)] = grad_low
            vec_ref[0:1, lanes_of(pair)] += column_sums(grad_low.astype(wide))


def ffn_grad_kernel(
    z,
    mine_ref,
    act_ref,
    act2_ref,
    cot_ref,
    cot2_ref,
    second_ref,
    second2_ref,
    gup_ref,
    gup2_ref,
    down_keep_ref,
    down_give_ref,
    up_keep_ref,
    up_give_ref,
):
    c1 = cot_ref[...].reshape(z.toks, z.width)
    c2 = cot2_ref[...].reshape(z.toks, z.width)
    down = (dot_tn(act_ref[...], c1) + dot_tn(act2_ref[...], c2)).astype(low)
    up = dot_tn(second_ref[...], gup_ref[...]) + dot_tn(second2_ref[...], gup2_ref[...])
    up = up.astype(low)
    rows, fold = down.shape[0], z.width // up.shape[1]
    tall = z.width // fold
    for distance in range(4):
        down_out = down_give_ref if distance % 2 else down_keep_ref
        up_out = up_give_ref if distance // 2 else up_keep_ref

        @pl.when(pl.program_id(0) == distance)
        def _():
            start = (distance // 2) * rows
            down_out[start : start + rows, :] = down
            start = (distance % 2) * tall
            for i in range(fold):
                lanes = slice(i * up.shape[1], (i + 1) * up.shape[1])
                up_out[start : start + tall, lanes] = up[i * tall : (i + 1) * tall]


def added(kept, got):
    return (kept.astype(wide) + got.astype(wide)).astype(low)


def first_pair_kernel(down_ref, down_got, up_ref, up_got, dk_ref, dg_ref, uk_ref, ug_ref):
    half = dk_ref.shape[0]
    for kept, got, keep, give in (
        (down_ref, down_got, dk_ref, dg_ref),
        (up_ref, up_got, uk_ref, ug_ref),
    ):
        keep[...] = added(kept[0:half, :], got[0:half, :])
        give[...] = added(kept[half : 2 * half, :], got[half : 2 * half, :])


def second_pair_kernel(bit, mine_ref, down_ref, down_got, up_ref, up_got, keep_ref, give_ref):
    upper = mine_ref[bit] > 0
    down, up = added(down_ref[...], down_got[...]), added(up_ref[...], up_got[...])
    keep_ref[...] = jnp.where(upper, up, down)
    give_ref[...] = jnp.where(upper, down, up)


def halve_kernel(bit, mine_ref, kept_ref, got_ref, keep_ref, give_ref):
    rows = keep_ref.shape[0]
    here = pl.ds(pl.multiple_of(mine_ref[bit] * rows, rows), rows)
    there = pl.ds(pl.multiple_of((1 - mine_ref[bit]) * rows, rows), rows)
    keep_ref[...] = added(kept_ref[here, :], got_ref[here, :])
    give_ref[...] = added(kept_ref[there, :], got_ref[there, :])


def add_kernel(kept_ref, got_ref, out_ref):
    out_ref[...] = added(kept_ref[...], got_ref[...])


def double_kernel(bit, mine_ref, own_ref, got_ref, out_ref):
    rows = own_ref.shape[0]
    out_ref[pl.ds(pl.multiple_of(mine_ref[bit] * rows, rows), rows), :] = own_ref[...]
    out_ref[pl.ds(pl.multiple_of((1 - mine_ref[bit]) * rows, rows), rows), :] = got_ref[...]


def cut_kernel(one_ref, two_ref, first_ref, second_ref):
    rows = first_ref.shape[0]
    first_ref[...] = one_ref[0:rows, :]
    second_ref[...] = two_ref[rows : 2 * rows, :]


def sum_kernel(level, mine_ref, *refs):
    pieces, outs, seen = refs[: level.radix], refs[level.radix : -1], refs[-1]
    rows = pieces[0].shape[0] - 16
    place = mine_ref[1 + level.index]
    for distance, piece in enumerate(pieces):
        seen[jnp.bitwise_xor(place, distance)] = piece[rows : rows + 16, :].astype(wide)
    vectors = seen[0]
    for i in range(1, level.radix):
        vectors = vectors + seen[i]
    last = outs[-1].dtype == wide
    parts = outs[:-1] if last else outs
    part_rows = rows // len(parts)
    for distance, out_ref in enumerate(parts):
        start = 0
        if not last:
            start = jnp.bitwise_xor(mine_ref[1 + level.index + 1], distance) * part_rows
            start = pl.multiple_of(start, part_rows)
        total = pieces[0][pl.ds(start, part_rows), :].astype(wide)
        for piece in pieces[1:]:
            total = total + piece[pl.ds(start, part_rows), :].astype(wide)
        out_ref[0:part_rows, :] = total.astype(low)
        if not last:
            out_ref[part_rows : part_rows + 16, :] = vectors.astype(low)
    if last:
        outs[-1][...] = vectors


def join_kernel(level, mine_ref, *refs):
    pieces, out_ref = refs[: level.radix], refs[level.radix]
    rows = pieces[0].shape[0]
    for distance, piece in enumerate(pieces):
        place = jnp.bitwise_xor(mine_ref[1 + level.index], distance)
        out_ref[pl.ds(pl.multiple_of(place * rows, rows), rows), :] = piece[...]


def unpack_ffn_kernel(down_ref, up_ref, *refs):
    down_out, up_out = refs[-2:]
    rows = down_out.shape[0]
    fold = up_ref.shape[1] // rows
    down_out[...] = down_ref[...].astype(wide)
    tall = up_out.shape[0] // fold
    for i in range(fold):
        lanes = slice(i * rows, (i + 1) * rows)
        up_out[i * tall : (i + 1) * tall, :] = up_ref[:, lanes].astype(wide)


def unpack_three_kernel(mine_ref, own_ref, x_ref, y_ref, down_out, up_out):
    rows = down_out.shape[0]
    for step, ref in enumerate((own_ref, x_ref, y_ref)):

        @pl.when(pl.program_id(0) == step)
        def _():
            down, up = ref.at[0:rows, :], ref.at[rows : 2 * rows, :]
            unpack_ffn_kernel(down, up, down_out, up_out)


def unpack_far_kernel(mine_ref, down_ref, up_ref, down_old, up_old, down_out, up_out):
    unpack_ffn_kernel(down_ref, up_ref, down_out, up_out)


def final_kernel(
    z,
    mine_ref,
    got_ref,
    kfeat_ref,
    vlow_ref,
    kslope_ref,
    gk_ref,
    gv_ref,
    cols_ref,
    gq_ref,
    gq2_ref,
    wq_ref,
    wq2_ref,
    wk_ref,
    wk2_ref,
    wv_ref,
    wv2_ref,
    tokens_ref,
    gain_ref,
    gbr_ref,
    vec_mid_ref,
    vec_loc_ref,
    gk1_ref,
    gk2_ref,
    gv1_ref,
    gv2_ref,
    gtok_ref,
    keep_ref,
    give_ref,
    held_ref,
    s_first,
):
    a = z.attn
    half = z.pairs // 2
    totals = read_states(z, got_ref, held_ref, True)
    keep_ref[...] = jnp.zeros_like(keep_ref)
    give_ref[...] = jnp.zeros_like(give_ref)
    for row in range(z.rows):
        last = cols_ref[z.span(row), 2:3]
        for pair in range(z.pairs):
            here = (z.span(row), lanes_of(pair))
            keys, values = kfeat_ref[here], vlow_ref[here]
            state, total = held_ref[row * z.pairs + pair], totals[row * z.pairs + pair]
            high = two_blocks(state).astype(low)
            grad_k = gk_ref[here].astype(wide) + last * (
                dot_nt(values, high) + total
            )
            grad_v = gv_ref[here].astype(wide) + last * dot(keys, high)
            grad_k = (grad_k * kslope_ref[here].astype(wide)).astype(low)
            grad_v = grad_v.astype(low)
            out_k, out_v = (gk1_ref, gv1_ref) if pair < half else (gk2_ref, gv2_ref)
            there = (z.span(row), lanes_of(pair % half))
            out_k[there] = grad_k
            out_v[there] = grad_v
    halves = (
        (keep_ref, gq_ref, gk1_ref, gv1_ref, wq_ref, wk_ref, wv_ref, 0),
        (give_ref, gq2_ref, gk2_ref, gv2_ref, wq2_ref, wk2_ref, wv2_ref, 1),
    )
    steps = z.hidden // z.width
    for out, gq, gk, gv, wq, wk, wv, part in halves:
        partial = dot_nt(gq[...], wq[...]) + dot_nt(gk[...], wk[...])
        partial = partial + dot_nt(gv[...], wv[...])
        if part == 0:
            s_first[...] = partial
        else:
            s_first[...] += partial
        out[2:6, :] = vec_mid_ref[0:4, :]
        out[6:7, 0:a] = vec_loc_ref[0:1, part * a : (part + 1) * a]
        out[6:7, a : 2 * a] = column_sums(gk[...].astype(wide))
        out[7:8, 0:a] = column_sums(gv[...].astype(wide))
        out[8 : 8 + steps, :] = vec_mid_ref[4 + part * steps : 4 + (part + 1) * steps, :]
    sums = [jnp.zeros((8, z.width), wide) for _ in range(2)]
    for row in range(z.rows):
        for tile in tiles(z.block):
            here = z.at(row, tile)
            normed, inverse = normalize(tokens_ref[row, tile, :].astype(wide))
            grad_first = s_first[here, :]
            grad_tokens = norm_backward(grad_first, normed, inverse, gain_ref[...])
            gtok_ref[here, :] = (gbr_ref[here, :].astype(wide) + grad_tokens).astype(low)
            values = (grad_first * normed, grad_first)
            sums = [total + fold_rows(value) for total, value in zip(sums, values)]
    for line, total in enumerate(sums):
        for out in (keep_ref, give_ref):
            out[line : line + 1, :] = column_sums(total)


def attn_grad_kernel(
    z,
    radix,
    mine_ref,
    first_ref,
    first2_ref,
    gq_ref,
    gq2_ref,
    gk_ref,
    gk2_ref,
    gv_ref,
    gv2_ref,
    att_ref,
    att2_ref,
    gbr_ref,
    gbr2_ref,
    keep_ref,
    got_ref,
    *outs,
):
    outs, out_ref = outs[:radix], outs[radix]
    a, w = z.attn, z.width
    first, first2 = first_ref[...], first2_ref[...]
    out_ref[0:w, 0:a] = (dot_tn(first, gq_ref[...]) + dot_tn(first2, gq2_ref[...])).astype(low)
    out_ref[0:w, a : 2 * a] = (dot_tn(first, gk_ref[...]) + dot_tn(first2, gk2_ref[...])).astype(
        low
    )
    grad_v = (dot_tn(first, gv_ref[...]) + dot_tn(first2, gv2_ref[...])).astype(low)
    half = w // 2
    out_ref[w : w + half, 0:a] = grad_v[0:half]
    out_ref[w : w + half, a : 2 * a] = grad_v[half:w]
    out_ref[w + half : w + half + a, :] = (
        dot_tn(att_ref[...], gbr_ref[...]) + dot_tn(att2_ref[...], gbr2_ref[...])
    ).astype(low)
    start = w + half + a
    if out_ref.shape[0] > start:
        out_ref[start:, :] = jnp.zeros((out_ref.shape[0] - start, w), low)
    vectors = (keep_ref[...] + got_ref[...]).astype(low)
    for distance, out in enumerate(outs):
        rows = out.shape[0] - 16
        first_row = jnp.bitwise_xor(mine_ref[1], distance) * rows
        out[0:rows, :] = out_ref[pl.ds(pl.multiple_of(first_row, rows), rows), :]
        out[rows : rows + 16, :] = vectors


def place_kernel(mine_ref, one_ref, one2_ref, two_ref, two2_ref, out_one_ref, out_two_ref):
    step = pl.program_id(0)

    @pl.when(step == 0)
    def _():
        out_one_ref[...] = one_ref[...].reshape(out_one_ref.shape)
        out_two_ref[...] = two_ref[...].reshape(out_two_ref.shape).astype(wide)

    @pl.when(step == 1)
    def _():
        out_one_ref[...] = one2_ref[...].reshape(out_one_ref.shape)
        out_two_ref[...] = two2_ref[...].reshape(out_two_ref.shape).astype(wide)


def unpack_attn_kernel(z, level, mine_ref, *refs):
    pieces, refs = refs[: level.radix], refs[level.radix :]
    vec_ref, lowest_ref, lowest2_ref, q_ref, k_ref, v_ref, o_ref = refs[:7]
    vecs, sums_ref = refs[7:18], refs[18]
    join_kernel(level, mine_ref, *pieces, sums_ref)
    a, w = z.attn, z.width
    half = w // 2
    q_ref[...] = sums_ref[0:w, 0:a].astype(wide)
    k_ref[...] = sums_ref[0:w, a : 2 * a].astype(wide)
    v_ref[0:half, :] = sums_ref[w : w + half, 0:a].astype(wide)
    v_ref[half:w, :] = sums_ref[w : w + half, a : 2 * a].astype(wide)
    o_ref[...] = sums_ref[w + half : w + half + a, :].astype(wide)
    table = vec_ref[...]
    g1, b1, ob, g2, b2, db, qb, kb, vb, upb, least = vecs
    for row, out in enumerate((g1, b1, ob, g2, b2, db)):
        out[...] = table[row : row + 1, :]
    qb[...] = table[6:7, 0:a]
    kb[...] = table[6:7, a : 2 * a]
    vb[...] = table[7:8, 0:a]
    for part in range(z.hidden // w):
        upb[:, part * w : (part + 1) * w] = table[8 + part : 9 + part, :]
    least[...] = jnp.minimum(lowest_ref[0:1, 0:1], lowest2_ref[0:1, 0:1])


def swap(value):
    return lax.ppermute(value, "mp", [(0, 1), (1, 0)])


def over_blocks(value):
    return lax.all_to_all(value, "seq", 0, 0)


class Level:
    def __init__(self, index, shift, radix):
        self.index, self.shift, self.radix = index, shift, radix

    def exchange(self, value, distance, count):
        other = distance << self.shift
        return lax.ppermute(value, "seq", [(i, i ^ other) for i in range(count)])


def levels_of(count):
    levels, shift = [], 0
    while (1 << shift) < count:
        radix = 4 if (4 << shift) <= count else 2
        levels.append(Level(len(levels), shift, radix))
        shift += 2 if radix == 4 else 1
    return levels


def shape(dims, kind):
    return jax.ShapeDtypeStruct(tuple(dims), kind)


HELD = pl.BlockSpec(memory_space=pltpu.VMEM)
PLACED = pl.BlockSpec(memory_space=pl.ANY)


def full(value):
    dims = tuple(value.shape)
    return pl.BlockSpec(dims, lambda *_: (0,) * len(dims))


def call(kernel, ins, outs, flops, mine=None, specs=None, out_specs=None, grid=(1,), scratch=(), limit=58, after=None, held=(), held_out=(), mark=False, aliases=None):
    specs, out_specs = specs or {}, out_specs or {}
    in_list = [specs.get(i, full(value)) for i, value in enumerate(ins)]
    out_list = [out_specs.get(i, full(value)) for i, value in enumerate(outs)]
    in_list = [HELD if i in held else spec for i, spec in enumerate(in_list)]
    out_list = [HELD if i in held_out else spec for i, spec in enumerate(out_list)]
    moved = sum(v.size * v.dtype.itemsize for v in list(ins) + list(outs))
    head = 0 if mine is None else 1
    ins = list(ins)
    outs = list(outs)
    count_in, count_out = head + len(ins), len(outs)
    if after is not None:
        in_list.append(HELD)
        ins.append(after)
    if mark:
        out_list.append(HELD)
        outs.append(jax.ShapeDtypeStruct((8, LANES), wide))

    def body(*refs):
        refs = list(refs)
        if after is not None:
            refs.pop(count_in)
        if mark:
            mark_ref = refs.pop(count_in + count_out)
            mark_ref[...] = jnp.zeros((8, LANES), wide)
        kernel(*refs)

    return pl.pallas_call(
        body,
        grid_spec=pltpu.PrefetchScalarGridSpec(
            num_scalar_prefetch=head,
            grid=grid,
            in_specs=in_list,
            out_specs=out_list,
            scratch_shapes=list(scratch),
        ),
        out_shape=list(outs),
        input_output_aliases=aliases or {},
        compiler_params=pltpu.CompilerParams(vmem_limit_bytes=limit * MEBI),
        cost_estimate=pl.CostEstimate(flops=int(flops), bytes_accessed=int(moved), transcendentals=0),
    )(*(() if mine is None else (mine,)), *ins)


def per_device(
    tokens,
    first_gain,
    first_bias,
    query_weight,
    query_bias,
    key_weight,
    key_bias,
    value_weight,
    value_bias,
    output_weight,
    output_bias,
    second_gain,
    second_bias,
    up_weight,
    up_bias,
    down_weight,
    down_bias,
    cotangent,
    doc_starts,
    valid_mask,
):
    blocks = lax.axis_size("seq")
    shares = lax.axis_size("mp")
    all_rows, block, width = tokens.shape
    a, hidden = query_weight.shape[1], up_weight.shape[1]
    z = Sizes(blocks, all_rows // shares, block, width, a, hidden)
    t = z.toks
    levels = levels_of(blocks)
    me = lax.axis_index("seq")
    places = [(me >> level.shift) & (level.radix - 1) for level in levels]
    far_bits = [1 << k for k in range(2, blocks.bit_length() - 1)]
    signs = [(me & bit) // bit for bit in far_bits]
    mine = jnp.stack([lax.axis_index("mp")] + places + signs + [me]).astype(jnp.int32)
    z.me = mine.shape[0] - 1
    first_bit = 1 + len(levels)

    def row(vector):
        return vector.reshape(1, vector.shape[0])

    g1, b1, g2, b2 = row(first_gain), row(first_bias), row(second_gain), row(second_bias)
    ob, db = row(output_bias), row(down_bias)
    wk2, wv2, wq2 = swap(key_weight), swap(value_weight), swap(query_weight)
    other_bias = swap(row(jnp.concatenate([query_bias, key_bias, value_bias, up_bias])))
    wo2, wup2, wd2 = swap(output_weight), swap(up_weight), swap(down_weight)

    def own_block(other=False):
        if other:
            return pl.BlockSpec((z.rows, block, width), lambda i, m: (1 - m[0], 0, 0))
        return pl.BlockSpec((z.rows, block, width), lambda i, m: (m[0], 0, 0))

    part = functools.partial
    sent_shape = shape((blocks, z.height, LANES), low)
    stage = pltpu.VMEM((z.height, LANES), wide)
    state_scratch = pltpu.VMEM((z.rows * z.pairs, HEAD_DIM, LANES), wide)
    thin = shape((t, LANES), wide)
    narrow, broad, half = shape((t, width), low), shape((t, width), wide), shape((t, a), low)

    first, kslope, kfeat, vlow, cols, segs, sent, means = call(
        part(project_kernel, z),
        (
            tokens,
            doc_starts,
            valid_mask,
            g1,
            b1,
            key_weight,
            wk2,
            row(key_bias),
            value_weight,
            wv2,
            row(value_bias),
            other_bias,
        ),
        (
            narrow,
            narrow,
            narrow,
            narrow,
            thin,
            shape((8 * z.rows, block), wide),
            sent_shape,
            shape((z.rows * z.pairs, LANES), wide),
        ),
        4e9,
        mine,
        specs={0: own_block()},
        scratch=[state_scratch, stage, pltpu.VMEM((2, t, a), wide)],
    )

    def scan(held, backward, after):
        return call(
            part(scan_kernel, z, backward),
            (held,),
            (sent_shape, shape((8, LANES), wide)),
            1e8,
            mine,
            scratch=[
                stage,
                pltpu.VMEM((2, blocks, LANES), wide),
                pltpu.VMEM((blocks, z.slice, LANES), wide),
            ],
            limit=10,
            after=after,
            held=(0,),
            held_out=(0, 1),
        )

    arriving = over_blocks(sent)
    qslope, qfeat, weights, within, sums, mark = call(
        part(score_kernel, z),
        (first, query_weight, wq2, row(query_bias), other_bias, kfeat, vlow, cols, segs),
        (narrow, narrow, shape((z.rows * z.pairs * 2, block, block), low), broad, thin),
        4e9,
        scratch=[pltpu.VMEM((2, t, a), wide)],
        mark=True,
    )
    entering, _ = scan(arriving, False, mark)
    entering = over_blocks(entering)
    steps = hidden // width
    up_block = pl.BlockSpec((width, width), lambda i, m: (0, i))
    down_block = pl.BlockSpec((width, width), lambda i, m: (i, 0))
    tok_block = pl.BlockSpec((t, width), lambda i, m: (0, i))
    bias_block = pl.BlockSpec((1, width), lambda i, m: (0, i))
    other_up = other_bias[:, 3 * a :]
    wider = shape((t, hidden), low)
    (
        layer,
        act,
        act2,
        gup,
        gup2,
        second,
        gbr,
        att,
        att2,
        gnum,
        gnorm,
        sent_back,
        vec_mid,
    ) = call(
        part(middle_kernel, z),
        (
            entering,
            qfeat,
            within,
            sums,
            cols,
            tokens,
            cotangent,
            output_weight,
            wo2,
            ob,
            g2,
            b2,
            up_weight,
            wup2,
            row(up_bias),
            other_up,
            down_weight,
            wd2,
            db,
            means,
        ),
        (
            narrow,
            wider,
            wider,
            wider,
            wider,
            narrow,
            narrow,
            half,
            half,
            broad,
            thin,
            sent_shape,
            shape((16, width), wide),
        ),
        12e9,
        mine,
        specs={
            5: own_block(),
            6: own_block(),
            12: up_block,
            13: up_block,
            14: bias_block,
            15: bias_block,
            16: down_block,
            17: down_block,
        },
        out_specs={1: tok_block, 2: tok_block, 3: tok_block, 4: tok_block},
        held=(0,),
        grid=(steps,),
        scratch=[
            pltpu.VMEM((t, width), wide),
            pltpu.VMEM((t, width), wide),
            pltpu.VMEM((t, LANES), wide),
            pltpu.VMEM((t, width), wide),
            pltpu.VMEM((t, width), wide),
            pltpu.VMEM((t, 2 * a), wide),
            pltpu.VMEM((t, 2 * a), wide),
            pltpu.VMEM((8, LANES), wide),
            state_scratch,
            stage,
            pltpu.VMEM((z.rows * z.pairs * LANES, LANES), low),
            pltpu.VMEM((z.rows, block, width), wide),
            pltpu.VMEM((z.rows, block, width), wide),
        ],
    )
    act_in, gup_in, second_in = swap(act2), swap(gup2), swap(second)
    piece = hidden // 4
    act_block = pl.BlockSpec((t, piece), lambda i, m: (0, jnp.bitwise_xor(m[1], i)))
    two = shape((2 * piece, width), low)
    one = shape((piece, width), low)
    table = shape((16, width), wide)
    height = max(2 * width, 16 * blocks)
    radix = levels[0].radix

    def to(value, distance):
        return levels[0].exchange(value, distance, blocks)

    def far(value, bit):
        return lax.ppermute(value, "seq", [(i, i ^ bit) for i in range(blocks)])

    def spread(level, parts):
        return [parts[0]] + [level.exchange(p, d, blocks) for d, p in enumerate(parts) if d]

    def small(kernel, ins, dims, after, scalars=None, scratch=()):
        outs = [shape(dim, low) if isinstance(dim, tuple) else dim for dim in dims]
        *outs, marks["last"] = call(
            kernel,
            ins,
            outs,
            1e6,
            scalars,
            limit=8,
            after=after,
            held=range(len(ins)),
            held_out=range(len(outs)),
            mark=True,
            scratch=scratch,
        )
        return outs

    marks = {}

    def summed(number, parts, after):
        level = levels[number]
        rows = parts[0].shape[0] - 16
        outs = [shape((rows, width), low), shape((16, width), wide)]
        if number + 1 < len(levels):
            following = levels[number + 1].radix
            outs = [shape((rows // following + 16, width), low)] * following
        seen = [pltpu.VMEM((level.radix, 16, width), wide)]
        return small(part(sum_kernel, level), parts, outs, after, mine, seen)

    def joined(number, value, after):
        level = levels[number]
        dims = [(level.radix * value.shape[0], width)]
        parts = spread(level, [value] * level.radix)
        return small(part(join_kernel, level), parts, dims, after, mine)[0]

    v = {"leaving": over_blocks(sent_back)}

    def ffn_gradients(after):
        down_keep, down_give, up_keep, up_give, mark = call(
            part(ffn_grad_kernel, z),
            (act, act_in, cotangent, cotangent, second, second_in, gup, gup_in),
            (two, two, two, two),
            4e9,
            mine,
            specs={
                0: act_block,
                1: act_block,
                2: own_block(),
                3: own_block(True),
                6: act_block,
                7: act_block,
            },
            grid=(4,),
            after=after,
            mark=True,
        )
        v["down"], v["up"] = (down_keep, to(down_give, 1)), (up_keep, to(up_give, 2))
        return mark

    def backward_scan(after):
        leaving, v["lowest"] = scan(v["leaving"], True, after)
        v["leaving"] = over_blocks(leaving)
        return v["lowest"]

    def local_gradients(after):
        *v["local"], mark = call(
            part(local_kernel, z),
            (entering, weights, qfeat, kfeat, vlow, gnum, gnorm, qslope, cols, segs),
            (half, half, narrow, narrow, shape((8, 2 * a), wide)),
            6e9,
            scratch=[state_scratch],
            after=after,
            mark=True,
        )
        return mark

    def final_gradients(after):
        gq, gq2, gk_local, gv_local, vec_loc = v["local"]
        *v["final"], mark = call(
            part(final_kernel, z),
            (
                v["leaving"],
                kfeat,
                vlow,
                kslope,
                gk_local,
                gv_local,
                cols,
                gq,
                gq2,
                query_weight,
                wq2,
                key_weight,
                wk2,
                value_weight,
                wv2,
                tokens,
                g1,
                gbr,
                vec_mid,
                vec_loc,
            ),
            (half, half, half, half, narrow, table, table),
            4e9,
            mine,
            specs={15: own_block()},
            scratch=[state_scratch, pltpu.VMEM((t, width), wide)],
            held=(0,),
            after=after,
            mark=True,
        )
        return mark

    def first_pair(after):
        dims = [(piece, width)] * 4
        ins = v["down"] + v["up"]
        down_keep, down_give, up_keep, up_give = small(first_pair_kernel, ins, dims, after)
        v["down"], v["up"] = (down_keep, to(down_give, 2)), (up_keep, to(up_give, 1))
        return marks["last"]

    def attn_gradients(after):
        gq, gq2 = v["local"][:2]
        gk, gk2, gv, gv2, _, keep, give = v["final"]
        *v["rest"], mark = call(
            part(attn_grad_kernel, z, radix),
            (
                first,
                swap(first),
                gq,
                swap(gq2),
                gk,
                swap(gk2),
                gv,
                swap(gv2),
                att,
                swap(att2),
                gbr,
                swap(gbr),
                keep,
                swap(give),
            ),
            [shape((height // radix + 16, width), low)] * radix,
            2e9,
            mine,
            scratch=[pltpu.VMEM((height, width), low)],
            after=after,
            mark=True,
        )
        v["rest"] = spread(levels[0], v["rest"])
        return mark

    def second_pair(after):
        dims = [(piece, width)] * 2
        ins = v["down"] + v["up"]
        keep, give = small(part(second_pair_kernel, first_bit), ins, dims, after, mine)
        v["ffn"] = (keep, far(give, far_bits[0]))
        return marks["last"]

    def first_half(after):
        dims = [(v["ffn"][0].shape[0] // 2, width)] * 2
        kernel = part(halve_kernel, first_bit + 1)
        keep, give = small(kernel, v["ffn"], dims, after, mine)
        v["ffn"] = (keep, far(give, far_bits[1]))
        return marks["last"]

    def last_half(after):
        for number in range(2, len(far_bits)):
            dims = [(v["ffn"][0].shape[0] // 2, width)] * 2
            kernel = part(halve_kernel, first_bit + number)
            keep, give = small(kernel, v["ffn"], dims, after, mine)
            v["ffn"] = (keep, far(give, far_bits[number]))
        (out,) = small(add_kernel, v["ffn"], [v["ffn"][0].shape], after)
        v["ffn"] = (out, far(out, far_bits[-1]))
        return marks["last"]

    def first_double(after):
        for number in reversed(range(1, len(far_bits))):
            dims = [(2 * v["ffn"][0].shape[0], width)]
            (out,) = small(part(double_kernel, first_bit + number), v["ffn"], dims, after, mine)
            v["ffn"] = (out, far(out, far_bits[number - 1]))
        return marks["last"]

    def last_double(after):
        dims = [(2 * v["ffn"][0].shape[0], width)]
        (out,) = small(part(double_kernel, first_bit), v["ffn"], dims, after, mine)
        v["ffn"] = (out, to(out, 1), to(out, 2))
        return marks["last"]

    def cut(after):
        out, out_x, out_y = v["ffn"]
        far_down, far_up = small(cut_kernel, (out_y, out_x), [(piece, width)] * 2, after)
        v["ffn"] = (out, out_x, out_y, to(far_down, 1), to(far_up, 2))
        return marks["last"]

    def first_sum(after):
        v["rest"] = summed(0, v["rest"], after)
        out = v["rest"][0]
        v["rest"] = spread(levels[1], v["rest"])
        return marks["last"]

    def last_sum(after):
        for number in range(1, len(levels)):
            v["rest"] = summed(number, v["rest"], after)
            if number + 1 < len(levels):
                v["rest"] = spread(levels[number + 1], v["rest"])
        return marks["last"]

    def join(after):
        out, v["vectors"] = v["rest"]
        for number in range(len(levels) - 1, 0, -1):
            out = joined(number, out, after)
        v["rest"] = spread(levels[0], [out] * radix)
        return marks["last"]

    def place(after):
        placed = pl.BlockSpec(
            (z.rows, block, width), lambda i, m: (jnp.where(i == 0, m[0], 1 - m[0]), 0, 0)
        )
        gtok = v["final"][4]
        *v["out"], mark = call(
            place_kernel,
            (layer, swap(layer), gtok, swap(gtok)),
            (shape(tokens.shape, low), shape(tokens.shape, wide)),
            1e6,
            mine,
            out_specs={0: placed, 1: placed},
            grid=(2,),
            after=after,
            mark=True,
        )
        return mark

    def piece_blocks(step):
        return [
            pl.BlockSpec((piece, width), lambda i, m: (jnp.bitwise_xor(m[1], i + step), 0)),
            pl.BlockSpec((width, piece), lambda i, m: (0, jnp.bitwise_xor(m[1], i + step))),
        ]

    def unpack_three(after):
        outs = (shape((hidden, width), wide), shape((width, hidden), wide))
        *v["grads"], mark = call(
            unpack_three_kernel,
            v["ffn"][:3],
            outs,
            1e6,
            mine,
            out_specs=dict(enumerate(piece_blocks(0))),
            grid=(3,),
            after=after,
            mark=True,
        )
        return mark

    def unpack_far(after):
        outs = (shape((hidden, width), wide), shape((width, hidden), wide))
        *v["ffn"], mark = call(
            unpack_far_kernel,
            (*v["ffn"][3:], *v["grads"]),
            outs,
            1e6,
            mine,
            specs={2: PLACED, 3: PLACED},
            out_specs=dict(enumerate(piece_blocks(3))),
            after=after,
            mark=True,
            aliases={3: 0, 4: 1},
        )
        return mark

    def unpack_attn(after):
        *v["rest"], mark = call(
            part(unpack_attn_kernel, z, levels[0]),
            (*v["rest"], v["vectors"], v["lowest"], swap(v["lowest"])),
            (
                shape((width, a), wide),
                shape((width, a), wide),
                shape((width, a), wide),
                shape((a, width), wide),
            )
            + tuple(shape((1, width), wide) for _ in range(6))
            + tuple(shape((1, a), wide) for _ in range(3))
            + (shape((1, hidden), wide), shape((1, 1), wide)),
            1e6,
            mine,
            scratch=[pltpu.VMEM((height, width), low)],
            after=after,
            mark=True,
        )
        return mark

    steps = dict(
        KF=ffn_gradients,
        S=backward_scan,
        KD=local_gradients,
        KE=final_gradients,
        KG=attn_gradients,
        p1=first_pair,
        p2=second_pair,
        h1=first_half,
        h2=last_half,
        d1=first_double,
        d2=last_double,
        c=cut,
        s1=first_sum,
        s2=last_sum,
        j=join,
        P=place,
        U3=unpack_three,
        UA=unpack_far,
        UB=unpack_attn,
    )
    after = None
    for name in ORDER:
        after = steps[name](after)
    layer_out, grad_tokens = v["out"]
    grad_down, grad_up = v["ffn"]
    grad_q, grad_k, grad_v, grad_o, g1, b1, ob, g2, b2, db, qb, kb, vb, upb, least = v["rest"]

    def flat(table):
        return table.reshape(table.shape[1])

    return (
        layer_out,
        grad_tokens,
        least.reshape(()),
        flat(g1),
        flat(b1),
        grad_q,
        flat(qb),
        grad_k,
        flat(kb),
        grad_v,
        flat(vb),
        grad_o,
        flat(ob),
        flat(g2),
        flat(b2),
        grad_up,
        flat(upb),
        grad_down,
        flat(db),
    )


def solution(mesh):
    return jax.shard_map(
        per_device,
        mesh=mesh,
        in_specs=(
            P(None, "seq", None),
            P(),
            P(),
            P(None, "mp"),
            P("mp"),
            P(None, "mp"),
            P("mp"),
            P(None, "mp"),
            P("mp"),
            P("mp", None),
            P(),
            P(),
            P(),
            P(None, "mp"),
            P("mp"),
            P("mp", None),
            P(),
            P(None, "seq", None),
            P(None, "seq"),
            P(None, "seq"),
        ),
        out_specs=(
            P(None, "seq", None),
            P(None, "seq", None),
            P(),
            P(),
            P(),
            P(None, "mp"),
            P("mp"),
            P(None, "mp"),
            P("mp"),
            P(None, "mp"),
            P("mp"),
            P("mp", None),
            P(),
            P(),
            P(),
            P(None, "mp"),
            P("mp"),
            P("mp", None),
            P(),
        ),
        check_vma=False,
    )
```

```python
import functools

import jax
import jax.numpy as jnp
from jax import lax
from jax.experimental import pallas as pl
from jax.experimental.pallas import tpu as pltpu
from jax.sharding import PartitionSpec as P

HEAD_DIM = 64
LANES = 128
EPSILON = 1e-05
LARGE_VALUE = 1e30
TINY = 1e-30
ORDER = (
    "KF",
    "S",
    "KD",
    "KE",
    "p1",
    "KG",
    "p2",
    "P",
    "h1",
    "h2",
    "s1",
    "s2",
    "d1",
    "d2",
    "j",
    "c",
    "U3",
    "UB",
    "UA",
)
MEBI = 1024 * 1024

low = jnp.bfloat16
wide = jnp.float32


def dot(left, right):
    return jnp.dot(left, right, preferred_element_type=wide)


def dot_nt(left, right):
    return lax.dot_general(left, right, (((1,), (1,)), ((), ())), preferred_element_type=wide)


def dot_tn(left, right):
    return lax.dot_general(left, right, (((0,), (0,)), ((), ())), preferred_element_type=wide)


def iota(shape, dim):
    return lax.broadcasted_iota(jnp.int32, shape, dim)


def first_head(shape):
    return iota(shape, 1) < HEAD_DIM


def only_head(pair, head):
    keep = first_head(pair.shape) if head == 0 else jnp.logical_not(first_head(pair.shape))
    return jnp.where(keep, pair, jnp.zeros_like(pair))


def head_sums(pair):
    keep = first_head(pair.shape)
    one = jnp.sum(jnp.where(keep, pair, 0.0), axis=1, keepdims=True)
    two = jnp.sum(jnp.where(keep, 0.0, pair), axis=1, keepdims=True)
    return jnp.where(keep, one, two)


def spread_heads(columns):
    return jnp.where(first_head((columns.shape[0], LANES)), columns[:, 0:1], columns[:, 1:2])


def two_terms(value):
    high = value.astype(low)
    return high, (value - high.astype(wide)).astype(low)


def two_blocks(state):
    return jnp.concatenate([only_head(state, 0), only_head(state, 1)], axis=0)


def compact(product):
    return jnp.where(
        first_head((HEAD_DIM, LANES)), product[:HEAD_DIM], product[HEAD_DIM:]
    )


def normalize(values):
    average = jnp.mean(values, axis=1, keepdims=True)
    centred = values - average
    spread = jnp.mean(centred * centred, axis=1, keepdims=True)
    inverse = lax.rsqrt(spread + EPSILON)
    return (centred * inverse, inverse)


def norm_backward(grad_out, normed, inverse, gain_row):
    grad_normed = grad_out * gain_row
    first_term = jnp.mean(grad_normed, axis=1, keepdims=True)
    second_term = jnp.mean(grad_normed * normed, axis=1, keepdims=True)
    return inverse * (grad_normed - first_term - normed * second_term)


def column_sums(values):
    return jnp.sum(values, axis=0, keepdims=True)


TILE = 32


def tiles(count):
    return [slice(start, start + TILE) for start in range(0, count, TILE)]


def fold_rows(values):
    total = values[0:8]
    for start in range(8, values.shape[0], 8):
        total = total + values[start : start + 8]
    return total


class Sizes:
    def __init__(self, blocks, rows, block, width, attn, hidden):
        self.blocks, self.rows, self.block = blocks, rows, block
        self.width, self.attn, self.hidden = width, attn, hidden
        self.toks = rows * block
        self.pairs = 2 * attn // LANES
        self.group = blocks // (rows * self.pairs)
        self.slice = HEAD_DIM // self.group
        self.height = -(-(self.slice + 7) // 16) * 16

    def at(self, row, tile):
        return slice(row * self.block + tile.start, row * self.block + tile.stop)

    def span(self, row):
        return slice(row * self.block, (row + 1) * self.block)


def lanes_of(pair):
    return slice(pair * LANES, (pair + 1) * LANES)


def rows_in_lanes(rows):
    same = jnp.where(iota((LANES, LANES), 0) == iota((LANES, LANES), 1), 1.0, 0.0).astype(low)
    return dot_nt(same, rows)


def write_piece(z, sent_ref, index, stage_ref, body, total, centre, restart, extra):
    k = z.slice
    stage_ref[0:k, :] = body
    line = k
    for value in (total, centre):
        for term in two_terms(value):
            stage_ref[line : line + 1, :] = term.astype(wide)
            line += 1
    stage_ref[line : line + 1, :] = jnp.broadcast_to(restart, (1, LANES))
    for term in two_terms(extra):
        line += 1
        stage_ref[line : line + 1, :] = term.astype(wide)
    if z.height > k + 7:
        stage_ref[k + 7 : z.height, :] = jnp.zeros((z.height - k - 7, LANES), wide)
    sent_ref[index] = stage_ref[...].astype(low)


def pair_sum(piece, line):
    return piece[line : line + 1, :] + piece[line + 1 : line + 2, :]


def centred(state, spread):
    centre = column_sums(state) / jnp.maximum(column_sums(spread), TINY)
    high, rest = two_terms(centre)
    centre = high.astype(wide) + rest.astype(wide)
    return state - spread * centre, centre


def write_state(z, sent_ref, held_ref, stage_ref, row, pair, state, total, centre, restart, extra):
    number = row * z.pairs + pair
    if state is not None:
        held_ref[number] = state
    for step in range(z.group):
        index = number * z.group + step
        body = held_ref[number, step * z.slice : (step + 1) * z.slice, :]
        write_piece(z, sent_ref, index, stage_ref, body, total, centre, restart, extra)


def read_states(z, got_ref, held_ref, backward):
    lane = iota((1, LANES), 1)
    place = jnp.where(lane < HEAD_DIM, lane, lane - HEAD_DIM) // z.slice
    totals, centres = [], []
    for number in range(z.rows * z.pairs):
        total = jnp.zeros((1, LANES), wide)
        centre = jnp.zeros((HEAD_DIM, LANES), wide)
        for step in range(z.group):
            piece = got_ref[number * z.group + step].astype(wide)
            held_ref[number, step * z.slice : (step + 1) * z.slice, :] = piece[0 : z.slice, :]
            total = jnp.where(place == step, pair_sum(piece, z.slice), total)
            if not backward:
                here = iota((HEAD_DIM, LANES), 0) // z.slice == step
                centre = jnp.where(here, pair_sum(piece, z.slice + 2), centre)
        totals.append(total)
        centres.append(centre)
    if not backward:
        high, rest = two_terms(jnp.concatenate(totals, axis=0))
        columns = rows_in_lanes(jnp.concatenate([high, rest], axis=0))
        count = len(totals)
        columns = columns[:, 0:count] + columns[:, count : 2 * count]
        for number, centre in enumerate(centres):
            column = columns[:, number : number + 1]
            spread = jnp.where(
                first_head((HEAD_DIM, LANES)), column[0:HEAD_DIM], column[HEAD_DIM:LANES]
            )
            held_ref[number] = held_ref[number] + spread * centre
    return totals


def mask_of(z, cols_ref, segs_ref, row):
    here = cols_ref[z.span(row), 0:1]
    there = segs_ref[row * 8 : row * 8 + 1, :]
    shape = (z.block, z.block)
    return jnp.logical_and(here == there, iota(shape, 0) >= iota(shape, 1))


def project_kernel(
    z,
    mine_ref,
    tokens_ref,
    starts_ref,
    valid_ref,
    gain_ref,
    bias_ref,
    wk_ref,
    wk2_ref,
    bk_ref,
    wv_ref,
    wv2_ref,
    bv_ref,
    other_bias_ref,
    first_ref,
    kslope_ref,
    kfeat_ref,
    vlow_ref,
    cols_ref,
    segs_ref,
    sent_ref,
    means_ref,
    held_ref,
    stage_ref,
    pre_ref,
):
    mine = mine_ref[0]
    for row in range(z.rows):
        for tile in tiles(z.block):
            x = tokens_ref[row, tile, :].astype(wide)
            normed, _ = normalize(x)
            first_ref[z.at(row, tile), :] = (normed * gain_ref[...] + bias_ref[...]).astype(low)
    a = z.attn
    first = first_ref[...]
    for part, (wk, wv, bk, bv) in enumerate(
        (
            (wk_ref, wv_ref, bk_ref[...], bv_ref[...]),
            (wk2_ref, wv2_ref, other_bias_ref[:, a : 2 * a], other_bias_ref[:, 2 * a : 3 * a]),
        )
    ):
        lanes = slice(part * a, (part + 1) * a)
        pre_ref[part] = dot(first, wk[...])
        vlow_ref[:, lanes] = (dot(first, wv[...]) + bv).astype(low)
        for tile in tiles(z.toks):
            key_pre = pre_ref[part, tile, :] + bk
            kslope_ref[tile, lanes] = jax.nn.sigmoid(key_pre).astype(low)
            kfeat_ref[tile, lanes] = softplus(key_pre).astype(low)
    square = (z.block, z.block)
    upto = iota(square, 0) <= iota(square, 1)
    upper = jnp.where(upto, 1.0, 0.0).astype(low)
    since = jnp.where(iota(square, 0) >= iota(square, 1), 1.0, 0.0).astype(low)
    same = jnp.where(iota(square, 0) == iota(square, 1), 1.0, 0.0).astype(low)
    for row in range(z.rows):
        other = z.rows + row

        def pick(ref):
            value = jnp.where(mine == 0, ref[row : row + 1, :], ref[other : other + 1, :])
            return jnp.broadcast_to(value.astype(wide), (8, z.block)).astype(low)

        starts, valid = pick(starts_ref), pick(valid_ref)
        seg_row = dot(starts, upper)
        seg_col = dot_nt(since, starts)[:, 0:1]
        valid_col = dot_nt(same, valid)[:, 0:1]
        seg_end = seg_row[0:1, z.block - 1 : z.block]
        segs_ref[row * 8 : (row + 1) * 8, :] = jnp.where(valid.astype(wide) > 0.0, seg_row, -1.0)
        carried = jnp.where(seg_col == 0.0, 1.0, 0.0)
        last = jnp.where(jnp.logical_and(seg_col == seg_end, valid_col > 0.0), 1.0, 0.0)
        restart = jnp.where(seg_end > 0.0, 1.0, 0.0)
        lane = iota((z.block, LANES), 1)
        cols = jnp.where(lane == 0, seg_col, 0.0)
        cols = jnp.where(lane == 1, carried, cols)
        cols = jnp.where(lane == 2, last, cols)
        cols = jnp.where(lane == 3, valid_col, cols)
        cols = jnp.where(lane == 4, restart, cols)
        cols_ref[z.span(row), :] = cols
        for pair in range(z.pairs):
            keys = kfeat_ref[z.span(row), lanes_of(pair)].astype(wide) * last
            keys_low, values = keys.astype(low), vlow_ref[z.span(row), lanes_of(pair)]
            ones = jnp.ones((z.block, LANES), low)
            product = dot_tn(keys_low, jnp.concatenate([values, ones], axis=1))
            spread = compact(product[:, LANES : 2 * LANES])
            state, centre = centred(compact(product[:, 0:LANES]), spread)
            line = row * z.pairs + pair
            means_ref[line : line + 1, :] = column_sums(values.astype(wide)) * (1.0 / z.block)
            write_state(
                z,
                sent_ref,
                held_ref,
                stage_ref,
                row,
                pair,
                state,
                column_sums(keys),
                centre,
                restart,
                jnp.zeros((1, LANES), wide),
            )


def softplus(values):
    return jnp.maximum(values, 0.0) + jnp.log1p(jnp.exp(-jnp.abs(values)))


def scan_kernel(z, backward, mine_ref, held_ref, scanned_ref, lowest_ref, stage_ref, rows_ref, runs_ref):
    k = z.slice
    shift = (mine_ref[z.me] & (z.group - 1)) * k
    picks = []
    for head in range(2):
        hit = iota((k, LANES), 1) == iota((k, LANES), 0) + shift + head * HEAD_DIM
        picks.append(jnp.where(hit, 1.0, 0.0).astype(low))
    half = iota((k, LANES), 1) < HEAD_DIM
    lane = iota((k, LANES), 1)
    columns = [jnp.zeros((k, LANES), wide) for _ in range(2)]
    if not backward:
        for block in range(z.blocks):
            rows_ref[0, block : block + 1, :] = held_ref[block, k : k + 16, :].astype(wide)[0:1]
            rows_ref[1, block : block + 1, :] = held_ref[block, k : k + 16, :].astype(wide)[1:2]
        terms = [rows_ref[i].astype(low) for i in range(2)]
        columns = [dot_nt(pick, terms[0]) + dot_nt(pick, terms[1]) for pick in picks]
    run = jnp.zeros((k, LANES), wide)
    run_total = jnp.zeros((1, LANES), wide)
    run_spread = jnp.zeros((k, LANES), wide)
    least = jnp.full((1, LANES), LARGE_VALUE, wide)
    none = jnp.zeros((1, LANES), wide)
    for step in range(z.blocks):
        block = z.blocks - 1 - step if backward else step
        here = held_ref[block].astype(wide)
        state, total, centre = here[0:k], pair_sum(here, k), pair_sum(here, k + 2)
        keep = 1.0 - here[k + 4 : k + 5]
        least = jnp.minimum(least, pair_sum(here, k + 5))
        if backward:
            lost = (run - run.astype(low).astype(wide)) * centre
            for head in range(2):
                sums = jnp.sum(only_head(lost, head), axis=1, keepdims=True)
                columns[head] = jnp.where(lane == block, sums, columns[head])
            runs_ref[block] = run
            rows_ref[0, block : block + 1, :] = run_total
        else:
            body, middle = centred(run, run_spread)
            write_piece(z, scanned_ref, block, stage_ref, body, run_total, middle, none, none)
            spread = jnp.where(
                half, columns[0][:, block : block + 1], columns[1][:, block : block + 1]
            )
            state = state + spread * centre
            run_spread = spread + keep * run_spread
        run = state + keep * run
        run_total = total + keep * run_total
    if backward:
        moved = dot_tn(columns[0].astype(low), picks[0]) + dot_tn(columns[1].astype(low), picks[1])
        for block in range(z.blocks):
            total = rows_ref[0, block : block + 1, :] + moved[block : block + 1, :]
            write_piece(z, scanned_ref, block, stage_ref, runs_ref[block], total, none, none, none)
    lowest_ref[...] = jnp.broadcast_to(least, (8, LANES))


def score_kernel(
    z,
    first_ref,
    wq_ref,
    wq2_ref,
    bq_ref,
    other_bias_ref,
    kfeat_ref,
    vlow_ref,
    cols_ref,
    segs_ref,
    qslope_ref,
    qfeat_ref,
    weights_ref,
    within_ref,
    sums_ref,
    pre_ref,
):
    a = z.attn
    for part, (wq, bq) in enumerate(((wq_ref, bq_ref[...]), (wq2_ref, other_bias_ref[:, 0:a]))):
        lanes = slice(part * a, (part + 1) * a)
        pre_ref[part] = dot(first_ref[...], wq[...])
        for tile in tiles(z.toks):
            query_pre = pre_ref[part, tile, :] + bq
            qslope_ref[tile, lanes] = jax.nn.sigmoid(query_pre).astype(low)
            qfeat_ref[tile, lanes] = softplus(query_pre).astype(low)
    for row in range(z.rows):
        mask = mask_of(z, cols_ref, segs_ref, row)
        table = jnp.zeros((z.block, LANES), wide)
        for pair in range(z.pairs):
            here = (z.span(row), lanes_of(pair))
            queries, keys, values = qfeat_ref[here], kfeat_ref[here], vlow_ref[here]
            within = jnp.zeros((z.block, LANES), wide)
            sums = []
            for head in range(2):
                scores = jnp.where(mask, dot_nt(only_head(queries, head), keys), 0.0)
                weights = scores.astype(low)
                weights_ref[(row * z.pairs + pair) * 2 + head] = weights
                within = within + dot(weights, only_head(values, head))
                sums.append(jnp.sum(scores, axis=1, keepdims=True))
            within_ref[here] = within
            lane = iota((z.block, LANES), 1)
            table = jnp.where(lane == 2 * pair, sums[0], table)
            table = jnp.where(lane == 2 * pair + 1, sums[1], table)
        sums_ref[z.span(row), :] = table


def middle_kernel(
    z,
    mine_ref,
    got_ref,
    qfeat_ref,
    within_ref,
    sums_ref,
    cols_ref,
    tokens_ref,
    cot_ref,
    wo_ref,
    wo2_ref,
    ob_ref,
    gain_ref,
    bias_ref,
    wup_ref,
    wup2_ref,
    bup_ref,
    bup2_ref,
    wd_ref,
    wd2_ref,
    db_ref,
    means_ref,
    layer_ref,
    act_ref,
    act2_ref,
    gup_ref,
    gup2_ref,
    second_ref,
    gbr_ref,
    att_ref,
    att2_ref,
    gnum_ref,
    gnorm_ref,
    sent_ref,
    vec_ref,
    s_mid,
    s_n2,
    s_r2,
    s_ffn,
    s_gsec,
    s_att,
    s_norm,
    s_min,
    held_ref,
    stage_ref,
    s_lost,
    s_up,
    s_gact,
):
    step = pl.program_id(0)
    a = z.attn

    @pl.when(step == 0)
    def _():
        totals = read_states(z, got_ref, held_ref, False)
        least = jnp.full((1, 1), LARGE_VALUE, wide)
        for row in range(z.rows):
            carried = cols_ref[z.span(row), 1:2]
            valid = cols_ref[z.span(row), 3:4]
            for pair in range(z.pairs):
                here = (z.span(row), lanes_of(pair))
                state, total = held_ref[row * z.pairs + pair], totals[row * z.pairs + pair]
                high, rest = two_terms(two_blocks(state))
                queries = qfeat_ref[here]
                across = dot(
                    jnp.concatenate([queries, queries], axis=1),
                    jnp.concatenate([high, rest], axis=0),
                )
                norm = spread_heads(sums_ref[z.span(row), 2 * pair : 2 * pair + 2])
                norm = norm + carried * head_sums(queries.astype(wide) * total)
                s_norm[here] = norm
                seen = jnp.where(valid > 0.0, norm, LARGE_VALUE)
                seen = jnp.min(jnp.min(seen, axis=0, keepdims=True), axis=1, keepdims=True)
                least = jnp.minimum(least, seen)
                attended = (within_ref[here] + across * carried) / jnp.maximum(norm, 1.0)
                s_att[here] = attended
        s_min[...] = jnp.broadcast_to(least, (8, LANES))
        att_ref[...] = s_att[:, 0:a].astype(low)
        att2_ref[...] = s_att[:, a : 2 * a].astype(low)
        s_mid[...] = dot(att_ref[...], wo_ref[...]) + dot(att2_ref[...], wo2_ref[...])
        for row in range(z.rows):
            for tile in tiles(z.block):
                here = z.at(row, tile)
                middle = tokens_ref[row, tile, :].astype(wide) + s_mid[here, :] + ob_ref[...]
                s_mid[here, :] = middle
                normed, inverse = normalize(middle)
                s_n2[here, :] = normed
                s_r2[here, :] = jnp.broadcast_to(inverse, (TILE, LANES))
                second_ref[here, :] = (normed * gain_ref[...] + bias_ref[...]).astype(low)
        s_ffn[...] = jnp.zeros_like(s_ffn)
        s_gsec[...] = jnp.zeros_like(s_gsec)
        vec_ref[...] = jnp.zeros_like(vec_ref)

    for part, (wup, bup, wd, act_out, gup_out) in enumerate(
        (
            (wup_ref, bup_ref, wd_ref, act_ref, gup_ref),
            (wup2_ref, bup2_ref, wd2_ref, act2_ref, gup2_ref),
        )
    ):
        sums = jnp.zeros((8, bup.shape[1]), wide)
        for row in range(z.rows):
            span = z.span(row)
            s_up[row] = dot(second_ref[span, :], wup[...])
            s_gact[row] = dot_nt(cot_ref[row], wd[...])
            for tile in tiles(z.block):
                up = s_up[row, tile, :] + bup[...]
                share = 0.5 * (1.0 + lax.erf(up * 0.7071067811865476))
                density = 0.3989422804014327 * jnp.exp(-0.5 * up * up)
                act_out[z.at(row, tile), :] = (up * share).astype(low)
                gup = (s_gact[row, tile, :] * (share + up * density)).astype(low)
                gup_out[z.at(row, tile), :] = gup
                sums = sums + fold_rows(gup.astype(wide))
            s_ffn[span, :] += dot(act_out[span, :], wd[...])
            s_gsec[span, :] += dot_nt(gup_out[span, :], wup[...])
        vec_ref[pl.ds(4 + part * pl.num_programs(0) + step, 1), :] = column_sums(sums)

    @pl.when(step == pl.num_programs(0) - 1)
    def _():
        sums = [jnp.zeros((8, z.width), wide) for _ in range(4)]
        for row in range(z.rows):
            for tile in tiles(z.block):
                here = z.at(row, tile)
                layer_ref[here, :] = (s_mid[here, :] + s_ffn[here, :] + db_ref[...]).astype(low)
                grad_out = cot_ref[row, tile, :].astype(wide)
                grad_second, normed = s_gsec[here, :], s_n2[here, :]
                inverse = s_r2[here, 0:1]
                grad_middle = grad_out + norm_backward(
                    grad_second, normed, inverse, gain_ref[...]
                )
                grad_branch = grad_middle.astype(low)
                gbr_ref[here, :] = grad_branch
                values = (grad_branch.astype(wide), grad_second * normed, grad_second, grad_out)
                sums = [total + fold_rows(value) for total, value in zip(sums, values)]
        for line, total in enumerate(sums):
            vec_ref[line : line + 1, :] = column_sums(total)
        grad_branch = gbr_ref[...]
        gnum_ref[:, 0:a] = dot_nt(grad_branch, wo_ref[...])
        gnum_ref[:, a : 2 * a] = dot_nt(grad_branch, wo2_ref[...])
        totals, centres = [], []
        for row in range(z.rows):
            carried = cols_ref[z.span(row), 1:2]
            table = jnp.zeros((z.block, LANES), wide)
            for pair in range(z.pairs):
                here = (z.span(row), lanes_of(pair))
                grad_att, norm = gnum_ref[here], s_norm[here]
                inverse = 1.0 / jnp.maximum(norm, 1.0)
                grad_num = grad_att * inverse
                gnum_ref[here] = grad_num
                along = head_sums(grad_att * s_att[here])
                grad_norm = jnp.where(norm > 1.0, -along * inverse, 0.0)
                lane = iota((z.block, LANES), 1)
                table = jnp.where(lane == 2 * pair, grad_norm[:, 0:1], table)
                table = jnp.where(
                    lane == 2 * pair + 1, grad_norm[:, HEAD_DIM : HEAD_DIM + 1], table
                )
                queries = qfeat_ref[here]
                high, rest = two_terms(grad_num * carried)
                product = dot_tn(queries, jnp.concatenate([high, rest], axis=1))
                product = product[:, 0:LANES] + product[:, LANES : 2 * LANES]
                total = column_sums(queries.astype(wide) * (grad_norm * carried))
                state = compact(product)
                number = row * z.pairs + pair
                held_ref[number] = state
                centre = means_ref[number : number + 1, :].astype(low).astype(wide)
                lost = (state - state.astype(low).astype(wide)) * centre
                s_lost[number * LANES : (number + 1) * LANES, :] = two_blocks(lost).astype(low)
                totals.append(total)
                centres.append(centre)
            gnorm_ref[z.span(row), :] = table
        lost = dot_nt(jnp.ones((8, LANES), low), s_lost[...])
        for row in range(z.rows):
            restart = cols_ref[row * z.block : row * z.block + 1, 4:5]
            for pair in range(z.pairs):
                number = row * z.pairs + pair
                total = totals[number] + lost[0:1, lanes_of(number)]
                write_state(
                    z,
                    sent_ref,
                    held_ref,
                    stage_ref,
                    row,
                    pair,
                    None,
                    total,
                    centres[number],
                    restart,
                    s_min[0:1, :],
                )


def local_kernel(
    z,
    got_ref,
    weights_ref,
    qfeat_ref,
    kfeat_ref,
    vlow_ref,
    gnum_ref,
    gnorm_ref,
    qslope_ref,
    cols_ref,
    segs_ref,
    gq_ref,
    gq2_ref,
    gk_ref,
    gv_ref,
    vec_ref,
    held_ref,
):
    a = z.attn
    vec_ref[...] = jnp.zeros_like(vec_ref)
    half = z.pairs // 2
    totals = read_states(z, got_ref, held_ref, False)
    for row in range(z.rows):
        mask = mask_of(z, cols_ref, segs_ref, row)
        carried = cols_ref[z.span(row), 1:2]
        for pair in range(z.pairs):
            here = (z.span(row), lanes_of(pair))
            queries, keys, values = qfeat_ref[here], kfeat_ref[here], vlow_ref[here]
            state, total = held_ref[row * z.pairs + pair], totals[row * z.pairs + pair]
            high, rest = two_terms(two_blocks(state))
            grad_norm = spread_heads(gnorm_ref[z.span(row), 2 * pair : 2 * pair + 2])
            num_high, num_rest = two_terms(gnum_ref[here])
            grad_q = carried * (
                dot_nt(
                    jnp.concatenate([num_high, num_rest, num_high], axis=1),
                    jnp.concatenate([high, high, rest], axis=1),
                )
                + grad_norm * total
            )
            grad_k = jnp.zeros((z.block, LANES), wide)
            grad_v = jnp.zeros((z.block, LANES), wide)
            for head in range(2):
                grad_low = only_head(num_high, head)
                norm_col = grad_norm[:, head * HEAD_DIM : head * HEAD_DIM + 1]
                grad_scores = jnp.where(mask, dot_nt(grad_low, values) + norm_col, 0.0).astype(low)
                grad_q = grad_q + dot(grad_scores, only_head(keys, head))
                grad_k = grad_k + dot_tn(grad_scores, only_head(queries, head))
                weights = weights_ref[(row * z.pairs + pair) * 2 + head]
                grad_v = grad_v + dot_tn(weights, grad_low)
            gk_ref[here] = grad_k.astype(low)
            gv_ref[here] = grad_v.astype(low)
            grad_low = (grad_q * qslope_ref[here].astype(wide)).astype(low)
            out = gq_ref if pair < half else gq2_ref
            out[z.span(row), lanes_of(pair % half)] = grad_low
            vec_ref[0:1, lanes_of(pair)] += column_sums(grad_low.astype(wide))


def ffn_grad_kernel(
    z,
    mine_ref,
    act_ref,
    act2_ref,
    cot_ref,
    cot2_ref,
    second_ref,
    second2_ref,
    gup_ref,
    gup2_ref,
    down_keep_ref,
    down_give_ref,
    up_keep_ref,
    up_give_ref,
):
    c1 = cot_ref[...].reshape(z.toks, z.width)
    c2 = cot2_ref[...].reshape(z.toks, z.width)
    down = (dot_tn(act_ref[...], c1) + dot_tn(act2_ref[...], c2)).astype(low)
    up = dot_tn(second_ref[...], gup_ref[...]) + dot_tn(second2_ref[...], gup2_ref[...])
    up = up.astype(low)
    rows, fold = down.shape[0], z.width // up.shape[1]
    tall = z.width // fold
    for distance in range(4):
        down_out = down_give_ref if distance % 2 else down_keep_ref
        up_out = up_give_ref if distance // 2 else up_keep_ref

        @pl.when(pl.program_id(0) == distance)
        def _():
            start = (distance // 2) * rows
            down_out[start : start + rows, :] = down
            start = (distance % 2) * tall
            for i in range(fold):
                lanes = slice(i * up.shape[1], (i + 1) * up.shape[1])
                up_out[start : start + tall, lanes] = up[i * tall : (i + 1) * tall]


def added(kept, got):
    return (kept.astype(wide) + got.astype(wide)).astype(low)


def first_pair_kernel(down_ref, down_got, up_ref, up_got, dk_ref, dg_ref, uk_ref, ug_ref):
    half = dk_ref.shape[0]
    for kept, got, keep, give in (
        (down_ref, down_got, dk_ref, dg_ref),
        (up_ref, up_got, uk_ref, ug_ref),
    ):
        keep[...] = added(kept[0:half, :], got[0:half, :])
        give[...] = added(kept[half : 2 * half, :], got[half : 2 * half, :])


def second_pair_kernel(bit, mine_ref, down_ref, down_got, up_ref, up_got, keep_ref, give_ref):
    upper = mine_ref[bit] > 0
    down, up = added(down_ref[...], down_got[...]), added(up_ref[...], up_got[...])
    keep_ref[...] = jnp.where(upper, up, down)
    give_ref[...] = jnp.where(upper, down, up)


def halve_kernel(bit, mine_ref, kept_ref, got_ref, keep_ref, give_ref):
    rows = keep_ref.shape[0]
    here = pl.ds(pl.multiple_of(mine_ref[bit] * rows, rows), rows)
    there = pl.ds(pl.multiple_of((1 - mine_ref[bit]) * rows, rows), rows)
    keep_ref[...] = added(kept_ref[here, :], got_ref[here, :])
    give_ref[...] = added(kept_ref[there, :], got_ref[there, :])


def add_kernel(kept_ref, got_ref, out_ref):
    out_ref[...] = added(kept_ref[...], got_ref[...])


def double_kernel(bit, mine_ref, own_ref, got_ref, out_ref):
    rows = own_ref.shape[0]
    out_ref[pl.ds(pl.multiple_of(mine_ref[bit] * rows, rows), rows), :] = own_ref[...]
    out_ref[pl.ds(pl.multiple_of((1 - mine_ref[bit]) * rows, rows), rows), :] = got_ref[...]


def cut_kernel(one_ref, two_ref, first_ref, second_ref):
    rows = first_ref.shape[0]
    first_ref[...] = one_ref[0:rows, :]
    second_ref[...] = two_ref[rows : 2 * rows, :]


def sum_kernel(level, mine_ref, *refs):
    pieces, outs, seen = refs[: level.radix], refs[level.radix : -1], refs[-1]
    rows = pieces[0].shape[0] - 16
    place = mine_ref[1 + level.index]
    for distance, piece in enumerate(pieces):
        seen[jnp.bitwise_xor(place, distance)] = piece[rows : rows + 16, :].astype(wide)
    vectors = seen[0]
    for i in range(1, level.radix):
        vectors = vectors + seen[i]
    last = outs[-1].dtype == wide
    parts = outs[:-1] if last else outs
    part_rows = rows // len(parts)
    for distance, out_ref in enumerate(parts):
        start = 0
        if not last:
            start = jnp.bitwise_xor(mine_ref[1 + level.index + 1], distance) * part_rows
            start = pl.multiple_of(start, part_rows)
        total = pieces[0][pl.ds(start, part_rows), :].astype(wide)
        for piece in pieces[1:]:
            total = total + piece[pl.ds(start, part_rows), :].astype(wide)
        out_ref[0:part_rows, :] = total.astype(low)
        if not last:
            out_ref[part_rows : part_rows + 16, :] = vectors.astype(low)
    if last:
        outs[-1][...] = vectors


def join_kernel(level, mine_ref, *refs):
    pieces, out_ref = refs[: level.radix], refs[level.radix]
    rows = pieces[0].shape[0]
    for distance, piece in enumerate(pieces):
        place = jnp.bitwise_xor(mine_ref[1 + level.index], distance)
        out_ref[pl.ds(pl.multiple_of(place * rows, rows), rows), :] = piece[...]


def unpack_ffn_kernel(down_ref, up_ref, *refs):
    down_out, up_out = refs[-2:]
    rows = down_out.shape[0]
    fold = up_ref.shape[1] // rows
    down_out[...] = down_ref[...].astype(wide)
    tall = up_out.shape[0] // fold
    for i in range(fold):
        lanes = slice(i * rows, (i + 1) * rows)
        up_out[i * tall : (i + 1) * tall, :] = up_ref[:, lanes].astype(wide)


def unpack_three_kernel(mine_ref, own_ref, x_ref, y_ref, down_out, up_out):
    rows = down_out.shape[0]
    for step, ref in enumerate((own_ref, x_ref, y_ref)):

        @pl.when(pl.program_id(0) == step)
        def _():
            down, up = ref.at[0:rows, :], ref.at[rows : 2 * rows, :]
            unpack_ffn_kernel(down, up, down_out, up_out)


def unpack_far_kernel(mine_ref, down_ref, up_ref, down_old, up_old, down_out, up_out):
    unpack_ffn_kernel(down_ref, up_ref, down_out, up_out)


def final_kernel(
    z,
    mine_ref,
    got_ref,
    kfeat_ref,
    vlow_ref,
    kslope_ref,
    gk_ref,
    gv_ref,
    cols_ref,
    gq_ref,
    gq2_ref,
    wq_ref,
    wq2_ref,
    wk_ref,
    wk2_ref,
    wv_ref,
    wv2_ref,
    tokens_ref,
    gain_ref,
    gbr_ref,
    vec_mid_ref,
    vec_loc_ref,
    gk1_ref,
    gk2_ref,
    gv1_ref,
    gv2_ref,
    gtok_ref,
    keep_ref,
    give_ref,
    held_ref,
    s_first,
):
    a = z.attn
    half = z.pairs // 2
    totals = read_states(z, got_ref, held_ref, True)
    keep_ref[...] = jnp.zeros_like(keep_ref)
    give_ref[...] = jnp.zeros_like(give_ref)
    for row in range(z.rows):
        last = cols_ref[z.span(row), 2:3]
        for pair in range(z.pairs):
            here = (z.span(row), lanes_of(pair))
            keys, values = kfeat_ref[here], vlow_ref[here]
            state, total = held_ref[row * z.pairs + pair], totals[row * z.pairs + pair]
            high = two_blocks(state).astype(low)
            grad_k = gk_ref[here].astype(wide) + last * (
                dot_nt(values, high) + total
            )
            grad_v = gv_ref[here].astype(wide) + last * dot(keys, high)
            grad_k = (grad_k * kslope_ref[here].astype(wide)).astype(low)
            grad_v = grad_v.astype(low)
            out_k, out_v = (gk1_ref, gv1_ref) if pair < half else (gk2_ref, gv2_ref)
            there = (z.span(row), lanes_of(pair % half))
            out_k[there] = grad_k
            out_v[there] = grad_v
    halves = (
        (keep_ref, gq_ref, gk1_ref, gv1_ref, wq_ref, wk_ref, wv_ref, 0),
        (give_ref, gq2_ref, gk2_ref, gv2_ref, wq2_ref, wk2_ref, wv2_ref, 1),
    )
    steps = z.hidden // z.width
    for out, gq, gk, gv, wq, wk, wv, part in halves:
        partial = dot_nt(gq[...], wq[...]) + dot_nt(gk[...], wk[...])
        partial = partial + dot_nt(gv[...], wv[...])
        if part == 0:
            s_first[...] = partial
        else:
            s_first[...] += partial
        out[2:6, :] = vec_mid_ref[0:4, :]
        out[6:7, 0:a] = vec_loc_ref[0:1, part * a : (part + 1) * a]
        out[6:7, a : 2 * a] = column_sums(gk[...].astype(wide))
        out[7:8, 0:a] = column_sums(gv[...].astype(wide))
        out[8 : 8 + steps, :] = vec_mid_ref[4 + part * steps : 4 + (part + 1) * steps, :]
    sums = [jnp.zeros((8, z.width), wide) for _ in range(2)]
    for row in range(z.rows):
        for tile in tiles(z.block):
            here = z.at(row, tile)
            normed, inverse = normalize(tokens_ref[row, tile, :].astype(wide))
            grad_first = s_first[here, :]
            grad_tokens = norm_backward(grad_first, normed, inverse, gain_ref[...])
            gtok_ref[here, :] = (gbr_ref[here, :].astype(wide) + grad_tokens).astype(low)
            values = (grad_first * normed, grad_first)
            sums = [total + fold_rows(value) for total, value in zip(sums, values)]
    for line, total in enumerate(sums):
        for out in (keep_ref, give_ref):
            out[line : line + 1, :] = column_sums(total)


def attn_grad_kernel(
    z,
    radix,
    mine_ref,
    first_ref,
    first2_ref,
    gq_ref,
    gq2_ref,
    gk_ref,
    gk2_ref,
    gv_ref,
    gv2_ref,
    att_ref,
    att2_ref,
    gbr_ref,
    gbr2_ref,
    keep_ref,
    got_ref,
    *outs,
):
    outs, out_ref = outs[:radix], outs[radix]
    a, w = z.attn, z.width
    first, first2 = first_ref[...], first2_ref[...]
    out_ref[0:w, 0:a] = (dot_tn(first, gq_ref[...]) + dot_tn(first2, gq2_ref[...])).astype(low)
    out_ref[0:w, a : 2 * a] = (dot_tn(first, gk_ref[...]) + dot_tn(first2, gk2_ref[...])).astype(
        low
    )
    grad_v = (dot_tn(first, gv_ref[...]) + dot_tn(first2, gv2_ref[...])).astype(low)
    half = w // 2
    out_ref[w : w + half, 0:a] = grad_v[0:half]
    out_ref[w : w + half, a : 2 * a] = grad_v[half:w]
    out_ref[w + half : w + half + a, :] = (
        dot_tn(att_ref[...], gbr_ref[...]) + dot_tn(att2_ref[...], gbr2_ref[...])
    ).astype(low)
    start = w + half + a
    if out_ref.shape[0] > start:
        out_ref[start:, :] = jnp.zeros((out_ref.shape[0] - start, w), low)
    vectors = (keep_ref[...] + got_ref[...]).astype(low)
    for distance, out in enumerate(outs):
        rows = out.shape[0] - 16
        first_row = jnp.bitwise_xor(mine_ref[1], distance) * rows
        out[0:rows, :] = out_ref[pl.ds(pl.multiple_of(first_row, rows), rows), :]
        out[rows : rows + 16, :] = vectors


def place_kernel(mine_ref, one_ref, one2_ref, two_ref, two2_ref, out_one_ref, out_two_ref):
    step = pl.program_id(0)

    @pl.when(step == 0)
    def _():
        out_one_ref[...] = one_ref[...].reshape(out_one_ref.shape)
        out_two_ref[...] = two_ref[...].reshape(out_two_ref.shape).astype(wide)

    @pl.when(step == 1)
    def _():
        out_one_ref[...] = one2_ref[...].reshape(out_one_ref.shape)
        out_two_ref[...] = two2_ref[...].reshape(out_two_ref.shape).astype(wide)


def unpack_attn_kernel(z, level, mine_ref, *refs):
    pieces, refs = refs[: level.radix], refs[level.radix :]
    vec_ref, lowest_ref, lowest2_ref, q_ref, k_ref, v_ref, o_ref = refs[:7]
    vecs, sums_ref = refs[7:18], refs[18]
    join_kernel(level, mine_ref, *pieces, sums_ref)
    a, w = z.attn, z.width
    half = w // 2
    q_ref[...] = sums_ref[0:w, 0:a].astype(wide)
    k_ref[...] = sums_ref[0:w, a : 2 * a].astype(wide)
    v_ref[0:half, :] = sums_ref[w : w + half, 0:a].astype(wide)
    v_ref[half:w, :] = sums_ref[w : w + half, a : 2 * a].astype(wide)
    o_ref[...] = sums_ref[w + half : w + half + a, :].astype(wide)
    table = vec_ref[...]
    g1, b1, ob, g2, b2, db, qb, kb, vb, upb, least = vecs
    for row, out in enumerate((g1, b1, ob, g2, b2, db)):
        out[...] = table[row : row + 1, :]
    qb[...] = table[6:7, 0:a]
    kb[...] = table[6:7, a : 2 * a]
    vb[...] = table[7:8, 0:a]
    for part in range(z.hidden // w):
        upb[:, part * w : (part + 1) * w] = table[8 + part : 9 + part, :]
    least[...] = jnp.minimum(lowest_ref[0:1, 0:1], lowest2_ref[0:1, 0:1])


def swap(value):
    return lax.ppermute(value, "mp", [(0, 1), (1, 0)])


def over_blocks(value):
    return lax.all_to_all(value, "seq", 0, 0)


class Level:
    def __init__(self, index, shift, radix):
        self.index, self.shift, self.radix = index, shift, radix

    def exchange(self, value, distance, count):
        other = distance << self.shift
        return lax.ppermute(value, "seq", [(i, i ^ other) for i in range(count)])


def levels_of(count):
    levels, shift = [], 0
    while (1 << shift) < count:
        radix = 4 if (4 << shift) <= count else 2
        levels.append(Level(len(levels), shift, radix))
        shift += 2 if radix == 4 else 1
    return levels


def shape(dims, kind):
    return jax.ShapeDtypeStruct(tuple(dims), kind)


HELD = pl.BlockSpec(memory_space=pltpu.VMEM)
PLACED = pl.BlockSpec(memory_space=pl.ANY)


def full(value):
    dims = tuple(value.shape)
    return pl.BlockSpec(dims, lambda *_: (0,) * len(dims))


def call(kernel, ins, outs, flops, mine=None, specs=None, out_specs=None, grid=(1,), scratch=(), limit=58, after=None, held=(), held_out=(), mark=False, aliases=None):
    specs, out_specs = specs or {}, out_specs or {}
    in_list = [specs.get(i, full(value)) for i, value in enumerate(ins)]
    out_list = [out_specs.get(i, full(value)) for i, value in enumerate(outs)]
    in_list = [HELD if i in held else spec for i, spec in enumerate(in_list)]
    out_list = [HELD if i in held_out else spec for i, spec in enumerate(out_list)]
    moved = sum(v.size * v.dtype.itemsize for v in list(ins) + list(outs))
    head = 0 if mine is None else 1
    ins = list(ins)
    outs = list(outs)
    count_in, count_out = head + len(ins), len(outs)
    if after is not None:
        in_list.append(HELD)
        ins.append(after)
    if mark:
        out_list.append(HELD)
        outs.append(jax.ShapeDtypeStruct((8, LANES), wide))

    def body(*refs):
        refs = list(refs)
        if after is not None:
            refs.pop(count_in)
        if mark:
            mark_ref = refs.pop(count_in + count_out)
            mark_ref[...] = jnp.zeros((8, LANES), wide)
        kernel(*refs)

    return pl.pallas_call(
        body,
        grid_spec=pltpu.PrefetchScalarGridSpec(
            num_scalar_prefetch=head,
            grid=grid,
            in_specs=in_list,
            out_specs=out_list,
            scratch_shapes=list(scratch),
        ),
        out_shape=list(outs),
        input_output_aliases=aliases or {},
        compiler_params=pltpu.CompilerParams(vmem_limit_bytes=limit * MEBI),
        cost_estimate=pl.CostEstimate(flops=int(flops), bytes_accessed=int(moved), transcendentals=0),
    )(*(() if mine is None else (mine,)), *ins)


def per_device(
    tokens,
    first_gain,
    first_bias,
    query_weight,
    query_bias,
    key_weight,
    key_bias,
    value_weight,
    value_bias,
    output_weight,
    output_bias,
    second_gain,
    second_bias,
    up_weight,
    up_bias,
    down_weight,
    down_bias,
    cotangent,
    doc_starts,
    valid_mask,
):
    blocks = lax.axis_size("seq")
    shares = lax.axis_size("mp")
    all_rows, block, width = tokens.shape
    a, hidden = query_weight.shape[1], up_weight.shape[1]
    z = Sizes(blocks, all_rows // shares, block, width, a, hidden)
    t = z.toks
    levels = levels_of(blocks)
    me = lax.axis_index("seq")
    places = [(me >> level.shift) & (level.radix - 1) for level in levels]
    far_bits = [1 << k for k in range(2, blocks.bit_length() - 1)]
    signs = [(me & bit) // bit for bit in far_bits]
    mine = jnp.stack([lax.axis_index("mp")] + places + signs + [me]).astype(jnp.int32)
    z.me = mine.shape[0] - 1
    first_bit = 1 + len(levels)

    def row(vector):
        return vector.reshape(1, vector.shape[0])

    g1, b1, g2, b2 = row(first_gain), row(first_bias), row(second_gain), row(second_bias)
    ob, db = row(output_bias), row(down_bias)
    wk2, wv2, wq2 = swap(key_weight), swap(value_weight), swap(query_weight)
    other_bias = swap(row(jnp.concatenate([query_bias, key_bias, value_bias, up_bias])))
    wo2, wup2, wd2 = swap(output_weight), swap(up_weight), swap(down_weight)

    def own_block(other=False):
        if other:
            return pl.BlockSpec((z.rows, block, width), lambda i, m: (1 - m[0], 0, 0))
        return pl.BlockSpec((z.rows, block, width), lambda i, m: (m[0], 0, 0))

    part = functools.partial
    sent_shape = shape((blocks, z.height, LANES), low)
    stage = pltpu.VMEM((z.height, LANES), wide)
    state_scratch = pltpu.VMEM((z.rows * z.pairs, HEAD_DIM, LANES), wide)
    thin = shape((t, LANES), wide)
    narrow, broad, half = shape((t, width), low), shape((t, width), wide), shape((t, a), low)

    first, kslope, kfeat, vlow, cols, segs, sent, means = call(
        part(project_kernel, z),
        (
            tokens,
            doc_starts,
            valid_mask,
            g1,
            b1,
            key_weight,
            wk2,
            row(key_bias),
            value_weight,
            wv2,
            row(value_bias),
            other_bias,
        ),
        (
            narrow,
            narrow,
            narrow,
            narrow,
            thin,
            shape((8 * z.rows, block), wide),
            sent_shape,
            shape((z.rows * z.pairs, LANES), wide),
        ),
        4e9,
        mine,
        specs={0: own_block()},
        scratch=[state_scratch, stage, pltpu.VMEM((2, t, a), wide)],
    )

    def scan(held, backward, after):
        return call(
            part(scan_kernel, z, backward),
            (held,),
            (sent_shape, shape((8, LANES), wide)),
            1e8,
            mine,
            scratch=[
                stage,
                pltpu.VMEM((2, blocks, LANES), wide),
                pltpu.VMEM((blocks, z.slice, LANES), wide),
            ],
            limit=10,
            after=after,
            held=(0,),
            held_out=(0, 1),
        )

    arriving = over_blocks(sent)
    qslope, qfeat, weights, within, sums, mark = call(
        part(score_kernel, z),
        (first, query_weight, wq2, row(query_bias), other_bias, kfeat, vlow, cols, segs),
        (narrow, narrow, shape((z.rows * z.pairs * 2, block, block), low), broad, thin),
        4e9,
        scratch=[pltpu.VMEM((2, t, a), wide)],
        mark=True,
    )
    entering, _ = scan(arriving, False, None)
    entering = over_blocks(entering)
    steps = hidden // width
    up_block = pl.BlockSpec((width, width), lambda i, m: (0, i))
    down_block = pl.BlockSpec((width, width), lambda i, m: (i, 0))
    tok_block = pl.BlockSpec((t, width), lambda i, m: (0, i))
    bias_block = pl.BlockSpec((1, width), lambda i, m: (0, i))
    other_up = other_bias[:, 3 * a :]
    wider = shape((t, hidden), low)
    (
        layer,
        act,
        act2,
        gup,
        gup2,
        second,
        gbr,
        att,
        att2,
        gnum,
        gnorm,
        sent_back,
        vec_mid,
    ) = call(
        part(middle_kernel, z),
        (
            entering,
            qfeat,
            within,
            sums,
            cols,
            tokens,
            cotangent,
            output_weight,
            wo2,
            ob,
            g2,
            b2,
            up_weight,
            wup2,
            row(up_bias),
            other_up,
            down_weight,
            wd2,
            db,
            means,
        ),
        (
            narrow,
            wider,
            wider,
            wider,
            wider,
            narrow,
            narrow,
            half,
            half,
            broad,
            thin,
            sent_shape,
            shape((16, width), wide),
        ),
        12e9,
        mine,
        specs={
            5: own_block(),
            6: own_block(),
            12: up_block,
            13: up_block,
            14: bias_block,
            15: bias_block,
            16: down_block,
            17: down_block,
        },
        out_specs={1: tok_block, 2: tok_block, 3: tok_block, 4: tok_block},
        held=(0,),
        grid=(steps,),
        scratch=[
            pltpu.VMEM((t, width), wide),
            pltpu.VMEM((t, width), wide),
            pltpu.VMEM((t, LANES), wide),
            pltpu.VMEM((t, width), wide),
            pltpu.VMEM((t, width), wide),
            pltpu.VMEM((t, 2 * a), wide),
            pltpu.VMEM((t, 2 * a), wide),
            pltpu.VMEM((8, LANES), wide),
            state_scratch,
            stage,
            pltpu.VMEM((z.rows * z.pairs * LANES, LANES), low),
            pltpu.VMEM((z.rows, block, width), wide),
            pltpu.VMEM((z.rows, block, width), wide),
        ],
    )
    act_in, gup_in, second_in = swap(act2), swap(gup2), swap(second)
    piece = hidden // 4
    act_block = pl.BlockSpec((t, piece), lambda i, m: (0, jnp.bitwise_xor(m[1], i)))
    two = shape((2 * piece, width), low)
    one = shape((piece, width), low)
    table = shape((16, width), wide)
    height = max(2 * width, 16 * blocks)
    radix = levels[0].radix

    def to(value, distance):
        return levels[0].exchange(value, distance, blocks)

    def far(value, bit):
        return lax.ppermute(value, "seq", [(i, i ^ bit) for i in range(blocks)])

    def spread(level, parts):
        return [parts[0]] + [level.exchange(p, d, blocks) for d, p in enumerate(parts) if d]

    def small(kernel, ins, dims, after, scalars=None, scratch=()):
        outs = [shape(dim, low) if isinstance(dim, tuple) else dim for dim in dims]
        *outs, marks["last"] = call(
            kernel,
            ins,
            outs,
            1e6,
            scalars,
            limit=8,
            after=after,
            held=range(len(ins)),
            held_out=range(len(outs)),
            mark=True,
            scratch=scratch,
        )
        return outs

    marks = {}

    def summed(number, parts, after):
        level = levels[number]
        rows = parts[0].shape[0] - 16
        outs = [shape((rows, width), low), shape((16, width), wide)]
        if number + 1 < len(levels):
            following = levels[number + 1].radix
            outs = [shape((rows // following + 16, width), low)] * following
        seen = [pltpu.VMEM((level.radix, 16, width), wide)]
        return small(part(sum_kernel, level), parts, outs, after, mine, seen)

    def joined(number, value, after):
        level = levels[number]
        dims = [(level.radix * value.shape[0], width)]
        parts = spread(level, [value] * level.radix)
        return small(part(join_kernel, level), parts, dims, after, mine)[0]

    v = {"leaving": over_blocks(sent_back)}

    def ffn_gradients(after):
        down_keep, down_give, up_keep, up_give, mark = call(
            part(ffn_grad_kernel, z),
            (act, act_in, cotangent, cotangent, second, second_in, gup, gup_in),
            (two, two, two, two),
            4e9,
            mine,
            specs={
                0: act_block,
                1: act_block,
                2: own_block(),
                3: own_block(True),
                6: act_block,
                7: act_block,
            },
            grid=(4,),
            after=after,
            mark=True,
        )
        v["down"], v["up"] = (down_keep, to(down_give, 1)), (up_keep, to(up_give, 2))
        return mark

    def backward_scan(after):
        leaving, v["lowest"] = scan(v["leaving"], True, after)
        v["leaving"] = over_blocks(leaving)
        return v["lowest"]

    def local_gradients(after):
        *v["local"], mark = call(
            part(local_kernel, z),
            (entering, weights, qfeat, kfeat, vlow, gnum, gnorm, qslope, cols, segs),
            (half, half, narrow, narrow, shape((8, 2 * a), wide)),
            6e9,
            scratch=[state_scratch],
            after=after,
            mark=True,
        )
        return mark

    def final_gradients(after):
        gq, gq2, gk_local, gv_local, vec_loc = v["local"]
        *v["final"], mark = call(
            part(final_kernel, z),
            (
                v["leaving"],
                kfeat,
                vlow,
                kslope,
                gk_local,
                gv_local,
                cols,
                gq,
                gq2,
                query_weight,
                wq2,
                key_weight,
                wk2,
                value_weight,
                wv2,
                tokens,
                g1,
                gbr,
                vec_mid,
                vec_loc,
            ),
            (half, half, half, half, narrow, table, table),
            4e9,
            mine,
            specs={15: own_block()},
            scratch=[state_scratch, pltpu.VMEM((t, width), wide)],
            held=(0,),
            after=after,
            mark=True,
        )
        return mark

    def first_pair(after):
        dims = [(piece, width)] * 4
        ins = v["down"] + v["up"]
        down_keep, down_give, up_keep, up_give = small(first_pair_kernel, ins, dims, after)
        v["down"], v["up"] = (down_keep, to(down_give, 2)), (up_keep, to(up_give, 1))
        return marks["last"]

    def attn_gradients(after):
        gq, gq2 = v["local"][:2]
        gk, gk2, gv, gv2, _, keep, give = v["final"]
        *v["rest"], mark = call(
            part(attn_grad_kernel, z, radix),
            (
                first,
                swap(first),
                gq,
                swap(gq2),
                gk,
                swap(gk2),
                gv,
                swap(gv2),
                att,
                swap(att2),
                gbr,
                swap(gbr),
                keep,
                swap(give),
            ),
            [shape((height // radix + 16, width), low)] * radix,
            2e9,
            mine,
            scratch=[pltpu.VMEM((height, width), low)],
            held=range(1, 14, 2),
            limit=30,
            after=after,
            mark=True,
        )
        v["rest"] = spread(levels[0], v["rest"])
        return mark

    def second_pair(after):
        dims = [(piece, width)] * 2
        ins = v["down"] + v["up"]
        keep, give = small(part(second_pair_kernel, first_bit), ins, dims, after, mine)
        v["ffn"] = (keep, far(give, far_bits[0]))
        return marks["last"]

    def first_half(after):
        dims = [(v["ffn"][0].shape[0] // 2, width)] * 2
        kernel = part(halve_kernel, first_bit + 1)
        keep, give = small(kernel, v["ffn"], dims, after, mine)
        v["ffn"] = (keep, far(give, far_bits[1]))
        return marks["last"]

    def last_half(after):
        for number in range(2, len(far_bits)):
            dims = [(v["ffn"][0].shape[0] // 2, width)] * 2
            kernel = part(halve_kernel, first_bit + number)
            keep, give = small(kernel, v["ffn"], dims, after, mine)
            v["ffn"] = (keep, far(give, far_bits[number]))
        (out,) = small(add_kernel, v["ffn"], [v["ffn"][0].shape], after)
        v["ffn"] = (out, far(out, far_bits[-1]))
        return marks["last"]

    def first_double(after):
        for number in reversed(range(1, len(far_bits))):
            dims = [(2 * v["ffn"][0].shape[0], width)]
            (out,) = small(part(double_kernel, first_bit + number), v["ffn"], dims, after, mine)
            v["ffn"] = (out, far(out, far_bits[number - 1]))
        return marks["last"]

    def last_double(after):
        dims = [(2 * v["ffn"][0].shape[0], width)]
        (out,) = small(part(double_kernel, first_bit), v["ffn"], dims, after, mine)
        v["ffn"] = (out, to(out, 1), to(out, 2))
        return marks["last"]

    def cut(after):
        out, out_x, out_y = v["ffn"]
        far_down, far_up = small(cut_kernel, (out_y, out_x), [(piece, width)] * 2, after)
        v["ffn"] = (out, out_x, out_y, to(far_down, 1), to(far_up, 2))
        return marks["last"]

    def first_sum(after):
        v["rest"] = summed(0, v["rest"], after)
        out = v["rest"][0]
        v["rest"] = spread(levels[1], v["rest"])
        return marks["last"]

    def last_sum(after):
        for number in range(1, len(levels)):
            v["rest"] = summed(number, v["rest"], after)
            if number + 1 < len(levels):
                v["rest"] = spread(levels[number + 1], v["rest"])
        return marks["last"]

    def join(after):
        out, v["vectors"] = v["rest"]
        for number in range(len(levels) - 1, 0, -1):
            out = joined(number, out, after)
        v["rest"] = spread(levels[0], [out] * radix)
        return marks["last"]

    def place(after):
        placed = pl.BlockSpec(
            (z.rows, block, width), lambda i, m: (jnp.where(i == 0, m[0], 1 - m[0]), 0, 0)
        )
        gtok = v["final"][4]
        *v["out"], mark = call(
            place_kernel,
            (layer, swap(layer), gtok, swap(gtok)),
            (shape(tokens.shape, low), shape(tokens.shape, wide)),
            1e6,
            mine,
            out_specs={0: placed, 1: placed},
            grid=(2,),
            held=(1, 3),
            limit=30,
            after=after,
            mark=True,
        )
        return mark

    def piece_blocks(step):
        return [
            pl.BlockSpec((piece, width), lambda i, m: (jnp.bitwise_xor(m[1], i + step), 0)),
            pl.BlockSpec((width, piece), lambda i, m: (0, jnp.bitwise_xor(m[1], i + step))),
        ]

    def unpack_three(after):
        outs = (shape((hidden, width), wide), shape((width, hidden), wide))
        *v["grads"], mark = call(
            unpack_three_kernel,
            v["ffn"][:3],
            outs,
            1e6,
            mine,
            out_specs=dict(enumerate(piece_blocks(0))),
            grid=(3,),
            held=(0, 1, 2),
            limit=24,
            after=after,
            mark=True,
        )
        return mark

    def unpack_far(after):
        outs = (shape((hidden, width), wide), shape((width, hidden), wide))
        *v["ffn"], mark = call(
            unpack_far_kernel,
            (*v["ffn"][3:], *v["grads"]),
            outs,
            1e6,
            mine,
            specs={2: PLACED, 3: PLACED},
            out_specs=dict(enumerate(piece_blocks(3))),
            held=(0, 1),
            limit=16,
            after=after,
            mark=True,
            aliases={3: 0, 4: 1},
        )
        return mark

    def unpack_attn(after):
        *v["rest"], mark = call(
            part(unpack_attn_kernel, z, levels[0]),
            (*v["rest"], v["vectors"], v["lowest"], swap(v["lowest"])),
            (
                shape((width, a), wide),
                shape((width, a), wide),
                shape((width, a), wide),
                shape((a, width), wide),
            )
            + tuple(shape((1, width), wide) for _ in range(6))
            + tuple(shape((1, a), wide) for _ in range(3))
            + (shape((1, hidden), wide), shape((1, 1), wide)),
            1e6,
            mine,
            scratch=[pltpu.VMEM((height, width), low)],
            held=range(radix),
            limit=24,
            after=after,
            mark=True,
        )
        return mark

    steps = dict(
        KF=ffn_gradients,
        S=backward_scan,
        KD=local_gradients,
        KE=final_gradients,
        KG=attn_gradients,
        p1=first_pair,
        p2=second_pair,
        h1=first_half,
        h2=last_half,
        d1=first_double,
        d2=last_double,
        c=cut,
        s1=first_sum,
        s2=last_sum,
        j=join,
        P=place,
        U3=unpack_three,
        UA=unpack_far,
        UB=unpack_attn,
    )
    after = None
    for name in ORDER:
        after = steps[name](after)
    layer_out, grad_tokens = v["out"]
    grad_down, grad_up = v["ffn"]
    grad_q, grad_k, grad_v, grad_o, g1, b1, ob, g2, b2, db, qb, kb, vb, upb, least = v["rest"]

    def flat(table):
        return table.reshape(table.shape[1])

    return (
        layer_out,
        grad_tokens,
        least.reshape(()),
        flat(g1),
        flat(b1),
        grad_q,
        flat(qb),
        grad_k,
        flat(kb),
        grad_v,
        flat(vb),
        grad_o,
        flat(ob),
        flat(g2),
        flat(b2),
        grad_up,
        flat(upb),
        grad_down,
        flat(db),
    )


def solution(mesh):
    return jax.shard_map(
        per_device,
        mesh=mesh,
        in_specs=(
            P(None, "seq", None),
            P(),
            P(),
            P(None, "mp"),
            P("mp"),
            P(None, "mp"),
            P("mp"),
            P(None, "mp"),
            P("mp"),
            P("mp", None),
            P(),
            P(),
            P(),
            P(None, "mp"),
            P("mp"),
            P("mp", None),
            P(),
            P(None, "seq", None),
            P(None, "seq"),
            P(None, "seq"),
        ),
        out_specs=(
            P(None, "seq", None),
            P(None, "seq", None),
            P(),
            P(),
            P(),
            P(None, "mp"),
            P("mp"),
            P(None, "mp"),
            P("mp"),
            P(None, "mp"),
            P("mp"),
            P("mp", None),
            P(),
            P(),
            P(),
            P(None, "mp"),
            P("mp"),
            P("mp", None),
            P(),
        ),
        check_vma=False,
    )
```

```python
import functools

import jax
import jax.numpy as jnp
from jax import lax
from jax.experimental import pallas as pl
from jax.experimental.pallas import tpu as pltpu
from jax.sharding import PartitionSpec as P

HEAD_DIM = 64
LANES = 128
EPSILON = 1e-05
LARGE_VALUE = 1e30
TINY = 1e-30
ORDER = (
    "KF",
    "S",
    "KD",
    "KE",
    "p1",
    "KG",
    "p2",
    "P",
    "h1",
    "h2",
    "s1",
    "s2",
    "d1",
    "d2",
    "j",
    "c",
    "U3",
    "UB",
    "UA",
)
MEBI = 1024 * 1024

low = jnp.bfloat16
wide = jnp.float32


def dot(left, right):
    return jnp.dot(left, right, preferred_element_type=wide)


def dot_nt(left, right):
    return lax.dot_general(left, right, (((1,), (1,)), ((), ())), preferred_element_type=wide)


def dot_tn(left, right):
    return lax.dot_general(left, right, (((0,), (0,)), ((), ())), preferred_element_type=wide)


def iota(shape, dim):
    return lax.broadcasted_iota(jnp.int32, shape, dim)


def first_head(shape):
    return iota(shape, 1) < HEAD_DIM


def only_head(pair, head):
    keep = first_head(pair.shape) if head == 0 else jnp.logical_not(first_head(pair.shape))
    return jnp.where(keep, pair, jnp.zeros_like(pair))


def head_sums(pair):
    keep = first_head(pair.shape)
    one = jnp.sum(jnp.where(keep, pair, 0.0), axis=1, keepdims=True)
    two = jnp.sum(jnp.where(keep, 0.0, pair), axis=1, keepdims=True)
    return jnp.where(keep, one, two)


def spread_heads(columns):
    return jnp.where(first_head((columns.shape[0], LANES)), columns[:, 0:1], columns[:, 1:2])


def two_terms(value):
    high = value.astype(low)
    return high, (value - high.astype(wide)).astype(low)


def two_blocks(state):
    return jnp.concatenate([only_head(state, 0), only_head(state, 1)], axis=0)


def compact(product):
    return jnp.where(
        first_head((HEAD_DIM, LANES)), product[:HEAD_DIM], product[HEAD_DIM:]
    )


def normalize(values):
    average = jnp.mean(values, axis=1, keepdims=True)
    centred = values - average
    spread = jnp.mean(centred * centred, axis=1, keepdims=True)
    inverse = lax.rsqrt(spread + EPSILON)
    return (centred * inverse, inverse)


def norm_backward(grad_out, normed, inverse, gain_row):
    grad_normed = grad_out * gain_row
    first_term = jnp.mean(grad_normed, axis=1, keepdims=True)
    second_term = jnp.mean(grad_normed * normed, axis=1, keepdims=True)
    return inverse * (grad_normed - first_term - normed * second_term)


def column_sums(values):
    return jnp.sum(values, axis=0, keepdims=True)


TILE = 32


def tiles(count):
    return [slice(start, start + TILE) for start in range(0, count, TILE)]


def fold_rows(values):
    total = values[0:8]
    for start in range(8, values.shape[0], 8):
        total = total + values[start : start + 8]
    return total


class Sizes:
    def __init__(self, blocks, rows, block, width, attn, hidden):
        self.blocks, self.rows, self.block = blocks, rows, block
        self.width, self.attn, self.hidden = width, attn, hidden
        self.toks = rows * block
        self.pairs = 2 * attn // LANES
        self.group = blocks // (rows * self.pairs)
        self.slice = HEAD_DIM // self.group
        self.height = -(-(self.slice + 7) // 16) * 16

    def at(self, row, tile):
        return slice(row * self.block + tile.start, row * self.block + tile.stop)

    def span(self, row):
        return slice(row * self.block, (row + 1) * self.block)


def lanes_of(pair):
    return slice(pair * LANES, (pair + 1) * LANES)


def rows_in_lanes(rows):
    same = jnp.where(iota((LANES, LANES), 0) == iota((LANES, LANES), 1), 1.0, 0.0).astype(low)
    return dot_nt(same, rows)


def write_piece(z, sent_ref, index, stage_ref, body, total, centre, restart, extra):
    k = z.slice
    stage_ref[0:k, :] = body
    line = k
    for value in (total, centre):
        for term in two_terms(value):
            stage_ref[line : line + 1, :] = term.astype(wide)
            line += 1
    stage_ref[line : line + 1, :] = jnp.broadcast_to(restart, (1, LANES))
    for term in two_terms(extra):
        line += 1
        stage_ref[line : line + 1, :] = term.astype(wide)
    if z.height > k + 7:
        stage_ref[k + 7 : z.height, :] = jnp.zeros((z.height - k - 7, LANES), wide)
    sent_ref[index] = stage_ref[...].astype(low)


def pair_sum(piece, line):
    return piece[line : line + 1, :] + piece[line + 1 : line + 2, :]


def centred(state, spread):
    centre = column_sums(state) / jnp.maximum(column_sums(spread), TINY)
    high, rest = two_terms(centre)
    centre = high.astype(wide) + rest.astype(wide)
    return state - spread * centre, centre


def write_state(z, sent_ref, held_ref, stage_ref, row, pair, state, total, centre, restart, extra):
    number = row * z.pairs + pair
    if state is not None:
        held_ref[number] = state
    for step in range(z.group):
        index = number * z.group + step
        body = held_ref[number, step * z.slice : (step + 1) * z.slice, :]
        write_piece(z, sent_ref, index, stage_ref, body, total, centre, restart, extra)


def read_states(z, got_ref, held_ref, backward):
    lane = iota((1, LANES), 1)
    place = jnp.where(lane < HEAD_DIM, lane, lane - HEAD_DIM) // z.slice
    totals, centres = [], []
    for number in range(z.rows * z.pairs):
        total = jnp.zeros((1, LANES), wide)
        centre = jnp.zeros((HEAD_DIM, LANES), wide)
        for step in range(z.group):
            piece = got_ref[number * z.group + step].astype(wide)
            held_ref[number, step * z.slice : (step + 1) * z.slice, :] = piece[0 : z.slice, :]
            total = jnp.where(place == step, pair_sum(piece, z.slice), total)
            if not backward:
                here = iota((HEAD_DIM, LANES), 0) // z.slice == step
                centre = jnp.where(here, pair_sum(piece, z.slice + 2), centre)
        totals.append(total)
        centres.append(centre)
    if not backward:
        high, rest = two_terms(jnp.concatenate(totals, axis=0))
        columns = rows_in_lanes(jnp.concatenate([high, rest], axis=0))
        count = len(totals)
        columns = columns[:, 0:count] + columns[:, count : 2 * count]
        for number, centre in enumerate(centres):
            column = columns[:, number : number + 1]
            spread = jnp.where(
                first_head((HEAD_DIM, LANES)), column[0:HEAD_DIM], column[HEAD_DIM:LANES]
            )
            held_ref[number] = held_ref[number] + spread * centre
    return totals


def mask_of(z, cols_ref, segs_ref, row):
    here = cols_ref[z.span(row), 0:1]
    there = segs_ref[row * 8 : row * 8 + 1, :]
    shape = (z.block, z.block)
    return jnp.logical_and(here == there, iota(shape, 0) >= iota(shape, 1))


def project_kernel(
    z,
    mine_ref,
    tokens_ref,
    starts_ref,
    valid_ref,
    gain_ref,
    bias_ref,
    wk_ref,
    wk2_ref,
    bk_ref,
    wv_ref,
    wv2_ref,
    bv_ref,
    other_bias_ref,
    first_ref,
    kslope_ref,
    kfeat_ref,
    vlow_ref,
    cols_ref,
    segs_ref,
    sent_ref,
    means_ref,
    held_ref,
    stage_ref,
    pre_ref,
):
    mine = mine_ref[0]
    for row in range(z.rows):
        for tile in tiles(z.block):
            x = tokens_ref[row, tile, :].astype(wide)
            normed, _ = normalize(x)
            first_ref[z.at(row, tile), :] = (normed * gain_ref[...] + bias_ref[...]).astype(low)
    a = z.attn
    first = first_ref[...]
    for part, (wk, wv, bk, bv) in enumerate(
        (
            (wk_ref, wv_ref, bk_ref[...], bv_ref[...]),
            (wk2_ref, wv2_ref, other_bias_ref[:, a : 2 * a], other_bias_ref[:, 2 * a : 3 * a]),
        )
    ):
        lanes = slice(part * a, (part + 1) * a)
        pre_ref[part] = dot(first, wk[...])
        vlow_ref[:, lanes] = (dot(first, wv[...]) + bv).astype(low)
        for tile in tiles(z.toks):
            key_pre = pre_ref[part, tile, :] + bk
            kslope_ref[tile, lanes] = jax.nn.sigmoid(key_pre).astype(low)
            kfeat_ref[tile, lanes] = softplus(key_pre).astype(low)
    square = (z.block, z.block)
    upto = iota(square, 0) <= iota(square, 1)
    upper = jnp.where(upto, 1.0, 0.0).astype(low)
    since = jnp.where(iota(square, 0) >= iota(square, 1), 1.0, 0.0).astype(low)
    same = jnp.where(iota(square, 0) == iota(square, 1), 1.0, 0.0).astype(low)
    for row in range(z.rows):
        other = z.rows + row

        def pick(ref):
            value = jnp.where(mine == 0, ref[row : row + 1, :], ref[other : other + 1, :])
            return jnp.broadcast_to(value.astype(wide), (8, z.block)).astype(low)

        starts, valid = pick(starts_ref), pick(valid_ref)
        seg_row = dot(starts, upper)
        seg_col = dot_nt(since, starts)[:, 0:1]
        valid_col = dot_nt(same, valid)[:, 0:1]
        seg_end = seg_row[0:1, z.block - 1 : z.block]
        segs_ref[row * 8 : (row + 1) * 8, :] = jnp.where(valid.astype(wide) > 0.0, seg_row, -1.0)
        carried = jnp.where(seg_col == 0.0, 1.0, 0.0)
        last = jnp.where(jnp.logical_and(seg_col == seg_end, valid_col > 0.0), 1.0, 0.0)
        restart = jnp.where(seg_end > 0.0, 1.0, 0.0)
        lane = iota((z.block, LANES), 1)
        cols = jnp.where(lane == 0, seg_col, 0.0)
        cols = jnp.where(lane == 1, carried, cols)
        cols = jnp.where(lane == 2, last, cols)
        cols = jnp.where(lane == 3, valid_col, cols)
        cols = jnp.where(lane == 4, restart, cols)
        cols_ref[z.span(row), :] = cols
        for pair in range(z.pairs):
            keys = kfeat_ref[z.span(row), lanes_of(pair)].astype(wide) * last
            keys_low, values = keys.astype(low), vlow_ref[z.span(row), lanes_of(pair)]
            ones = jnp.ones((z.block, LANES), low)
            product = dot_tn(keys_low, jnp.concatenate([values, ones], axis=1))
            spread = compact(product[:, LANES : 2 * LANES])
            state, centre = centred(compact(product[:, 0:LANES]), spread)
            line = row * z.pairs + pair
            means_ref[line : line + 1, :] = column_sums(values.astype(wide)) * (1.0 / z.block)
            write_state(
                z,
                sent_ref,
                held_ref,
                stage_ref,
                row,
                pair,
                state,
                column_sums(keys),
                centre,
                restart,
                jnp.zeros((1, LANES), wide),
            )


def softplus(values):
    return jnp.maximum(values, 0.0) + jnp.log1p(jnp.exp(-jnp.abs(values)))


def scan_kernel(z, backward, mine_ref, held_ref, scanned_ref, lowest_ref, stage_ref, rows_ref, runs_ref):
    k = z.slice
    shift = (mine_ref[z.me] & (z.group - 1)) * k
    picks = []
    for head in range(2):
        hit = iota((k, LANES), 1) == iota((k, LANES), 0) + shift + head * HEAD_DIM
        picks.append(jnp.where(hit, 1.0, 0.0).astype(low))
    half = iota((k, LANES), 1) < HEAD_DIM
    lane = iota((k, LANES), 1)
    columns = [jnp.zeros((k, LANES), wide) for _ in range(2)]
    if not backward:
        for block in range(z.blocks):
            rows_ref[0, block : block + 1, :] = held_ref[block].astype(wide)[k : k + 1]
            rows_ref[1, block : block + 1, :] = held_ref[block].astype(wide)[k + 1 : k + 2]
        terms = [rows_ref[i].astype(low) for i in range(2)]
        columns = [dot_nt(pick, terms[0]) + dot_nt(pick, terms[1]) for pick in picks]
    run = jnp.zeros((k, LANES), wide)
    run_total = jnp.zeros((1, LANES), wide)
    run_spread = jnp.zeros((k, LANES), wide)
    least = jnp.full((1, LANES), LARGE_VALUE, wide)
    none = jnp.zeros((1, LANES), wide)
    for step in range(z.blocks):
        block = z.blocks - 1 - step if backward else step
        here = held_ref[block].astype(wide)
        state, total, centre = here[0:k], pair_sum(here, k), pair_sum(here, k + 2)
        keep = 1.0 - here[k + 4 : k + 5]
        least = jnp.minimum(least, pair_sum(here, k + 5))
        if backward:
            lost = (run - run.astype(low).astype(wide)) * centre
            for head in range(2):
                sums = jnp.sum(only_head(lost, head), axis=1, keepdims=True)
                columns[head] = jnp.where(lane == block, sums, columns[head])
            runs_ref[block] = run
            rows_ref[0, block : block + 1, :] = run_total
        else:
            body, middle = centred(run, run_spread)
            write_piece(z, scanned_ref, block, stage_ref, body, run_total, middle, none, none)
            spread = jnp.where(
                half, columns[0][:, block : block + 1], columns[1][:, block : block + 1]
            )
            state = state + spread * centre
            run_spread = spread + keep * run_spread
        run = state + keep * run
        run_total = total + keep * run_total
    if backward:
        moved = dot_tn(columns[0].astype(low), picks[0]) + dot_tn(columns[1].astype(low), picks[1])
        for block in range(z.blocks):
            total = rows_ref[0, block : block + 1, :] + moved[block : block + 1, :]
            write_piece(z, scanned_ref, block, stage_ref, runs_ref[block], total, none, none, none)
    lowest_ref[...] = jnp.broadcast_to(least, (8, LANES))


def score_kernel(
    z,
    first_ref,
    wq_ref,
    wq2_ref,
    bq_ref,
    other_bias_ref,
    kfeat_ref,
    vlow_ref,
    cols_ref,
    segs_ref,
    qslope_ref,
    qfeat_ref,
    weights_ref,
    within_ref,
    sums_ref,
    pre_ref,
):
    a = z.attn
    for part, (wq, bq) in enumerate(((wq_ref, bq_ref[...]), (wq2_ref, other_bias_ref[:, 0:a]))):
        lanes = slice(part * a, (part + 1) * a)
        pre_ref[part] = dot(first_ref[...], wq[...])
        for tile in tiles(z.toks):
            query_pre = pre_ref[part, tile, :] + bq
            qslope_ref[tile, lanes] = jax.nn.sigmoid(query_pre).astype(low)
            qfeat_ref[tile, lanes] = softplus(query_pre).astype(low)
    for row in range(z.rows):
        mask = mask_of(z, cols_ref, segs_ref, row)
        table = jnp.zeros((z.block, LANES), wide)
        for pair in range(z.pairs):
            here = (z.span(row), lanes_of(pair))
            queries, keys, values = qfeat_ref[here], kfeat_ref[here], vlow_ref[here]
            within = jnp.zeros((z.block, LANES), wide)
            sums = []
            for head in range(2):
                scores = jnp.where(mask, dot_nt(only_head(queries, head), keys), 0.0)
                weights = scores.astype(low)
                weights_ref[(row * z.pairs + pair) * 2 + head] = weights
                within = within + dot(weights, only_head(values, head))
                sums.append(jnp.sum(scores, axis=1, keepdims=True))
            within_ref[here] = within
            lane = iota((z.block, LANES), 1)
            table = jnp.where(lane == 2 * pair, sums[0], table)
            table = jnp.where(lane == 2 * pair + 1, sums[1], table)
        sums_ref[z.span(row), :] = table


def middle_kernel(
    z,
    mine_ref,
    got_ref,
    qfeat_ref,
    within_ref,
    sums_ref,
    cols_ref,
    tokens_ref,
    cot_ref,
    wo_ref,
    wo2_ref,
    ob_ref,
    gain_ref,
    bias_ref,
    wup_ref,
    wup2_ref,
    bup_ref,
    bup2_ref,
    wd_ref,
    wd2_ref,
    db_ref,
    means_ref,
    layer_ref,
    act_ref,
    act2_ref,
    gup_ref,
    gup2_ref,
    second_ref,
    gbr_ref,
    att_ref,
    att2_ref,
    gnum_ref,
    gnorm_ref,
    sent_ref,
    vec_ref,
    s_mid,
    s_n2,
    s_r2,
    s_ffn,
    s_gsec,
    s_att,
    s_norm,
    s_min,
    held_ref,
    stage_ref,
    s_lost,
    s_up,
    s_gact,
):
    step = pl.program_id(0)
    a = z.attn

    @pl.when(step == 0)
    def _():
        totals = read_states(z, got_ref, held_ref, False)
        least = jnp.full((1, 1), LARGE_VALUE, wide)
        for row in range(z.rows):
            carried = cols_ref[z.span(row), 1:2]
            valid = cols_ref[z.span(row), 3:4]
            for pair in range(z.pairs):
                here = (z.span(row), lanes_of(pair))
                state, total = held_ref[row * z.pairs + pair], totals[row * z.pairs + pair]
                high, rest = two_terms(two_blocks(state))
                queries = qfeat_ref[here]
                across = dot(
                    jnp.concatenate([queries, queries], axis=1),
                    jnp.concatenate([high, rest], axis=0),
                )
                norm = spread_heads(sums_ref[z.span(row), 2 * pair : 2 * pair + 2])
                norm = norm + carried * head_sums(queries.astype(wide) * total)
                s_norm[here] = norm
                seen = jnp.where(valid > 0.0, norm, LARGE_VALUE)
                seen = jnp.min(jnp.min(seen, axis=0, keepdims=True), axis=1, keepdims=True)
                least = jnp.minimum(least, seen)
                attended = (within_ref[here] + across * carried) / jnp.maximum(norm, 1.0)
                s_att[here] = attended
        s_min[...] = jnp.broadcast_to(least, (8, LANES))
        att_ref[...] = s_att[:, 0:a].astype(low)
        att2_ref[...] = s_att[:, a : 2 * a].astype(low)
        s_mid[...] = dot(att_ref[...], wo_ref[...]) + dot(att2_ref[...], wo2_ref[...])
        for row in range(z.rows):
            for tile in tiles(z.block):
                here = z.at(row, tile)
                middle = tokens_ref[row, tile, :].astype(wide) + s_mid[here, :] + ob_ref[...]
                s_mid[here, :] = middle
                normed, inverse = normalize(middle)
                s_n2[here, :] = normed
                s_r2[here, :] = jnp.broadcast_to(inverse, (TILE, LANES))
                second_ref[here, :] = (normed * gain_ref[...] + bias_ref[...]).astype(low)
        s_ffn[...] = jnp.zeros_like(s_ffn)
        s_gsec[...] = jnp.zeros_like(s_gsec)
        vec_ref[...] = jnp.zeros_like(vec_ref)

    for part, (wup, bup, wd, act_out, gup_out) in enumerate(
        (
            (wup_ref, bup_ref, wd_ref, act_ref, gup_ref),
            (wup2_ref, bup2_ref, wd2_ref, act2_ref, gup2_ref),
        )
    ):
        sums = jnp.zeros((8, bup.shape[1]), wide)
        for row in range(z.rows):
            span = z.span(row)
            s_up[row] = dot(second_ref[span, :], wup[...])
            s_gact[row] = dot_nt(cot_ref[row], wd[...])
            for tile in tiles(z.block):
                up = s_up[row, tile, :] + bup[...]
                share = 0.5 * (1.0 + lax.erf(up * 0.7071067811865476))
                density = 0.3989422804014327 * jnp.exp(-0.5 * up * up)
                act_out[z.at(row, tile), :] = (up * share).astype(low)
                gup = (s_gact[row, tile, :] * (share + up * density)).astype(low)
                gup_out[z.at(row, tile), :] = gup
                sums = sums + fold_rows(gup.astype(wide))
            s_ffn[span, :] += dot(act_out[span, :], wd[...])
            s_gsec[span, :] += dot_nt(gup_out[span, :], wup[...])
        vec_ref[pl.ds(4 + part * pl.num_programs(0) + step, 1), :] = column_sums(sums)

    @pl.when(step == pl.num_programs(0) - 1)
    def _():
        sums = [jnp.zeros((8, z.width), wide) for _ in range(4)]
        for row in range(z.rows):
            for tile in tiles(z.block):
                here = z.at(row, tile)
                layer_ref[here, :] = (s_mid[here, :] + s_ffn[here, :] + db_ref[...]).astype(low)
                grad_out = cot_ref[row, tile, :].astype(wide)
                grad_second, normed = s_gsec[here, :], s_n2[here, :]
                inverse = s_r2[here, 0:1]
                grad_middle = grad_out + norm_backward(
                    grad_second, normed, inverse, gain_ref[...]
                )
                grad_branch = grad_middle.astype(low)
                gbr_ref[here, :] = grad_branch
                values = (grad_branch.astype(wide), grad_second * normed, grad_second, grad_out)
                sums = [total + fold_rows(value) for total, value in zip(sums, values)]
        for line, total in enumerate(sums):
            vec_ref[line : line + 1, :] = column_sums(total)
        grad_branch = gbr_ref[...]
        gnum_ref[:, 0:a] = dot_nt(grad_branch, wo_ref[...])
        gnum_ref[:, a : 2 * a] = dot_nt(grad_branch, wo2_ref[...])
        totals, centres = [], []
        for row in range(z.rows):
            carried = cols_ref[z.span(row), 1:2]
            table = jnp.zeros((z.block, LANES), wide)
            for pair in range(z.pairs):
                here = (z.span(row), lanes_of(pair))
                grad_att, norm = gnum_ref[here], s_norm[here]
                inverse = 1.0 / jnp.maximum(norm, 1.0)
                grad_num = grad_att * inverse
                gnum_ref[here] = grad_num
                along = head_sums(grad_att * s_att[here])
                grad_norm = jnp.where(norm > 1.0, -along * inverse, 0.0)
                lane = iota((z.block, LANES), 1)
                table = jnp.where(lane == 2 * pair, grad_norm[:, 0:1], table)
                table = jnp.where(
                    lane == 2 * pair + 1, grad_norm[:, HEAD_DIM : HEAD_DIM + 1], table
                )
                queries = qfeat_ref[here]
                high, rest = two_terms(grad_num * carried)
                product = dot_tn(queries, jnp.concatenate([high, rest], axis=1))
                product = product[:, 0:LANES] + product[:, LANES : 2 * LANES]
                total = column_sums(queries.astype(wide) * (grad_norm * carried))
                state = compact(product)
                number = row * z.pairs + pair
                held_ref[number] = state
                centre = means_ref[number : number + 1, :].astype(low).astype(wide)
                lost = (state - state.astype(low).astype(wide)) * centre
                s_lost[number * LANES : (number + 1) * LANES, :] = two_blocks(lost).astype(low)
                totals.append(total)
                centres.append(centre)
            gnorm_ref[z.span(row), :] = table
        lost = dot_nt(jnp.ones((8, LANES), low), s_lost[...])
        for row in range(z.rows):
            restart = cols_ref[row * z.block : row * z.block + 1, 4:5]
            for pair in range(z.pairs):
                number = row * z.pairs + pair
                total = totals[number] + lost[0:1, lanes_of(number)]
                write_state(
                    z,
                    sent_ref,
                    held_ref,
                    stage_ref,
                    row,
                    pair,
                    None,
                    total,
                    centres[number],
                    restart,
                    s_min[0:1, :],
                )


def local_kernel(
    z,
    got_ref,
    weights_ref,
    qfeat_ref,
    kfeat_ref,
    vlow_ref,
    gnum_ref,
    gnorm_ref,
    qslope_ref,
    cols_ref,
    segs_ref,
    gq_ref,
    gq2_ref,
    gk_ref,
    gv_ref,
    vec_ref,
    held_ref,
):
    a = z.attn
    vec_ref[...] = jnp.zeros_like(vec_ref)
    half = z.pairs // 2
    totals = read_states(z, got_ref, held_ref, False)
    for row in range(z.rows):
        mask = mask_of(z, cols_ref, segs_ref, row)
        carried = cols_ref[z.span(row), 1:2]
        for pair in range(z.pairs):
            here = (z.span(row), lanes_of(pair))
            queries, keys, values = qfeat_ref[here], kfeat_ref[here], vlow_ref[here]
            state, total = held_ref[row * z.pairs + pair], totals[row * z.pairs + pair]
            high, rest = two_terms(two_blocks(state))
            grad_norm = spread_heads(gnorm_ref[z.span(row), 2 * pair : 2 * pair + 2])
            num_high, num_rest = two_terms(gnum_ref[here])
            grad_q = carried * (
                dot_nt(
                    jnp.concatenate([num_high, num_rest, num_high], axis=1),
                    jnp.concatenate([high, high, rest], axis=1),
                )
                + grad_norm * total
            )
            grad_k = jnp.zeros((z.block, LANES), wide)
            grad_v = jnp.zeros((z.block, LANES), wide)
            for head in range(2):
                grad_low = only_head(num_high, head)
                norm_col = grad_norm[:, head * HEAD_DIM : head * HEAD_DIM + 1]
                grad_scores = jnp.where(mask, dot_nt(grad_low, values) + norm_col, 0.0).astype(low)
                grad_q = grad_q + dot(grad_scores, only_head(keys, head))
                grad_k = grad_k + dot_tn(grad_scores, only_head(queries, head))
                weights = weights_ref[(row * z.pairs + pair) * 2 + head]
                grad_v = grad_v + dot_tn(weights, grad_low)
            gk_ref[here] = grad_k.astype(low)
            gv_ref[here] = grad_v.astype(low)
            grad_low = (grad_q * qslope_ref[here].astype(wide)).astype(low)
            out = gq_ref if pair < half else gq2_ref
            out[z.span(row), lanes_of(pair % half)] = grad_low
            vec_ref[0:1, lanes_of(pair)] += column_sums(grad_low.astype(wide))


def ffn_grad_kernel(
    z,
    mine_ref,
    act_ref,
    act2_ref,
    cot_ref,
    cot2_ref,
    second_ref,
    second2_ref,
    gup_ref,
    gup2_ref,
    down_keep_ref,
    down_give_ref,
    up_keep_ref,
    up_give_ref,
):
    c1 = cot_ref[...].reshape(z.toks, z.width)
    c2 = cot2_ref[...].reshape(z.toks, z.width)
    down = (dot_tn(act_ref[...], c1) + dot_tn(act2_ref[...], c2)).astype(low)
    up = dot_tn(second_ref[...], gup_ref[...]) + dot_tn(second2_ref[...], gup2_ref[...])
    up = up.astype(low)
    rows, fold = down.shape[0], z.width // up.shape[1]
    tall = z.width // fold
    for distance in range(4):
        down_out = down_give_ref if distance % 2 else down_keep_ref
        up_out = up_give_ref if distance // 2 else up_keep_ref

        @pl.when(pl.program_id(0) == distance)
        def _():
            start = (distance // 2) * rows
            down_out[start : start + rows, :] = down
            start = (distance % 2) * tall
            for i in range(fold):
                lanes = slice(i * up.shape[1], (i + 1) * up.shape[1])
                up_out[start : start + tall, lanes] = up[i * tall : (i + 1) * tall]


def added(kept, got):
    return (kept.astype(wide) + got.astype(wide)).astype(low)


def first_pair_kernel(down_ref, down_got, up_ref, up_got, dk_ref, dg_ref, uk_ref, ug_ref):
    half = dk_ref.shape[0]
    for kept, got, keep, give in (
        (down_ref, down_got, dk_ref, dg_ref),
        (up_ref, up_got, uk_ref, ug_ref),
    ):
        keep[...] = added(kept[0:half, :], got[0:half, :])
        give[...] = added(kept[half : 2 * half, :], got[half : 2 * half, :])


def second_pair_kernel(bit, mine_ref, down_ref, down_got, up_ref, up_got, keep_ref, give_ref):
    upper = mine_ref[bit] > 0
    down, up = added(down_ref[...], down_got[...]), added(up_ref[...], up_got[...])
    keep_ref[...] = jnp.where(upper, up, down)
    give_ref[...] = jnp.where(upper, down, up)


def halve_kernel(bit, mine_ref, kept_ref, got_ref, keep_ref, give_ref):
    rows = keep_ref.shape[0]
    here = pl.ds(pl.multiple_of(mine_ref[bit] * rows, rows), rows)
    there = pl.ds(pl.multiple_of((1 - mine_ref[bit]) * rows, rows), rows)
    keep_ref[...] = added(kept_ref[here, :], got_ref[here, :])
    give_ref[...] = added(kept_ref[there, :], got_ref[there, :])


def add_kernel(kept_ref, got_ref, out_ref):
    out_ref[...] = added(kept_ref[...], got_ref[...])


def double_kernel(bit, mine_ref, own_ref, got_ref, out_ref):
    rows = own_ref.shape[0]
    out_ref[pl.ds(pl.multiple_of(mine_ref[bit] * rows, rows), rows), :] = own_ref[...]
    out_ref[pl.ds(pl.multiple_of((1 - mine_ref[bit]) * rows, rows), rows), :] = got_ref[...]


def cut_kernel(one_ref, two_ref, first_ref, second_ref):
    rows = first_ref.shape[0]
    first_ref[...] = one_ref[0:rows, :]
    second_ref[...] = two_ref[rows : 2 * rows, :]


def sum_kernel(level, mine_ref, *refs):
    pieces, outs, seen = refs[: level.radix], refs[level.radix : -1], refs[-1]
    rows = pieces[0].shape[0] - 16
    place = mine_ref[1 + level.index]
    for distance, piece in enumerate(pieces):
        seen[jnp.bitwise_xor(place, distance)] = piece[rows : rows + 16, :].astype(wide)
    vectors = seen[0]
    for i in range(1, level.radix):
        vectors = vectors + seen[i]
    last = outs[-1].dtype == wide
    parts = outs[:-1] if last else outs
    part_rows = rows // len(parts)
    for distance, out_ref in enumerate(parts):
        start = 0
        if not last:
            start = jnp.bitwise_xor(mine_ref[1 + level.index + 1], distance) * part_rows
            start = pl.multiple_of(start, part_rows)
        total = pieces[0][pl.ds(start, part_rows), :].astype(wide)
        for piece in pieces[1:]:
            total = total + piece[pl.ds(start, part_rows), :].astype(wide)
        out_ref[0:part_rows, :] = total.astype(low)
        if not last:
            out_ref[part_rows : part_rows + 16, :] = vectors.astype(low)
    if last:
        outs[-1][...] = vectors


def join_kernel(level, mine_ref, *refs):
    pieces, out_ref = refs[: level.radix], refs[level.radix]
    rows = pieces[0].shape[0]
    for distance, piece in enumerate(pieces):
        place = jnp.bitwise_xor(mine_ref[1 + level.index], distance)
        out_ref[pl.ds(pl.multiple_of(place * rows, rows), rows), :] = piece[...]


def unpack_ffn_kernel(down_ref, up_ref, *refs):
    down_out, up_out = refs[-2:]
    rows = down_out.shape[0]
    fold = up_ref.shape[1] // rows
    down_out[...] = down_ref[...].astype(wide)
    tall = up_out.shape[0] // fold
    for i in range(fold):
        lanes = slice(i * rows, (i + 1) * rows)
        up_out[i * tall : (i + 1) * tall, :] = up_ref[:, lanes].astype(wide)


def unpack_three_kernel(mine_ref, own_ref, x_ref, y_ref, down_out, up_out):
    rows = down_out.shape[0]
    for step, ref in enumerate((own_ref, x_ref, y_ref)):

        @pl.when(pl.program_id(0) == step)
        def _():
            down, up = ref.at[0:rows, :], ref.at[rows : 2 * rows, :]
            unpack_ffn_kernel(down, up, down_out, up_out)


def unpack_far_kernel(mine_ref, down_ref, up_ref, down_old, up_old, down_out, up_out):
    unpack_ffn_kernel(down_ref, up_ref, down_out, up_out)


def final_kernel(
    z,
    mine_ref,
    got_ref,
    kfeat_ref,
    vlow_ref,
    kslope_ref,
    gk_ref,
    gv_ref,
    cols_ref,
    gq_ref,
    gq2_ref,
    wq_ref,
    wq2_ref,
    wk_ref,
    wk2_ref,
    wv_ref,
    wv2_ref,
    tokens_ref,
    gain_ref,
    gbr_ref,
    vec_mid_ref,
    vec_loc_ref,
    gk1_ref,
    gk2_ref,
    gv1_ref,
    gv2_ref,
    gtok_ref,
    keep_ref,
    give_ref,
    held_ref,
    s_first,
):
    a = z.attn
    half = z.pairs // 2
    totals = read_states(z, got_ref, held_ref, True)
    keep_ref[...] = jnp.zeros_like(keep_ref)
    give_ref[...] = jnp.zeros_like(give_ref)
    for row in range(z.rows):
        last = cols_ref[z.span(row), 2:3]
        for pair in range(z.pairs):
            here = (z.span(row), lanes_of(pair))
            keys, values = kfeat_ref[here], vlow_ref[here]
            state, total = held_ref[row * z.pairs + pair], totals[row * z.pairs + pair]
            high = two_blocks(state).astype(low)
            grad_k = gk_ref[here].astype(wide) + last * (
                dot_nt(values, high) + total
            )
            grad_v = gv_ref[here].astype(wide) + last * dot(keys, high)
            grad_k = (grad_k * kslope_ref[here].astype(wide)).astype(low)
            grad_v = grad_v.astype(low)
            out_k, out_v = (gk1_ref, gv1_ref) if pair < half else (gk2_ref, gv2_ref)
            there = (z.span(row), lanes_of(pair % half))
            out_k[there] = grad_k
            out_v[there] = grad_v
    halves = (
        (keep_ref, gq_ref, gk1_ref, gv1_ref, wq_ref, wk_ref, wv_ref, 0),
        (give_ref, gq2_ref, gk2_ref, gv2_ref, wq2_ref, wk2_ref, wv2_ref, 1),
    )
    steps = z.hidden // z.width
    for out, gq, gk, gv, wq, wk, wv, part in halves:
        partial = dot_nt(gq[...], wq[...]) + dot_nt(gk[...], wk[...])
        partial = partial + dot_nt(gv[...], wv[...])
        if part == 0:
            s_first[...] = partial
        else:
            s_first[...] += partial
        out[2:6, :] = vec_mid_ref[0:4, :]
        out[6:7, 0:a] = vec_loc_ref[0:1, part * a : (part + 1) * a]
        out[6:7, a : 2 * a] = column_sums(gk[...].astype(wide))
        out[7:8, 0:a] = column_sums(gv[...].astype(wide))
        out[8 : 8 + steps, :] = vec_mid_ref[4 + part * steps : 4 + (part + 1) * steps, :]
    sums = [jnp.zeros((8, z.width), wide) for _ in range(2)]
    for row in range(z.rows):
        for tile in tiles(z.block):
            here = z.at(row, tile)
            normed, inverse = normalize(tokens_ref[row, tile, :].astype(wide))
            grad_first = s_first[here, :]
            grad_tokens = norm_backward(grad_first, normed, inverse, gain_ref[...])
            gtok_ref[here, :] = (gbr_ref[here, :].astype(wide) + grad_tokens).astype(low)
            values = (grad_first * normed, grad_first)
            sums = [total + fold_rows(value) for total, value in zip(sums, values)]
    for line, total in enumerate(sums):
        for out in (keep_ref, give_ref):
            out[line : line + 1, :] = column_sums(total)


def attn_grad_kernel(
    z,
    radix,
    mine_ref,
    first_ref,
    first2_ref,
    gq_ref,
    gq2_ref,
    gk_ref,
    gk2_ref,
    gv_ref,
    gv2_ref,
    att_ref,
    att2_ref,
    gbr_ref,
    gbr2_ref,
    keep_ref,
    got_ref,
    *outs,
):
    outs, out_ref = outs[:radix], outs[radix]
    a, w = z.attn, z.width
    first, first2 = first_ref[...], first2_ref[...]
    out_ref[0:w, 0:a] = (dot_tn(first, gq_ref[...]) + dot_tn(first2, gq2_ref[...])).astype(low)
    out_ref[0:w, a : 2 * a] = (dot_tn(first, gk_ref[...]) + dot_tn(first2, gk2_ref[...])).astype(
        low
    )
    grad_v = (dot_tn(first, gv_ref[...]) + dot_tn(first2, gv2_ref[...])).astype(low)
    half = w // 2
    out_ref[w : w + half, 0:a] = grad_v[0:half]
    out_ref[w : w + half, a : 2 * a] = grad_v[half:w]
    out_ref[w + half : w + half + a, :] = (
        dot_tn(att_ref[...], gbr_ref[...]) + dot_tn(att2_ref[...], gbr2_ref[...])
    ).astype(low)
    start = w + half + a
    if out_ref.shape[0] > start:
        out_ref[start:, :] = jnp.zeros((out_ref.shape[0] - start, w), low)
    vectors = (keep_ref[...] + got_ref[...]).astype(low)
    for distance, out in enumerate(outs):
        rows = out.shape[0] - 16
        first_row = jnp.bitwise_xor(mine_ref[1], distance) * rows
        out[0:rows, :] = out_ref[pl.ds(pl.multiple_of(first_row, rows), rows), :]
        out[rows : rows + 16, :] = vectors


def place_kernel(mine_ref, one_ref, one2_ref, two_ref, two2_ref, out_one_ref, out_two_ref):
    step = pl.program_id(0)

    @pl.when(step == 0)
    def _():
        out_one_ref[...] = one_ref[...].reshape(out_one_ref.shape)
        out_two_ref[...] = two_ref[...].reshape(out_two_ref.shape).astype(wide)

    @pl.when(step == 1)
    def _():
        out_one_ref[...] = one2_ref[...].reshape(out_one_ref.shape)
        out_two_ref[...] = two2_ref[...].reshape(out_two_ref.shape).astype(wide)


def unpack_attn_kernel(z, level, mine_ref, *refs):
    pieces, refs = refs[: level.radix], refs[level.radix :]
    vec_ref, lowest_ref, lowest2_ref, q_ref, k_ref, v_ref, o_ref = refs[:7]
    vecs, sums_ref = refs[7:18], refs[18]
    join_kernel(level, mine_ref, *pieces, sums_ref)
    a, w = z.attn, z.width
    half = w // 2
    q_ref[...] = sums_ref[0:w, 0:a].astype(wide)
    k_ref[...] = sums_ref[0:w, a : 2 * a].astype(wide)
    v_ref[0:half, :] = sums_ref[w : w + half, 0:a].astype(wide)
    v_ref[half:w, :] = sums_ref[w : w + half, a : 2 * a].astype(wide)
    o_ref[...] = sums_ref[w + half : w + half + a, :].astype(wide)
    table = vec_ref[...]
    g1, b1, ob, g2, b2, db, qb, kb, vb, upb, least = vecs
    for row, out in enumerate((g1, b1, ob, g2, b2, db)):
        out[...] = table[row : row + 1, :]
    qb[...] = table[6:7, 0:a]
    kb[...] = table[6:7, a : 2 * a]
    vb[...] = table[7:8, 0:a]
    for part in range(z.hidden // w):
        upb[:, part * w : (part + 1) * w] = table[8 + part : 9 + part, :]
    least[...] = jnp.minimum(lowest_ref[0:1, 0:1], lowest2_ref[0:1, 0:1])


def swap(value):
    return lax.ppermute(value, "mp", [(0, 1), (1, 0)])


def over_blocks(value):
    return lax.all_to_all(value, "seq", 0, 0)


class Level:
    def __init__(self, index, shift, radix):
        self.index, self.shift, self.radix = index, shift, radix

    def exchange(self, value, distance, count):
        other = distance << self.shift
        return lax.ppermute(value, "seq", [(i, i ^ other) for i in range(count)])


def levels_of(count):
    levels, shift = [], 0
    while (1 << shift) < count:
        radix = 4 if (4 << shift) <= count else 2
        levels.append(Level(len(levels), shift, radix))
        shift += 2 if radix == 4 else 1
    return levels


def shape(dims, kind):
    return jax.ShapeDtypeStruct(tuple(dims), kind)


HELD = pl.BlockSpec(memory_space=pltpu.VMEM)
PLACED = pl.BlockSpec(memory_space=pl.ANY)


def full(value):
    dims = tuple(value.shape)
    return pl.BlockSpec(dims, lambda *_: (0,) * len(dims))


def call(kernel, ins, outs, flops, mine=None, specs=None, out_specs=None, grid=(1,), scratch=(), limit=58, after=None, held=(), held_out=(), mark=False, aliases=None):
    specs, out_specs = specs or {}, out_specs or {}
    in_list = [specs.get(i, full(value)) for i, value in enumerate(ins)]
    out_list = [out_specs.get(i, full(value)) for i, value in enumerate(outs)]
    in_list = [HELD if i in held else spec for i, spec in enumerate(in_list)]
    out_list = [HELD if i in held_out else spec for i, spec in enumerate(out_list)]
    moved = sum(v.size * v.dtype.itemsize for v in list(ins) + list(outs))
    head = 0 if mine is None else 1
    ins = list(ins)
    outs = list(outs)
    count_in, count_out = head + len(ins), len(outs)
    if after is not None:
        in_list.append(HELD)
        ins.append(after)
    if mark:
        out_list.append(HELD)
        outs.append(jax.ShapeDtypeStruct((8, LANES), wide))

    def body(*refs):
        refs = list(refs)
        if after is not None:
            refs.pop(count_in)
        if mark:
            mark_ref = refs.pop(count_in + count_out)
            mark_ref[...] = jnp.zeros((8, LANES), wide)
        kernel(*refs)

    return pl.pallas_call(
        body,
        grid_spec=pltpu.PrefetchScalarGridSpec(
            num_scalar_prefetch=head,
            grid=grid,
            in_specs=in_list,
            out_specs=out_list,
            scratch_shapes=list(scratch),
        ),
        out_shape=list(outs),
        input_output_aliases=aliases or {},
        compiler_params=pltpu.CompilerParams(vmem_limit_bytes=limit * MEBI),
        cost_estimate=pl.CostEstimate(flops=int(flops), bytes_accessed=int(moved), transcendentals=0),
    )(*(() if mine is None else (mine,)), *ins)


def per_device(
    tokens,
    first_gain,
    first_bias,
    query_weight,
    query_bias,
    key_weight,
    key_bias,
    value_weight,
    value_bias,
    output_weight,
    output_bias,
    second_gain,
    second_bias,
    up_weight,
    up_bias,
    down_weight,
    down_bias,
    cotangent,
    doc_starts,
    valid_mask,
):
    blocks = lax.axis_size("seq")
    shares = lax.axis_size("mp")
    all_rows, block, width = tokens.shape
    a, hidden = query_weight.shape[1], up_weight.shape[1]
    z = Sizes(blocks, all_rows // shares, block, width, a, hidden)
    t = z.toks
    levels = levels_of(blocks)
    me = lax.axis_index("seq")
    places = [(me >> level.shift) & (level.radix - 1) for level in levels]
    far_bits = [1 << k for k in range(2, blocks.bit_length() - 1)]
    signs = [(me & bit) // bit for bit in far_bits]
    mine = jnp.stack([lax.axis_index("mp")] + places + signs + [me]).astype(jnp.int32)
    z.me = mine.shape[0] - 1
    first_bit = 1 + len(levels)

    def row(vector):
        return vector.reshape(1, vector.shape[0])

    g1, b1, g2, b2 = row(first_gain), row(first_bias), row(second_gain), row(second_bias)
    ob, db = row(output_bias), row(down_bias)
    wk2, wv2, wq2 = swap(key_weight), swap(value_weight), swap(query_weight)
    other_bias = swap(row(jnp.concatenate([query_bias, key_bias, value_bias, up_bias])))
    wo2, wup2, wd2 = swap(output_weight), swap(up_weight), swap(down_weight)

    def own_block(other=False):
        if other:
            return pl.BlockSpec((z.rows, block, width), lambda i, m: (1 - m[0], 0, 0))
        return pl.BlockSpec((z.rows, block, width), lambda i, m: (m[0], 0, 0))

    part = functools.partial
    sent_shape = shape((blocks, z.height, LANES), low)
    stage = pltpu.VMEM((z.height, LANES), wide)
    state_scratch = pltpu.VMEM((z.rows * z.pairs, HEAD_DIM, LANES), wide)
    thin = shape((t, LANES), wide)
    narrow, broad, half = shape((t, width), low), shape((t, width), wide), shape((t, a), low)

    first, kslope, kfeat, vlow, cols, segs, sent, means = call(
        part(project_kernel, z),
        (
            tokens,
            doc_starts,
            valid_mask,
            g1,
            b1,
            key_weight,
            wk2,
            row(key_bias),
            value_weight,
            wv2,
            row(value_bias),
            other_bias,
        ),
        (
            narrow,
            narrow,
            narrow,
            narrow,
            thin,
            shape((8 * z.rows, block), wide),
            sent_shape,
            shape((z.rows * z.pairs, LANES), wide),
        ),
        4e9,
        mine,
        specs={0: own_block()},
        scratch=[state_scratch, stage, pltpu.VMEM((2, t, a), wide)],
    )

    def scan(held, backward, after):
        return call(
            part(scan_kernel, z, backward),
            (held,),
            (sent_shape, shape((8, LANES), wide)),
            1e8,
            mine,
            scratch=[
                stage,
                pltpu.VMEM((2, blocks, LANES), wide),
                pltpu.VMEM((blocks, z.slice, LANES), wide),
            ],
            limit=10,
            after=after,
            held=(0,),
            held_out=(0,),
        )

    arriving = over_blocks(sent)
    qslope, qfeat, weights, within, sums, mark = call(
        part(score_kernel, z),
        (first, query_weight, wq2, row(query_bias), other_bias, kfeat, vlow, cols, segs),
        (narrow, narrow, shape((z.rows * z.pairs * 2, block, block), low), broad, thin),
        4e9,
        scratch=[pltpu.VMEM((2, t, a), wide)],
        mark=True,
    )
    entering, _ = scan(arriving, False, None)
    entering = over_blocks(entering)
    steps = hidden // width
    up_block = pl.BlockSpec((width, width), lambda i, m: (0, i))
    down_block = pl.BlockSpec((width, width), lambda i, m: (i, 0))
    tok_block = pl.BlockSpec((t, width), lambda i, m: (0, i))
    bias_block = pl.BlockSpec((1, width), lambda i, m: (0, i))
    other_up = other_bias[:, 3 * a :]
    wider = shape((t, hidden), low)
    (
        layer,
        act,
        act2,
        gup,
        gup2,
        second,
        gbr,
        att,
        att2,
        gnum,
        gnorm,
        sent_back,
        vec_mid,
    ) = call(
        part(middle_kernel, z),
        (
            entering,
            qfeat,
            within,
            sums,
            cols,
            tokens,
            cotangent,
            output_weight,
            wo2,
            ob,
            g2,
            b2,
            up_weight,
            wup2,
            row(up_bias),
            other_up,
            down_weight,
            wd2,
            db,
            means,
        ),
        (
            narrow,
            wider,
            wider,
            wider,
            wider,
            narrow,
            narrow,
            half,
            half,
            broad,
            thin,
            sent_shape,
            shape((16, width), wide),
        ),
        12e9,
        mine,
        specs={
            5: own_block(),
            6: own_block(),
            12: up_block,
            13: up_block,
            14: bias_block,
            15: bias_block,
            16: down_block,
            17: down_block,
        },
        out_specs={1: tok_block, 2: tok_block, 3: tok_block, 4: tok_block},
        held=(0,),
        grid=(steps,),
        scratch=[
            pltpu.VMEM((t, width), wide),
            pltpu.VMEM((t, width), wide),
            pltpu.VMEM((t, LANES), wide),
            pltpu.VMEM((t, width), wide),
            pltpu.VMEM((t, width), wide),
            pltpu.VMEM((t, 2 * a), wide),
            pltpu.VMEM((t, 2 * a), wide),
            pltpu.VMEM((8, LANES), wide),
            state_scratch,
            stage,
            pltpu.VMEM((z.rows * z.pairs * LANES, LANES), low),
            pltpu.VMEM((z.rows, block, width), wide),
            pltpu.VMEM((z.rows, block, width), wide),
        ],
    )
    act_in, gup_in, second_in = swap(act2), swap(gup2), swap(second)
    piece = hidden // 4
    act_block = pl.BlockSpec((t, piece), lambda i, m: (0, jnp.bitwise_xor(m[1], i)))
    two = shape((2 * piece, width), low)
    one = shape((piece, width), low)
    table = shape((16, width), wide)
    height = max(2 * width, 16 * blocks)
    radix = levels[0].radix

    def to(value, distance):
        return levels[0].exchange(value, distance, blocks)

    def far(value, bit):
        return lax.ppermute(value, "seq", [(i, i ^ bit) for i in range(blocks)])

    def spread(level, parts):
        return [parts[0]] + [level.exchange(p, d, blocks) for d, p in enumerate(parts) if d]

    def small(kernel, ins, dims, after, scalars=None, scratch=()):
        outs = [shape(dim, low) if isinstance(dim, tuple) else dim for dim in dims]
        *outs, marks["last"] = call(
            kernel,
            ins,
            outs,
            1e6,
            scalars,
            limit=8,
            after=after,
            held=range(len(ins)),
            held_out=range(len(outs)),
            mark=True,
            scratch=scratch,
        )
        return outs

    marks = {}

    def summed(number, parts, after):
        level = levels[number]
        rows = parts[0].shape[0] - 16
        outs = [shape((rows, width), low), shape((16, width), wide)]
        if number + 1 < len(levels):
            following = levels[number + 1].radix
            outs = [shape((rows // following + 16, width), low)] * following
        seen = [pltpu.VMEM((level.radix, 16, width), wide)]
        return small(part(sum_kernel, level), parts, outs, after, mine, seen)

    def joined(number, value, after):
        level = levels[number]
        dims = [(level.radix * value.shape[0], width)]
        parts = spread(level, [value] * level.radix)
        return small(part(join_kernel, level), parts, dims, after, mine)[0]

    v = {"leaving": over_blocks(sent_back)}

    def ffn_gradients(after):
        down_keep, down_give, up_keep, up_give, mark = call(
            part(ffn_grad_kernel, z),
            (act, act_in, cotangent, cotangent, second, second_in, gup, gup_in),
            (two, two, two, two),
            4e9,
            mine,
            specs={
                0: act_block,
                1: act_block,
                2: own_block(),
                3: own_block(True),
                6: act_block,
                7: act_block,
            },
            grid=(4,),
            after=after,
            mark=True,
        )
        v["down"], v["up"] = (down_keep, to(down_give, 1)), (up_keep, to(up_give, 2))
        return mark

    def backward_scan(after):
        leaving, v["lowest"] = scan(v["leaving"], True, after)
        v["leaving"] = over_blocks(leaving)
        return v["lowest"]

    def local_gradients(after):
        *v["local"], mark = call(
            part(local_kernel, z),
            (entering, weights, qfeat, kfeat, vlow, gnum, gnorm, qslope, cols, segs),
            (half, half, narrow, narrow, shape((8, 2 * a), wide)),
            6e9,
            scratch=[state_scratch],
            after=after,
            mark=True,
        )
        return mark

    def final_gradients(after):
        gq, gq2, gk_local, gv_local, vec_loc = v["local"]
        *v["final"], mark = call(
            part(final_kernel, z),
            (
                v["leaving"],
                kfeat,
                vlow,
                kslope,
                gk_local,
                gv_local,
                cols,
                gq,
                gq2,
                query_weight,
                wq2,
                key_weight,
                wk2,
                value_weight,
                wv2,
                tokens,
                g1,
                gbr,
                vec_mid,
                vec_loc,
            ),
            (half, half, half, half, narrow, table, table),
            4e9,
            mine,
            specs={15: own_block()},
            scratch=[state_scratch, pltpu.VMEM((t, width), wide)],
            held=(0,),
            after=after,
            mark=True,
        )
        return mark

    def first_pair(after):
        dims = [(piece, width)] * 4
        ins = v["down"] + v["up"]
        down_keep, down_give, up_keep, up_give = small(first_pair_kernel, ins, dims, after)
        v["down"], v["up"] = (down_keep, to(down_give, 2)), (up_keep, to(up_give, 1))
        return marks["last"]

    def attn_gradients(after):
        gq, gq2 = v["local"][:2]
        gk, gk2, gv, gv2, _, keep, give = v["final"]
        *v["rest"], mark = call(
            part(attn_grad_kernel, z, radix),
            (
                first,
                swap(first),
                gq,
                swap(gq2),
                gk,
                swap(gk2),
                gv,
                swap(gv2),
                att,
                swap(att2),
                gbr,
                swap(gbr),
                keep,
                swap(give),
            ),
            [shape((height // radix + 16, width), low)] * radix,
            2e9,
            mine,
            scratch=[pltpu.VMEM((height, width), low)],
            held=range(1, 14, 2),
            limit=30,
            after=after,
            mark=True,
        )
        v["rest"] = spread(levels[0], v["rest"])
        return mark

    def second_pair(after):
        dims = [(piece, width)] * 2
        ins = v["down"] + v["up"]
        keep, give = small(part(second_pair_kernel, first_bit), ins, dims, after, mine)
        v["ffn"] = (keep, far(give, far_bits[0]))
        return marks["last"]

    def first_half(after):
        dims = [(v["ffn"][0].shape[0] // 2, width)] * 2
        kernel = part(halve_kernel, first_bit + 1)
        keep, give = small(kernel, v["ffn"], dims, after, mine)
        v["ffn"] = (keep, far(give, far_bits[1]))
        return marks["last"]

    def last_half(after):
        for number in range(2, len(far_bits)):
            dims = [(v["ffn"][0].shape[0] // 2, width)] * 2
            kernel = part(halve_kernel, first_bit + number)
            keep, give = small(kernel, v["ffn"], dims, after, mine)
            v["ffn"] = (keep, far(give, far_bits[number]))
        (out,) = small(add_kernel, v["ffn"], [v["ffn"][0].shape], after)
        v["ffn"] = (out, far(out, far_bits[-1]))
        return marks["last"]

    def first_double(after):
        for number in reversed(range(1, len(far_bits))):
            dims = [(2 * v["ffn"][0].shape[0], width)]
            (out,) = small(part(double_kernel, first_bit + number), v["ffn"], dims, after, mine)
            v["ffn"] = (out, far(out, far_bits[number - 1]))
        return marks["last"]

    def last_double(after):
        dims = [(2 * v["ffn"][0].shape[0], width)]
        (out,) = small(part(double_kernel, first_bit), v["ffn"], dims, after, mine)
        v["ffn"] = (out, to(out, 1), to(out, 2))
        return marks["last"]

    def cut(after):
        out, out_x, out_y = v["ffn"]
        far_down, far_up = small(cut_kernel, (out_y, out_x), [(piece, width)] * 2, after)
        v["ffn"] = (out, out_x, out_y, to(far_down, 1), to(far_up, 2))
        return marks["last"]

    def first_sum(after):
        v["rest"] = summed(0, v["rest"], after)
        out = v["rest"][0]
        v["rest"] = spread(levels[1], v["rest"])
        return marks["last"]

    def last_sum(after):
        for number in range(1, len(levels)):
            v["rest"] = summed(number, v["rest"], after)
            if number + 1 < len(levels):
                v["rest"] = spread(levels[number + 1], v["rest"])
        return marks["last"]

    def join(after):
        out, v["vectors"] = v["rest"]
        for number in range(len(levels) - 1, 0, -1):
            out = joined(number, out, after)
        v["rest"] = spread(levels[0], [out] * radix)
        return marks["last"]

    def place(after):
        placed = pl.BlockSpec(
            (z.rows, block, width), lambda i, m: (jnp.where(i == 0, m[0], 1 - m[0]), 0, 0)
        )
        gtok = v["final"][4]
        *v["out"], mark = call(
            place_kernel,
            (layer, swap(layer), gtok, swap(gtok)),
            (shape(tokens.shape, low), shape(tokens.shape, wide)),
            1e6,
            mine,
            out_specs={0: placed, 1: placed},
            grid=(2,),
            held=(1, 3),
            limit=30,
            after=after,
            mark=True,
        )
        return mark

    def piece_blocks(step):
        return [
            pl.BlockSpec((piece, width), lambda i, m: (jnp.bitwise_xor(m[1], i + step), 0)),
            pl.BlockSpec((width, piece), lambda i, m: (0, jnp.bitwise_xor(m[1], i + step))),
        ]

    def unpack_three(after):
        outs = (shape((hidden, width), wide), shape((width, hidden), wide))
        *v["grads"], mark = call(
            unpack_three_kernel,
            v["ffn"][:3],
            outs,
            1e6,
            mine,
            out_specs=dict(enumerate(piece_blocks(0))),
            grid=(3,),
            held=(0, 1, 2),
            limit=24,
            after=after,
            mark=True,
        )
        return mark

    def unpack_far(after):
        outs = (shape((hidden, width), wide), shape((width, hidden), wide))
        *v["ffn"], mark = call(
            unpack_far_kernel,
            (*v["ffn"][3:], *v["grads"]),
            outs,
            1e6,
            mine,
            specs={2: PLACED, 3: PLACED},
            out_specs=dict(enumerate(piece_blocks(3))),
            held=(0, 1),
            limit=16,
            after=after,
            mark=True,
            aliases={3: 0, 4: 1},
        )
        return mark

    def unpack_attn(after):
        *v["rest"], mark = call(
            part(unpack_attn_kernel, z, levels[0]),
            (*v["rest"], v["vectors"], v["lowest"], swap(v["lowest"])),
            (
                shape((width, a), wide),
                shape((width, a), wide),
                shape((width, a), wide),
                shape((a, width), wide),
            )
            + tuple(shape((1, width), wide) for _ in range(6))
            + tuple(shape((1, a), wide) for _ in range(3))
            + (shape((1, hidden), wide), shape((1, 1), wide)),
            1e6,
            mine,
            scratch=[pltpu.VMEM((height, width), low)],
            held=range(radix),
            limit=24,
            after=after,
            mark=True,
        )
        return mark

    steps = dict(
        KF=ffn_gradients,
        S=backward_scan,
        KD=local_gradients,
        KE=final_gradients,
        KG=attn_gradients,
        p1=first_pair,
        p2=second_pair,
        h1=first_half,
        h2=last_half,
        d1=first_double,
        d2=last_double,
        c=cut,
        s1=first_sum,
        s2=last_sum,
        j=join,
        P=place,
        U3=unpack_three,
        UA=unpack_far,
        UB=unpack_attn,
    )
    after = None
    for name in ORDER:
        after = steps[name](after)
    layer_out, grad_tokens = v["out"]
    grad_down, grad_up = v["ffn"]
    grad_q, grad_k, grad_v, grad_o, g1, b1, ob, g2, b2, db, qb, kb, vb, upb, least = v["rest"]

    def flat(table):
        return table.reshape(table.shape[1])

    return (
        layer_out,
        grad_tokens,
        least.reshape(()),
        flat(g1),
        flat(b1),
        grad_q,
        flat(qb),
        grad_k,
        flat(kb),
        grad_v,
        flat(vb),
        grad_o,
        flat(ob),
        flat(g2),
        flat(b2),
        grad_up,
        flat(upb),
        grad_down,
        flat(db),
    )


def solution(mesh):
    return jax.shard_map(
        per_device,
        mesh=mesh,
        in_specs=(
            P(None, "seq", None),
            P(),
            P(),
            P(None, "mp"),
            P("mp"),
            P(None, "mp"),
            P("mp"),
            P(None, "mp"),
            P("mp"),
            P("mp", None),
            P(),
            P(),
            P(),
            P(None, "mp"),
            P("mp"),
            P("mp", None),
            P(),
            P(None, "seq", None),
            P(None, "seq"),
            P(None, "seq"),
        ),
        out_specs=(
            P(None, "seq", None),
            P(None, "seq", None),
            P(),
            P(),
            P(),
            P(None, "mp"),
            P("mp"),
            P(None, "mp"),
            P("mp"),
            P(None, "mp"),
            P("mp"),
            P("mp", None),
            P(),
            P(),
            P(),
            P(None, "mp"),
            P("mp"),
            P("mp", None),
            P(),
        ),
        check_vma=False,
    )
```
